32 devices in a mesh: row: 4 (over y, x), seq: 2 (over core), pat: 4 (over z).
Axes of the slice: x: 2, y: 2, z: 4, core: 2. Of those that a mesh axis runs over, the one named last changes fastest.
Arguments:
- block_input: bfloat16 [4, 1024, 768], P('row', 'seq'), may hold values from -6 to 6
- doc_ids: int32 [4, 1024], P('row'), may hold values from 0 to 2, as said below
- ln1_gain: float32 [768], replicated, may hold values from 0.5 to 1.5
- ln1_bias: float32 [768], replicated, may hold values from -2 to 2
- w_query: bfloat16 [768, 768], replicated, may hold values from -0.21875 to 0.21875
- w_key: bfloat16 [768, 768], replicated, may hold values from -0.21875 to 0.21875
- w_value: bfloat16 [768, 768], replicated, may hold values from -0.21875 to 0.21875
- w_out: bfloat16 [768, 768], replicated, may hold values from -1.75 to 1.75
- ln2_gain: float32 [768], replicated, may hold values from 0.5 to 1.5
- ln2_bias: float32 [768], replicated, may hold values from -2 to 2
- w_up: bfloat16 [768, 3072], P(None, 'pat'), may hold values from -0.21875 to 0.21875
- w_down: bfloat16 [3072, 768], P('pat'), may hold values from -0.109375 to 0.109375
- cotangent: bfloat16 [4, 1024, 768], P('row', 'seq', 'pat'), may hold values from -6 to 6
Outputs:
- output: bfloat16 [4, 1024, 768], P('row', 'seq', 'pat')
- grad_input: bfloat16 [4, 1024, 768], P('row', ('seq', 'pat'))
- grad_ln1_gain: float32 [768], replicated
- grad_ln1_bias: float32 [768], replicated
- grad_query: float32 [768, 768], replicated
- grad_key: float32 [768, 768], replicated
- grad_value: float32 [768, 768], replicated
- grad_out: float32 [768, 768], replicated
- grad_ln2_gain: float32 [768], replicated
- grad_ln2_bias: float32 [768], replicated
- grad_up: float32 [768, 3072], P(None, 'pat')
- grad_down: float32 [3072, 768], P('pat')
The draws below stay inside these ranges and needn't reach their ends.
Inputs may be any that keep to these rules, and one draw needn't show every extreme that they name: `doc_ids`: along each row the ids never fall.
All inputs are finite; a program needn't handle non-finite values.
Results may differ from the reference program's by a relative error of at most 0.02.
Values may be sent and summed in bfloat16 or wider, within the bound.
No kernel may reach another device: no remote copies, remote signals or barrier semaphores. Data moves between devices by JAX's collectives and lax.ppermute only.
A program may use at most 192 MiB of HBM per device.

```python
import jax
import jax.numpy as jnp
from jax import lax

D = 768
HEADS = 12
HDIM = 64
FF = 3072
SPAN = 512
ROWS = 4
LENGTH = 1024


def draw_doc_ids(key, part):
    key = jax.random.fold_in(key, 11)
    first_key, second_key = jax.random.split(key)
    first_cut = jax.random.randint(first_key, (ROWS, 1), 1, SPAN)
    second_cut = jax.random.randint(second_key, (ROWS, 1), LENGTH - SPAN + 1, LENGTH)
    positions = jnp.arange(LENGTH, dtype=jnp.int32)[None, :]
    return ((positions >= first_cut).astype(jnp.int32) + (positions >= second_cut).astype(jnp.int32)).astype(jnp.int32)


def shard_levels(stream_key, dims, cuts, smallest, largest):
    def one(axis_at, shards_of):
        draws = jax.random.uniform(jax.random.fold_in(jax.random.fold_in(stream_key, 6), axis_at), (shards_of,), jnp.float32, smallest / len(cuts), largest / len(cuts))
        return jnp.repeat(jnp.exp(draws), dims[axis_at] // shards_of).reshape((-1,) + (1,) * (len(dims) - axis_at - 1))

    level = one(*cuts[0])
    for cut in cuts[1:]:
        level = level * one(*cut)
    return level


def bell_draw(rng, shape, scale, most, pieces=(), held_as=jnp.bfloat16):
    values = scale * jax.random.normal(rng, shape, jnp.float32)
    if pieces:
        values = values * shard_levels(rng, shape, pieces, -0.22, 0.18)
    return jnp.clip(values, -most, most).astype(held_as)


def setup_inputs(seed: int = 0) -> dict:
    key_of = jax.random.split(jax.random.key(seed), 14)
    block_input = bell_draw(key_of[0], (ROWS, LENGTH, D), 1.0, 6.0, ((0, 4), (1, 2)))
    doc_ids = draw_doc_ids(jax.random.fold_in(key_of[13], 71), 0)
    ln1_gain = jnp.clip(1.0 + 0.1 * jax.random.normal(key_of[2], (D,), jnp.float32), 0.5, 1.5)
    ln1_bias = bell_draw(key_of[3], (D,), 0.3, 2.0, (), jnp.float32)
    w_query = bell_draw(key_of[4], (D, D), D ** -0.5, 0.21875)
    w_key = bell_draw(key_of[5], (D, D), D ** -0.5, 0.21875)
    w_value = bell_draw(key_of[6], (D, D), D ** -0.5, 0.21875)
    w_out = bell_draw(key_of[7], (D, D), (D // 64) ** -0.5, 1.75)
    ln2_gain = jnp.clip(1.0 + 0.1 * jax.random.normal(key_of[8], (D,), jnp.float32), 0.5, 1.5)
    ln2_bias = bell_draw(key_of[9], (D,), 0.3, 2.0, (), jnp.float32)
    w_up = bell_draw(key_of[10], (D, FF), D ** -0.5, 0.21875, ((1, 4),))
    w_down = bell_draw(key_of[11], (FF, D), FF ** -0.5, 0.109375, ((0, 4),))
    cotangent = bell_draw(key_of[12], (ROWS, LENGTH, D), 1.0, 6.0, ((0, 4), (1, 2), (2, 4)))
    return {"block_input": block_input, "doc_ids": doc_ids, "ln1_gain": ln1_gain, "ln1_bias": ln1_bias, "w_query": w_query, "w_key": w_key, "w_value": w_value, "w_out": w_out, "ln2_gain": ln2_gain, "ln2_bias": ln2_bias, "w_up": w_up, "w_down": w_down, "cotangent": cotangent}


epsilon = 1e-05
masked_low = -1e+30
segment_parts = (1, 2, 4, 8, 16)
dilations = (1, 2, 4, 6, 12)

@jax.custom_vjp
def low(v):
    return lax.optimization_barrier(v.astype(jnp.bfloat16)).astype(jnp.float32)

@jax.custom_vjp
def low_back(v):
    return v

def low_keep(v):
    return (low(v), None)

def low_pass(kept, grad):
    return (grad,)

def back_keep(v):
    return (v, None)

def back_low(kept, grad):
    return (low(grad),)
low.defvjp(low_keep, low_pass)
low_back.defvjp(back_keep, back_low)

def layer_norm(values, gain, bias):
    center = values - lax.optimization_barrier(jnp.mean(values, axis=-1, keepdims=True))
    spread = lax.optimization_barrier(jnp.mean(center * center, axis=-1, keepdims=True))
    return center * lax.rsqrt(spread + epsilon) * gain + bias

def matmul(left, right):
    return jnp.dot(left, right, precision=lax.Precision.HIGHEST)

def multiplicity(query_pos, key_pos, query_doc, key_doc, row_length, members):
    head_ids = jnp.arange(HEADS, dtype=jnp.int32)
    counted = jnp.zeros((HEADS, query_pos.shape[0], key_pos.shape[0]), jnp.float32)
    for pattern in range(5):
        seg_width = row_length * segment_parts[pattern] // 16
        dilation = dilations[pattern]
        offset = (head_ids % dilation)[:, None]
        same_segment = query_pos[:, None] // seg_width == key_pos[None, :] // seg_width
        query_in = ((query_pos % seg_width)[None, :] - offset) % dilation == 0
        key_in = ((key_pos % seg_width)[None, :] - offset) % dilation == 0
        covered = same_segment[None] & query_in[:, :, None] & key_in[:, None, :]
        counted = counted + members[pattern] * covered.astype(jnp.float32)
    allowed = (key_pos[None, :] <= query_pos[:, None]) & (query_doc[:, None] == key_doc[None, :])
    return counted * allowed[None].astype(jnp.float32)

def forward(row_in, gain_one, bias_one, weight_query, weight_key, weight_value, weight_out, gain_two, bias_two, weight_up, weight_down, row_docs):
    length = row_in.shape[0]
    normed = low(layer_norm(row_in, gain_one, bias_one))
    queries = low_back(low(matmul(normed, weight_query))).reshape(length, HEADS, HDIM)
    keys = low_back(low(matmul(normed, weight_key))).reshape(length, HEADS, HDIM)
    values = low_back(low(matmul(normed, weight_value))).reshape(length, HEADS, HDIM)
    block = 512 if length % 512 == 0 else length
    positions = jnp.arange(length, dtype=jnp.int32)
    members = (1.0, 1.0, 1.0, 1.0, 1.0)

    def one_block(start):
        query_block = lax.dynamic_slice_in_dim(queries, start, block, 0)
        query_pos = start + jnp.arange(block, dtype=jnp.int32)
        query_doc = lax.dynamic_slice_in_dim(row_docs, start, block, 0)
        scores = jnp.einsum('qhd,khd->hqk', query_block, keys, precision=lax.Precision.HIGHEST) * HDIM ** (-0.5)
        scores = low_back(scores)
        counts = multiplicity(query_pos, positions, query_doc, row_docs, length, members)
        row_max = lax.optimization_barrier(jnp.max(jnp.where(counts > 0, scores, masked_low), axis=2, keepdims=True))
        weights = counts * jnp.exp(jnp.where(counts > 0, scores - row_max, -60.0))
        numerator = jnp.einsum('hqk,khd->qhd', low(weights), values, precision=lax.Precision.HIGHEST)
        denominator = lax.optimization_barrier(jnp.sum(weights, axis=2))
        return (numerator / denominator.T[:, :, None]).reshape(block, HEADS * HDIM)
    starts = jnp.arange(length // block, dtype=jnp.int32) * block
    mixed = lax.map(jax.checkpoint(one_block), starts).reshape(length, HEADS * HDIM)
    branch = low_back(matmul(low_back(low(mixed)), weight_out))
    resid = row_in + branch
    normed_two = low(layer_norm(resid, gain_two, bias_two))
    hidden = low_back(matmul(normed_two, weight_up))
    activated = low(jax.nn.gelu(hidden, approximate=False))
    return resid + matmul(activated, weight_down)

def reference(block_input, doc_ids, ln1_gain, ln1_bias, w_query, w_key, w_value, w_out, ln2_gain, ln2_bias, w_up, w_down, cotangent):
    params = tuple((p.astype(jnp.float32) for p in (ln1_gain, ln1_bias, w_query, w_key, w_value, w_out, ln2_gain, ln2_bias, w_up, w_down)))

    def per_row(carry, item):
        row_in, row_docs, row_grad = item

        def run(inputs, *weights):
            return forward(inputs, *weights, row_docs)
        result, back = jax.vjp(run, row_in, *params)
        grads = back(row_grad)
        summed = tuple((c + g for c, g in zip(carry, grads[1:])))
        return (summed, (result.astype(jnp.bfloat16), grads[0].astype(jnp.bfloat16)))
    start = tuple((jnp.zeros_like(p) for p in params))
    totals, stacked = lax.scan(per_row, start, (block_input.astype(jnp.float32), doc_ids, cotangent.astype(jnp.float32)))
    output, grad_input = stacked
    return (output, grad_input, totals[0], totals[1], totals[2], totals[3], totals[4], totals[5], totals[6], totals[7], totals[8], totals[9])
```

```python
import functools

import jax
import jax.numpy as jnp
from jax import lax
from jax.experimental import pallas as pl
from jax.experimental.pallas import tpu as pltpu
from jax.sharding import PartitionSpec as P

D = 768
HEADS = 12
HDIM = 64

epsilon = 1e-05
masked_low = -1e30
segment_parts = (1, 2, 4, 8, 16)
dilations = (1, 2, 4, 6, 12)
DOCS = 3
FEATS = 128
TILE = 256
VMEM_LIMIT = 60 * 1024 * 1024
f32 = jnp.float32
bf16 = jnp.bfloat16


def dot(a, b):
    return lax.dot_general(a, b, (((1,), (0,)), ((), ())), preferred_element_type=f32)


def dot_nt(a, b):
    return lax.dot_general(a, b, (((1,), (1,)), ((), ())), preferred_element_type=f32)


def dot_tn(a, b):
    return lax.dot_general(a, b, (((0,), (0,)), ((), ())), preferred_element_type=f32)


def kernel_call(body, out_shape, scratch=(), in_specs=None, flops=0):
    return pl.pallas_call(
        body,
        out_shape=out_shape,
        in_specs=in_specs,
        out_specs=jax.tree.map(lambda _: pl.BlockSpec(memory_space=pltpu.VMEM), out_shape),
        scratch_shapes=list(scratch),
        compiler_params=pltpu.CompilerParams(vmem_limit_bytes=VMEM_LIMIT),
        cost_estimate=pl.CostEstimate(flops=flops, bytes_accessed=1 << 22, transcendentals=0),
    )


def specs(n_scalar, n_arrays):
    return [pl.BlockSpec(memory_space=pltpu.SMEM)] * n_scalar + [
        pl.BlockSpec(memory_space=pltpu.VMEM)
    ] * n_arrays


def normalise(values):
    center = values - jnp.mean(values, axis=-1, keepdims=True)
    scale = lax.rsqrt(jnp.mean(center * center, axis=-1, keepdims=True) + epsilon)
    return center * scale, scale


def norm_backward(hat, scale, grad):
    return scale * (
        grad
        - jnp.mean(grad, axis=-1, keepdims=True)
        - hat * jnp.mean(grad * hat, axis=-1, keepdims=True)
    )


def project_kernel(parts, where, x, gain, bias, wq, wk, wv, normed, q, k, v, own):
    width = D // parts
    for part in range(parts):

        @pl.when(where[0] == part)
        def _():
            for at, w in enumerate((wq, wk, wv)):
                own[at] = w[:, part * width : (part + 1) * width]

    for start in range(0, x.shape[0], TILE):
        rows = pl.ds(start, TILE)
        hat, _ = normalise(x[rows, :].astype(f32))
        low = (hat * gain[...] + bias[...]).astype(bf16)
        normed[rows, :] = low
        q[rows, :] = (dot(low, own[0]).astype(bf16).astype(f32) * HDIM**-0.5).astype(bf16)
        k[rows, :] = dot(low, own[1]).astype(bf16)
        v[rows, :] = dot(low, own[2]).astype(bf16)


def head_mask(heads, width):
    lane = lax.broadcasted_iota(jnp.int32, (1, width), 1)
    return [((lane >= h * HDIM) & (lane < (h + 1) * HDIM)).astype(bf16) for h in range(heads)]


def attention_kernel(
    heads, span, where, q, k, v, k_far, v_far, feats, mixed, mixed_t, lse, q_head, v_t, vf_t
):
    width = heads * HDIM
    masks = head_mask(heads, width)
    for h in range(heads):
        q_head[h] = q[...] * masks[h]
    v_t[...] = v[...].T
    far = k_far.shape[0] // span

    def turn(j, _):
        rows = pl.ds(pl.multiple_of(j * span, span), span)
        vf_t[j] = v_far[rows, :].T
        return 0

    mine = where[0]
    lax.fori_loop(0, jnp.minimum(mine, far), turn, 0)
    own_start = pl.multiple_of(mine * span, span)
    lse[...] = jnp.zeros(lse.shape, f32)
    for start in range(0, span, TILE):
        for h in range(heads):
            q_tile = q_head[h, start : start + TILE, :]
            f_tile = feats[h, pl.ds(own_start + start, TILE), :]

            def part(k_rows, f_rows, v_rows, low_from, state):
                counts = dot_nt(f_rows, f_tile)
                if low_from is not None:
                    at_k = lax.broadcasted_iota(jnp.int32, counts.shape, 0)
                    at_q = lax.broadcasted_iota(jnp.int32, counts.shape, 1) + low_from
                    counts = jnp.where(at_k <= at_q, counts, 0.0)
                scores = jnp.where(counts > 0, dot_nt(k_rows, q_tile), masked_low)
                top, total, acc = state
                new_top = jnp.maximum(top, jnp.max(scores, axis=0, keepdims=True))
                weights = counts * jnp.exp(scores - new_top)
                factor = jnp.exp(top - new_top)
                return (
                    new_top,
                    total * factor + jnp.sum(weights, axis=0, keepdims=True),
                    acc * factor + dot(v_rows, weights.astype(bf16)),
                )

            state = (
                jnp.full((1, TILE), masked_low, f32),
                jnp.zeros((1, TILE), f32),
                jnp.zeros((HDIM, TILE), f32),
            )
            size = start + TILE
            head_rows = slice(h * HDIM, (h + 1) * HDIM)
            state = part(
                k[:size, :],
                feats[h, pl.ds(own_start, size), :],
                v_t[head_rows, :size],
                start,
                state,
            )

            def far_part(j, state):
                rows = pl.ds(pl.multiple_of(j * span, span), span)
                return part(k_far[rows, :], feats[h, rows, :], vf_t[j, head_rows, :], None, state)

            top, total, acc = lax.fori_loop(0, mine, far_part, state)
            mixed_t[head_rows, start : start + TILE] = acc / total
            lse[h : h + 1, start : start + TILE] = top + jnp.log(total)
    mixed[...] = mixed_t[...].T.astype(bf16)


def attention_back_kernel(
    heads,
    span,
    where,
    parts,
    mixed_t,
    lse,
    q,
    k,
    v,
    k_far,
    v_far,
    feats,
    grad_q,
    grad_k,
    grad_v,
    grad_kf,
    grad_vf,
    q_head,
    g_head,
    dots,
    probs,
    slopes,
    k_t,
    gq_t,
):
    width = heads * HDIM
    masks = head_mask(heads, width)
    mine = where[0]
    far = k_far.shape[0] // span
    total = parts[0].astype(f32)
    for part in range(1, parts.shape[0]):
        total = total + parts[part].astype(f32)
    low = total.astype(bf16)
    for h in range(heads):
        q_head[h] = q[...] * masks[h]
        g_head[h] = low * masks[h]
    product = low.astype(f32).T * mixed_t[...]
    for h in range(heads):
        dots[h : h + 1, :] = jnp.sum(product[h * HDIM : (h + 1) * HDIM], axis=0, keepdims=True)
    own_start = pl.multiple_of(mine * span, span)

    def block(h, start, k_rows, v_rows, f_rows, low_from):
        tile = slice(start, start + TILE)
        counts = dot_nt(f_rows, feats[h, pl.ds(own_start + start, TILE), :])
        if low_from is not None:
            at_k = lax.broadcasted_iota(jnp.int32, counts.shape, 0)
            at_q = lax.broadcasted_iota(jnp.int32, counts.shape, 1) + low_from
            counts = jnp.where(at_k <= at_q, counts, 0.0)
        scores = jnp.where(counts > 0, dot_nt(k_rows, q_head[h, tile, :]), masked_low)
        prob = counts * jnp.exp(scores - lse[h : h + 1, tile])
        grad_prob = dot_nt(v_rows, g_head[h, tile, :])
        slope = prob * (grad_prob - dots[h : h + 1, tile])
        size = k_rows.shape[0]
        columns = slice(h * span + start, h * span + start + TILE)
        probs[:size, columns] = prob.astype(bf16)
        slopes[:size, columns] = slope.astype(bf16)
        if size < span:
            probs[size:, columns] = jnp.zeros((span - size, TILE), bf16)
            slopes[size:, columns] = jnp.zeros((span - size, TILE), bf16)

    def finish(k_rows):
        k_t[...] = k_rows.T
        grad_v_rows = dot(probs[...], g_head[...].reshape(heads * span, width))
        grad_k_rows = dot(slopes[...], q_head[...].reshape(heads * span, width))
        terms = [
            dot(k_t[h * HDIM : (h + 1) * HDIM, :], slopes[:, h * span : (h + 1) * span])
            for h in range(heads)
        ]
        return grad_k_rows, grad_v_rows, terms

    for start in range(0, span, TILE):
        for h in range(heads):
            size = start + TILE
            block(h, start, k[:size, :], v[:size, :], feats[h, pl.ds(own_start, size), :], start)
    grad_k_rows, grad_v_rows, terms = finish(k[...])
    grad_k[...] = grad_k_rows
    grad_v[...] = grad_v_rows
    for h in range(heads):
        gq_t[h * HDIM : (h + 1) * HDIM, :] = terms[h]
    grad_kf[...] = jnp.zeros(grad_kf.shape, bf16)
    grad_vf[...] = jnp.zeros(grad_vf.shape, bf16)

    def far_block(j, _):
        rows = pl.ds(pl.multiple_of(j * span, span), span)
        for start in range(0, span, TILE):
            for h in range(heads):
                block(h, start, k_far[rows, :], v_far[rows, :], feats[h, rows, :], None)
        grad_k_rows, grad_v_rows, terms = finish(k_far[rows, :])
        grad_kf[rows, :] = grad_k_rows.astype(bf16)
        grad_vf[rows, :] = grad_v_rows.astype(bf16)
        for h in range(heads):
            gq_t[h * HDIM : (h + 1) * HDIM, :] += terms[h]
        return 0

    lax.fori_loop(0, jnp.minimum(mine, far), far_block, 0)
    grad_q[...] = (gq_t[...] * HDIM**-0.5).T.astype(bf16)


def middle_kernel(
    blocks,
    x,
    mixed4,
    c4,
    w_out,
    w_up,
    w_down,
    gain,
    bias,
    gm,
    ffn,
    gr,
    wide,
    sums,
    mixed,
    c,
    act,
    gh,
    low,
    branch,
):
    parts = mixed4.shape[0]
    width = D // parts
    for part in range(parts):
        columns = slice(part * width, (part + 1) * width)
        mixed[:, columns] = mixed4[part]
        c[:, columns] = c4[part]
    gain_sum = jnp.zeros((1, D), f32)
    bias_sum = jnp.zeros((1, D), f32)
    for start in range(0, x.shape[0], TILE):
        rows = slice(start, start + TILE)
        resid = x[rows, :].astype(f32) + dot(mixed[rows, :], w_out[...])
        hat, scale = normalise(resid)
        normed = (hat * gain[...] + bias[...]).astype(bf16)
        low[rows, :] = normed
        hidden = dot(normed, w_up[...])
        bell = 0.5 + 0.5 * lax.erf(hidden * (0.5**0.5))
        activated = (hidden * bell).astype(bf16)
        act[rows, :] = activated
        slope = bell + hidden * jnp.exp(-0.5 * hidden * hidden) * 0.3989422804014327
        grad_hidden = (slope * dot_nt(c[rows, :], w_down[...])).astype(bf16)
        gh[rows, :] = grad_hidden
        grad_normed = dot_nt(grad_hidden, w_up[...])
        gain_sum = gain_sum + jnp.sum(grad_normed * hat, axis=0, keepdims=True)
        bias_sum = bias_sum + jnp.sum(grad_normed, axis=0, keepdims=True)
        grad_resid = norm_backward(hat, scale, grad_normed * gain[...]) + c[rows, :].astype(
            f32
        ) * (1.0 / parts)
        gr[rows, :] = grad_resid
        grad_low = grad_resid.astype(bf16)
        branch[rows, :] = grad_low
        out_part = (dot(activated, w_down[...]) + resid * (1.0 / parts)).astype(bf16)
        for part in range(parts):
            columns = slice(part * width, (part + 1) * width)
            gm[part, rows, :] = dot_nt(grad_low, w_out[columns, :]).astype(bf16)
            ffn[part, rows, :] = out_part[:, columns]
    sums[0:1, :] = gain_sum
    sums[1:2, :] = bias_sum
    size = D // blocks
    for at, (left, right) in enumerate(((act, c), (low, gh), (mixed, branch))):
        product = dot_tn(left[...], right[...]).astype(bf16)
        for block in range(blocks):
            wide[block, at * size : (at + 1) * size, :] = product[
                block * size : (block + 1) * size, :
            ]


def last_kernel(
    blocks,
    parts,
    x,
    gain,
    normed,
    own,
    gq,
    gk,
    gv,
    gk_more,
    gv_more,
    gr,
    sums,
    narrow,
    back,
    small,
    gk_low,
    gv_low,
):
    gk_low[...] = (gk[...] + gk_more[...].astype(f32)).astype(bf16)
    gv_low[...] = (gv[...] + gv_more[...].astype(f32)).astype(bf16)
    width = D // parts
    gain_sum = jnp.zeros((1, D), f32)
    bias_sum = jnp.zeros((1, D), f32)
    span = x.shape[0]
    piece = span // parts
    for start in range(0, span, TILE):
        rows = slice(start, start + TILE)
        hat, scale = normalise(x[rows, :].astype(f32))
        grad_normed = (
            dot_nt(gq[rows, :], own[0])
            + dot_nt(gk_low[rows, :], own[1])
            + dot_nt(gv_low[rows, :], own[2])
        )
        gain_sum = gain_sum + jnp.sum(grad_normed * hat, axis=0, keepdims=True)
        bias_sum = bias_sum + jnp.sum(grad_normed, axis=0, keepdims=True)
        grad_in = gr[rows, :] + norm_backward(hat, scale, grad_normed * gain[...])
        back[rows, :] = grad_in.astype(bf16)
    for at, row in enumerate((gain_sum, bias_sum, sums[0:1, :], sums[1:2, :])):
        for part in range(parts):
            small[at * parts + part : at * parts + part + 1, :] = row[
                :, part * width : (part + 1) * width
            ]
    size = D // blocks
    tail = small[...].astype(bf16)
    for at, right in enumerate((gq, gk_low, gv_low)):
        product = dot_tn(normed[...], right[...]).astype(bf16)
        for block in range(blocks):
            narrow[block, at * size : (at + 1) * size, :] = product[
                block * size : (block + 1) * size, :
            ]
    for block in range(blocks):
        narrow[block, 3 * size :, :] = tail


def spread_kernel(rows_count, seq_count, where, mine, other, *outs):
    parts = mine.shape[1]
    width = mine.shape[3]
    size = (mine.shape[2] - 16) // 4
    seq = where[0]
    for row in range(rows_count):
        for half, source in enumerate((mine, other)):
            at = seq if half == 0 else 1 - seq
            start = pl.multiple_of((row * seq_count + at) * size, size)
            for part in range(parts):
                columns = slice(part * width, (part + 1) * width)
                for grad in range(4):
                    outs[grad][pl.ds(start, size), columns] = source[
                        row, part, grad * size : (grad + 1) * size, :
                    ].astype(f32)


def broadcast_exchange(value, axis):
    count = lax.axis_size(axis)
    return lax.all_to_all(
        jnp.broadcast_to(value[None], (count,) + value.shape), axis, 0, 0, tiled=False
    )


def swap(value):
    return lax.ppermute(value, "seq", [(0, 1), (1, 0)])


def one_hot_features(row_docs, heads, pat_index):
    length = row_docs.shape[0]
    position = jnp.arange(length, dtype=jnp.int32)
    head = pat_index * heads + jnp.arange(heads, dtype=jnp.int32)
    feature = jnp.arange(FEATS, dtype=jnp.int32)
    hit = jnp.zeros((heads, length, FEATS), jnp.bool_)
    base = 0
    for part, dilation in zip(segment_parts, dilations, strict=True):
        seg_width = length * part // 16
        inside = ((position % seg_width)[None, :] - (head % dilation)[:, None]) % dilation == 0
        key = base + (position // seg_width) * DOCS + row_docs
        key = jnp.where(inside, key[None, :], -1)
        hit = hit | (key[:, :, None] == feature[None, None, :])
        base += DOCS * (16 // part)
    return hit.astype(bf16)


def per_device(
    block_input,
    doc_ids,
    ln1_gain,
    ln1_bias,
    w_query,
    w_key,
    w_value,
    w_out,
    ln2_gain,
    ln2_bias,
    w_up,
    w_down,
    cotangent,
):
    span = block_input.shape[1]
    rows_count = lax.axis_size("row")
    seq_count = lax.axis_size("seq")
    parts = lax.axis_size("pat")
    seq_index = lax.axis_index("seq")
    pat_index = lax.axis_index("pat")
    pair = seq_count == 2
    heads = HEADS // parts
    width = D // parts
    quarter = span // parts
    blocks = rows_count * seq_count if (D // (rows_count * seq_count)) % 16 == 0 and pair else 1
    here = seq_index.astype(jnp.int32)[None]
    part_here = pat_index.astype(jnp.int32)[None]
    gain_one, bias_one = ln1_gain[None], ln1_bias[None]
    gain_two, bias_two = ln2_gain[None], ln2_bias[None]
    x = block_input[0]

    def shape(*dims, kind=bf16):
        return jax.ShapeDtypeStruct(dims, kind)

    c4 = broadcast_exchange(cotangent[0], "pat")
    feats = one_hot_features(doc_ids[0], heads, pat_index)
    normed, q, k, v, own = kernel_call(
        functools.partial(project_kernel, parts),
        (
            shape(span, D),
            shape(span, width),
            shape(span, width),
            shape(span, width),
            shape(3, D, width),
        ),
        in_specs=specs(1, 6),
        flops=2 * span * D * width * 3,
    )(part_here, x, gain_one, bias_one, w_query, w_key, w_value)

    if pair:
        k_far, v_far = swap(k), swap(v)
    else:
        k_far = lax.all_gather(k, "seq", axis=0, tiled=True)
        v_far = lax.all_gather(v, "seq", axis=0, tiled=True)
    far_rows = k_far.shape[0]

    mixed, mixed_t, lse = kernel_call(
        functools.partial(attention_kernel, heads, span),
        (shape(span, width), shape(width, span, kind=f32), shape(8, span, kind=f32)),
        scratch=[
            pltpu.VMEM((heads, span, width), bf16),
            pltpu.VMEM((width, span), bf16),
            pltpu.VMEM((far_rows // span, width, span), bf16),
        ],
        in_specs=specs(1, 6),
        flops=1 << 31,
    )(here, q, k, v, k_far, v_far, feats)

    mixed4 = lax.all_gather(mixed, "pat")
    gm, ffn, gr, wide, sums = kernel_call(
        functools.partial(middle_kernel, blocks),
        (
            shape(parts, span, width),
            shape(parts, span, width),
            shape(span, D, kind=f32),
            shape(blocks, 3 * D // blocks, D),
            shape(8, D, kind=f32),
        ),
        scratch=[pltpu.VMEM((span, D), bf16)] * 6,
        in_specs=specs(0, 8),
        flops=2 * span * D * D * 9,
    )(x, mixed4, c4, w_out, w_up, w_down, gain_two, bias_two)

    gm_parts = lax.all_to_all(gm, "pat", 0, 0, tiled=True)
    ffn_parts = lax.all_to_all(ffn, "pat", 0, 0, tiled=True)
    output = jnp.sum(ffn_parts.astype(f32), axis=0).astype(bf16)[None]

    gq, gk, gv, gkf, gvf = kernel_call(
        functools.partial(attention_back_kernel, heads, span),
        (
            shape(span, width),
            shape(span, width, kind=f32),
            shape(span, width, kind=f32),
            shape(far_rows, width),
            shape(far_rows, width),
        ),
        scratch=[
            pltpu.VMEM((heads, span, width), bf16),
            pltpu.VMEM((heads, span, width), bf16),
            pltpu.VMEM((8, span), f32),
            pltpu.VMEM((span, heads * span), bf16),
            pltpu.VMEM((span, heads * span), bf16),
            pltpu.VMEM((width, span), bf16),
            pltpu.VMEM((width, span), f32),
        ],
        in_specs=specs(1, 9),
        flops=1 << 32,
    )(here, gm_parts, mixed_t, lse, q, k, v, k_far, v_far, feats)

    if pair:
        gk_more, gv_more = swap(gkf), swap(gvf)
    else:
        gk_more = lax.psum_scatter(gkf, "seq", scatter_dimension=0, tiled=True)
        gv_more = lax.psum_scatter(gvf, "seq", scatter_dimension=0, tiled=True)

    size = D // blocks
    narrow, back = kernel_call(
        functools.partial(last_kernel, blocks, parts),
        (shape(blocks, 3 * size + 16, width), shape(span, D)),
        scratch=[
            pltpu.VMEM((16, width), f32),
            pltpu.VMEM((span, width), bf16),
            pltpu.VMEM((span, width), bf16),
        ],
        in_specs=specs(0, 11),
        flops=2 * span * D * width * 6,
    )(x, gain_one, normed, own, gq, gk, gv, gk_more, gv_more, gr, sums)

    back_parts = lax.all_to_all(back.reshape(parts, quarter, D), "pat", 0, 0, tiled=True)
    grad_input = jnp.sum(back_parts.astype(f32), axis=0).astype(bf16)[None]

    def total(value):
        return jnp.sum(value.astype(f32), axis=0).astype(bf16)

    both = ("row", "seq")
    if blocks > 1:
        wide_sum = total(lax.all_to_all(wide, both, 0, 0, tiled=True))
        ffn_own = wide_sum[: 2 * size]
        out_own = wide_sum[2 * size :].reshape(size, parts, width).transpose(1, 0, 2)
        out_own = total(lax.all_to_all(out_own, "pat", 0, 0, tiled=True))
        narrow_own = total(lax.all_to_all(narrow, both, 0, 0, tiled=True))
        mine = jnp.concatenate([narrow_own[: 3 * size], out_own, narrow_own[3 * size :]], axis=0)
        mine = lax.all_gather(mine, "pat")
        mine = broadcast_exchange(mine, "row")
        other = swap(mine)
        ffn_mine = broadcast_exchange(ffn_own, "row")
        ffn_other = swap(ffn_mine)
        grads = kernel_call(
            functools.partial(spread_kernel, rows_count, seq_count),
            (shape(D, D, kind=f32),) * 4,
            in_specs=specs(1, 2),
            flops=1 << 28,
        )(here, mine, other)
        vectors = jnp.sum(mine[0, :, 4 * size :, :].astype(f32), axis=0).reshape(4, D)
        first = jnp.where(seq_index == 0, ffn_mine, ffn_other)
        second = jnp.where(seq_index == 0, ffn_other, ffn_mine)
        halves = jnp.stack([first, second], axis=1).reshape(blocks, 2, size, D)
        grad_down = halves[:, 0].reshape(D, D).astype(f32)
        grad_up = halves[:, 1].reshape(D, D).astype(f32)
    else:
        wide_sum = lax.psum(wide[0], both).astype(f32)
        grad_down, grad_up = wide_sum[:D], wide_sum[D : 2 * D]
        grad_out = lax.psum(wide_sum[2 * D :].astype(bf16), "pat").astype(f32)
        narrow_sum = lax.all_gather(lax.psum(narrow[0], both), "pat").astype(f32)
        grads = [
            narrow_sum[:, at * D : (at + 1) * D].transpose(1, 0, 2).reshape(D, D)
            for at in range(3)
        ] + [grad_out]
        vectors = jnp.sum(narrow_sum[:, 3 * D :], axis=0).reshape(4, D)
    return (
        output,
        grad_input,
        vectors[0],
        vectors[1],
        grads[0],
        grads[1],
        grads[2],
        grads[3],
        vectors[2],
        vectors[3],
        grad_up,
        grad_down,
    )


def solution(mesh):
    placed = (
        P("row", "seq", None),
        P("row", None),
        P(),
        P(),
        P(),
        P(),
        P(),
        P(),
        P(),
        P(),
        P(None, "pat"),
        P("pat", None),
        P("row", "seq", "pat"),
    )
    return jax.shard_map(
        per_device,
        mesh=mesh,
        in_specs=placed,
        out_specs=(
            P("row", "seq", "pat"),
            P("row", ("seq", "pat"), None),
            P(),
            P(),
            P(),
            P(),
            P(),
            P(),
            P(),
            P(),
            P(None, "pat"),
            P("pat", None),
        ),
        check_vma=False,
    )
```

```python
import functools

import jax
import jax.numpy as jnp
from jax import lax
from jax.experimental import pallas as pl
from jax.experimental.pallas import tpu as pltpu
from jax.sharding import PartitionSpec as P

D = 768
HEADS = 12
HDIM = 64

epsilon = 1e-05
masked_low = -1e30
segment_parts = (1, 2, 4, 8, 16)
dilations = (1, 2, 4, 6, 12)
DOCS = 3
FEATS = 128
TILE = 256
VMEM_LIMIT = 60 * 1024 * 1024
SMALL_LIMIT = 20 * 1024 * 1024
COPIES = 24
f32 = jnp.float32
bf16 = jnp.bfloat16


def dot(a, b):
    return lax.dot_general(a, b, (((1,), (0,)), ((), ())), preferred_element_type=f32)


def dot_nt(a, b):
    return lax.dot_general(a, b, (((1,), (1,)), ((), ())), preferred_element_type=f32)


def dot_tn(a, b):
    return lax.dot_general(a, b, (((0,), (0,)), ((), ())), preferred_element_type=f32)


class Staged:
    def __init__(self, outside, inside, sems, free):
        self.outside, self.inside, self.sems, self.free = outside, inside, sems, free
        self.pending = []

    def start(self, source=None, target=None):
        copy = pltpu.make_async_copy(
            self.outside if source is None else source,
            self.inside if target is None else target,
            self.sems.at[next(self.free)],
        )
        copy.start()
        self.pending.append(copy)

    def get(self):
        for copy in self.pending:
            copy.wait()
        self.pending = []
        return self.inside

    def send(self, at=...):
        copy = pltpu.make_async_copy(
            self.inside.at[at], self.outside.at[at], self.sems.at[next(self.free)]
        )
        copy.start()
        self.pending.append(copy)


def staged_call(body, scalars, arrays, outs, scratch=(), windows=None, limit=VMEM_LIMIT, late=0, aliases=()):
    windows = windows or {}
    n_scalar, n_in, n_out = len(scalars), len(arrays), len(outs)

    def kernel(*refs):
        scalar_refs, refs = refs[:n_scalar], refs[n_scalar:]
        outside, refs = refs[: n_in + n_out], refs[n_in + n_out :]
        inside, refs = refs[: n_in + n_out], refs[n_in + n_out :]
        sems, rest = refs[0], refs[1:]
        free = iter(range(COPIES))
        every = [Staged(o, i, sems, free) for o, i in zip(outside, inside, strict=True)]
        ins, results = every[:n_in], every[n_in:]
        for at, one in enumerate(ins[: n_in - late]):
            if at in windows:
                start = windows[at](scalar_refs)
                size = one.inside.shape[-1]
                one.start(one.outside.at[:, pl.ds(pl.multiple_of(start, 128), size)])
            else:
                one.start()
        body(scalar_refs, ins, results, rest)
        for one in ins + results:
            one.get()

    def buffer(at, array):
        dims = array.shape
        if at >= n_in - late:
            return pltpu.VMEM((16, 128), array.dtype)
        if at in windows:
            dims = (*dims[:-1], 256)
        return pltpu.VMEM(dims, array.dtype)

    return pl.pallas_call(
        kernel,
        out_shape=tuple(outs),
        in_specs=[pl.BlockSpec(memory_space=pltpu.SMEM)] * n_scalar
        + [pl.BlockSpec(memory_space=pl.ANY)] * n_in,
        out_specs=(pl.BlockSpec(memory_space=pltpu.HBM),) * n_out,
        scratch_shapes=[buffer(at, a) for at, a in enumerate(arrays)]
        + [
            pltpu.VMEM((16, 128) if at in dict(aliases).values() else o.shape, o.dtype)
            for at, o in enumerate(outs)
        ]
        + [pltpu.SemaphoreType.DMA((COPIES,))]
        + list(scratch),
        input_output_aliases={n_scalar + a: o for a, o in aliases},
        compiler_params=pltpu.CompilerParams(vmem_limit_bytes=limit),
        cost_estimate=pl.CostEstimate(flops=0, bytes_accessed=0, transcendentals=0),
    )(*scalars, *arrays)


def normalise(values):
    center = values - jnp.mean(values, axis=-1, keepdims=True)
    scale = lax.rsqrt(jnp.mean(center * center, axis=-1, keepdims=True) + epsilon)
    return center * scale, scale


def norm_backward(hat, scale, grad):
    return scale * (
        grad
        - jnp.mean(grad, axis=-1, keepdims=True)
        - hat * jnp.mean(grad * hat, axis=-1, keepdims=True)
    )


def project_kernel(parts, scalars, ins, outs, scratch):
    x, gain, bias, *weights = ins
    normed, q, kv, own = outs
    width = D // parts
    where = scalars[0]
    own.inside[:, 3 * width :] = jnp.zeros((D, D - 3 * width), bf16)
    gain = gain.get()[...].reshape(1, D)
    bias = bias.get()[...].reshape(1, D)
    x.get()
    span = x.inside.shape[0]
    for start in range(0, span, TILE):
        rows = slice(start, start + TILE)
        hat, _ = normalise(x.inside[rows, :].astype(f32))
        normed.inside[rows, :] = (hat * gain + bias).astype(bf16)
    normed.send()
    for w in weights:
        w.get()
    for odd in range(2):

        @pl.when(where[0] % 2 == odd)
        def _():
            for at, w in enumerate(weights):
                own.inside[:, at * width : (at + 1) * width] = w.inside[
                    :, odd * 64 : odd * 64 + width
                ]

    own.send()
    for start in range(0, span, TILE):
        rows = slice(start, start + TILE)
        made = dot(normed.inside[rows, :], own.inside[:, : 3 * width]).astype(bf16)
        q.inside[rows, :] = (made[:, :width].astype(f32) * HDIM**-0.5).astype(bf16)
        kv.inside[rows, :] = made[:, width:]
    kv.send()
    q.send()


def head_mask(heads, width):
    lane = lax.broadcasted_iota(jnp.int32, (1, width), 1)
    return [((lane >= h * HDIM) & (lane < (h + 1) * HDIM)).astype(bf16) for h in range(heads)]


def attention_kernel(heads, span, scalars, ins, outs, scratch):
    where = scalars[0]
    q, kv, feats, kv_far = (one.get() for one in ins)
    mixed_low, mixed_t, lse = (one.inside for one in outs)
    q_head, k, v_t, kf, vf_t = scratch
    width = heads * HDIM
    masks = head_mask(heads, width)
    for h in range(heads):
        q_head[h] = q[...] * masks[h]
    k[...] = kv[:, :width]
    v_t[...] = kv[:, width:].T
    far = kv_far.shape[0] // span

    def turn(j, _):
        rows = pl.ds(pl.multiple_of(j * span, span), span)
        kf[rows, :] = kv_far[rows, :width]
        vf_t[j] = kv_far[rows, width:].T
        return 0

    mine = where[0]
    lax.fori_loop(0, jnp.minimum(mine, far), turn, 0)
    own_start = pl.multiple_of(mine * span, span)
    lse[...] = jnp.zeros(lse.shape, f32)
    for start in range(0, span, TILE):
        for h in range(heads):
            q_tile = q_head[h, start : start + TILE, :]
            f_tile = feats[h, pl.ds(own_start + start, TILE), :]

            def part(k_rows, f_rows, v_rows, low_from, state):
                counts = dot_nt(f_rows, f_tile)
                if low_from is not None:
                    at_k = lax.broadcasted_iota(jnp.int32, counts.shape, 0)
                    at_q = lax.broadcasted_iota(jnp.int32, counts.shape, 1) + low_from
                    counts = jnp.where(at_k <= at_q, counts, 0.0)
                scores = jnp.where(counts > 0, dot_nt(k_rows, q_tile), masked_low)
                top, total, acc = state
                new_top = jnp.maximum(top, jnp.max(scores, axis=0, keepdims=True))
                weights = counts * jnp.exp(scores - new_top)
                factor = jnp.exp(top - new_top)
                return (
                    new_top,
                    total * factor + jnp.sum(weights, axis=0, keepdims=True),
                    acc * factor + dot(v_rows, weights.astype(bf16)),
                )

            state = (
                jnp.full((1, TILE), masked_low, f32),
                jnp.zeros((1, TILE), f32),
                jnp.zeros((HDIM, TILE), f32),
            )
            size = start + TILE
            head_rows = slice(h * HDIM, (h + 1) * HDIM)
            state = part(
                k[:size, :],
                feats[h, pl.ds(own_start, size), :],
                v_t[head_rows, :size],
                start,
                state,
            )

            def far_part(j, state):
                rows = pl.ds(pl.multiple_of(j * span, span), span)
                return part(kf[rows, :], feats[h, rows, :], vf_t[j, head_rows, :], None, state)

            top, total, acc = lax.fori_loop(0, mine, far_part, state)
            done = acc / total
            mixed_t[head_rows, start : start + TILE] = done
            mixed_low[head_rows, start : start + TILE] = done.astype(bf16)
            lse[h : h + 1, start : start + TILE] = top + jnp.log(total)
    for one in outs:
        one.send()


def attention_back_kernel(heads, span, scalars, ins, outs, scratch):
    where = scalars[0]
    parts, q, mixed_t, lse, kv, feats, kv_far = (one.get() for one in ins)
    grad_q, grad_kv, grad_far = (one.inside for one in outs)
    q_head, g_head, dots, probs, slopes, k, v, k_t, gq_t = scratch
    width = heads * HDIM
    masks = head_mask(heads, width)
    mine = where[0]
    far = kv_far.shape[0] // span
    total = parts[0].astype(f32)
    for part in range(1, parts.shape[0]):
        total = total + parts[part].astype(f32)
    low_t = total.astype(bf16)
    low = low_t.T
    for h in range(heads):
        q_head[h] = q[...] * masks[h]
        g_head[h] = low * masks[h]
    product = low_t.astype(f32) * mixed_t[...]
    for h in range(heads):
        dots[h : h + 1, :] = jnp.sum(product[h * HDIM : (h + 1) * HDIM], axis=0, keepdims=True)
    own_start = pl.multiple_of(mine * span, span)

    def block(h, start, size, f_rows, low_from):
        tile = slice(start, start + TILE)
        counts = dot_nt(f_rows, feats[h, pl.ds(own_start + start, TILE), :])
        if low_from is not None:
            at_k = lax.broadcasted_iota(jnp.int32, counts.shape, 0)
            at_q = lax.broadcasted_iota(jnp.int32, counts.shape, 1) + low_from
            counts = jnp.where(at_k <= at_q, counts, 0.0)
        scores = jnp.where(counts > 0, dot_nt(k[:size, :], q_head[h, tile, :]), masked_low)
        prob = counts * jnp.exp(scores - lse[h : h + 1, tile])
        grad_prob = dot_nt(v[:size, :], g_head[h, tile, :])
        slope = prob * (grad_prob - dots[h : h + 1, tile])
        columns = slice(h * span + start, h * span + start + TILE)
        probs[:size, columns] = prob.astype(bf16)
        slopes[:size, columns] = slope.astype(bf16)
        if size < span:
            probs[size:, columns] = jnp.zeros((span - size, TILE), bf16)
            slopes[size:, columns] = jnp.zeros((span - size, TILE), bf16)

    def finish():
        k_t[...] = k[...].T
        grad_v_rows = dot(probs[...], g_head[...].reshape(heads * span, width))
        grad_k_rows = dot(slopes[...], q_head[...].reshape(heads * span, width))
        terms = [
            dot(k_t[h * HDIM : (h + 1) * HDIM, :], slopes[:, h * span : (h + 1) * span])
            for h in range(heads)
        ]
        return grad_k_rows, grad_v_rows, terms

    k[...] = kv[:, :width]
    v[...] = kv[:, width:]
    for start in range(0, span, TILE):
        for h in range(heads):
            size = start + TILE
            block(h, start, size, feats[h, pl.ds(own_start, size), :], start)
    grad_k_rows, grad_v_rows, terms = finish()
    grad_kv[:, :width] = grad_k_rows
    grad_kv[:, width:] = grad_v_rows
    outs[1].send()
    for h in range(heads):
        gq_t[h * HDIM : (h + 1) * HDIM, :] = terms[h]

    def far_block(j, _):
        rows = pl.ds(pl.multiple_of(j * span, span), span)
        k[...] = kv_far[rows, :width]
        v[...] = kv_far[rows, width:]
        for start in range(0, span, TILE):
            for h in range(heads):
                block(h, start, span, feats[h, rows, :], None)
        grad_k_rows, grad_v_rows, terms = finish()
        grad_far[rows, :width] = grad_k_rows.astype(bf16)
        grad_far[rows, width:] = grad_v_rows.astype(bf16)
        for h in range(heads):
            gq_t[h * HDIM : (h + 1) * HDIM, :] += terms[h]
        return 0

    used = jnp.minimum(mine, far)
    lax.fori_loop(0, used, far_block, 0)

    def clear(j, _):
        grad_far[pl.ds(pl.multiple_of(j * span, span), span), :] = jnp.zeros((span, 2 * width), bf16)
        return 0

    lax.fori_loop(used, far, clear, 0)
    outs[2].send()
    grad_q[...] = (gq_t[...] * HDIM**-0.5).T.astype(bf16)
    outs[0].send()


def middle_kernel(pair, scalars, ins, outs, scratch):
    mixed4, x, w_out, gain, bias, w_up, w_down, *c_parts = ins
    gm, gr, sums, ffn, *wide = outs
    act, low, gh, branch, c, resids, made, c4 = scratch
    parts, width, span = mixed4.inside.shape
    for step, one in enumerate(c_parts):
        one.start(target=c4.at[scalars[1][0] ^ step])
    chunk = span // parts
    mixed_t = mixed4.get()[...].reshape(D, span)
    x.get(), w_out.get()
    gain = gain.get()[...].reshape(1, D)
    bias = bias.get()[...].reshape(1, D)
    gain_sum = jnp.zeros((1, D), f32)
    bias_sum = jnp.zeros((1, D), f32)
    for start in range(0, span, TILE):
        rows = slice(start, start + TILE)
        resid = x.inside[rows, :].astype(f32) + dot_tn(mixed_t[:, rows], w_out.inside[...])
        resids[rows, :] = resid
        hat, scale = normalise(resid)
        normed = (hat * gain + bias).astype(bf16)
        low[rows, :] = normed
        w_up.get()
        hidden = dot(normed, w_up.inside[...])
        bell = 0.5 + 0.5 * lax.erf(hidden * (0.5**0.5))
        act[rows, :] = (hidden * bell).astype(bf16)
        slope = bell + hidden * jnp.exp(-0.5 * hidden * hidden) * 0.3989422804014327
        if start == 0:
            w_down.get()
            for one in c_parts:
                one.get()
            for part in range(parts):
                c[:, part * width : (part + 1) * width] = c4[part].T
        grad_hidden = (slope * dot_nt(c[rows, :], w_down.inside[...])).astype(bf16)
        gh[rows, :] = grad_hidden
        grad_normed = dot_nt(grad_hidden, w_up.inside[...])
        gain_sum = gain_sum + jnp.sum(grad_normed * hat, axis=0, keepdims=True)
        bias_sum = bias_sum + jnp.sum(grad_normed, axis=0, keepdims=True)
        grad_resid = norm_backward(hat, scale, grad_normed * gain) + c[rows, :].astype(f32) * (
            1.0 / parts
        )
        gr.inside[rows, :] = grad_resid
        grad_low = grad_resid.astype(bf16)
        branch[rows, :] = grad_low
        for part in range(parts):
            gm.inside[part, :, rows] = dot_nt(
                w_out.inside[part * width : (part + 1) * width, :], grad_low
            ).astype(bf16)
    gm.send()
    gr.send()
    sums.inside[0:1, :] = gain_sum
    sums.inside[1:2, :] = bias_sum
    sums.send()
    where = scalars[0]
    lefts = (lambda: dot_tn(act[...], c[...]), lambda: dot_tn(low[...], gh[...]))
    lefts += (lambda: dot(mixed_t, branch[...]),)
    for at, product in enumerate(lefts):
        if not pair:
            wide[0].inside[at] = product().astype(bf16)
            continue
        made[...] = product().astype(bf16)
        rows_count = wide[0].inside.shape[1]
        size = D // (2 * rows_count)
        for row in range(rows_count):
            for out, half in ((wide[0], where[0]), (wide[1], 1 - where[0])):
                start = pl.multiple_of((2 * row + half) * size, size)
                out.inside[at, row] = made[pl.ds(start, size), :]
        wide[1].send(at)
        wide[0].send(at)
    if not pair:
        wide[0].send()
    for start in range(0, span, TILE):
        rows = slice(start, start + TILE)
        out = dot(act[rows, :], w_down.inside[...]) + resids[rows, :] * (1.0 / parts)
        out_t = out.astype(bf16).T
        for part in range(parts):
            for at in range(start, start + TILE, chunk):
                ffn.inside[part, at // chunk * width : (at // chunk + 1) * width, :] = out_t[
                    part * width : (part + 1) * width, at - start : at - start + chunk
                ]
    ffn.send()


def add_kernel(scalars, ins, outs, scratch):
    keep, more = ins
    keep.get(), more.get()
    for at, out in enumerate(outs):
        block = scalars[0][0] ^ at
        for group in range(keep.inside.shape[0]):
            out.inside[group] = (
                keep.inside[group, block].astype(f32) + more.inside[group, block].astype(f32)
            ).astype(bf16)
    for out in outs[1:] + outs[:1]:
        out.send()


def row_sum_kernel(parts, scalars, ins, outs, scratch):
    ffn_own, both = outs
    (tail,) = scratch
    total = ins[0].get()[...].astype(f32)
    for one in ins[1:-1]:
        total = total + one.get()[...].astype(f32)
    total = total.astype(bf16)
    size = total.shape[1]
    half = size // 2
    width = D // parts
    ffn_own.inside[...] = total[:2].reshape(2 * size, D)
    ffn_own.send()
    for part in range(parts):
        start = part * width
        top = total[2, :half, start : start + width]
        low = total[2, half:, start : start + width]
        tail[part, :half, :] = top[:, :128]
        tail[part, half : 2 * half, :64] = top[:, 128:]
        tail[part, half : 2 * half, 64:] = low[:, :64]
        tail[part, 2 * half :, :] = low[:, 64:]
    span = both.outside.shape[1] - 3 * half
    copies = []
    for part in range(parts):
        copy = pltpu.make_async_copy(
            tail.at[part],
            both.outside.at[part, pl.ds(span, 3 * half), :],
            both.sems.at[next(both.free)],
        )
        copy.start()
        copies.append(copy)
    for copy in copies:
        copy.wait()


SLOT = 64


def last_kernel(parts, pair, scalars, ins, outs, scratch):
    gq, normed, gkv, own, x, gain, gr, sums, gkv_more = ins
    back, *narrow = outs
    grads, small, made = scratch
    width = D // parts
    span = x.inside.shape[0]
    piece = span // parts
    lanes = 3 * width + SLOT
    grads[:, :width] = gq.get()[...]
    grads[:, 3 * width :] = jnp.zeros((span, D - 3 * width), bf16)
    gkv.get(), gkv_more.get()
    grads[:, width : 3 * width] = (
        gkv.inside[...] + gkv_more.inside[...].astype(f32)
    ).astype(bf16)
    own.get(), x.get(), gr.get(), sums.get()
    gain = gain.get()[...].reshape(1, D)
    gain_sum = jnp.zeros((1, D), f32)
    bias_sum = jnp.zeros((1, D), f32)
    for start in range(0, span, TILE):
        rows = slice(start, start + TILE)
        hat, scale = normalise(x.inside[rows, :].astype(f32))
        grad_normed = dot_nt(grads[rows, :], own.inside[...])
        gain_sum = gain_sum + jnp.sum(grad_normed * hat, axis=0, keepdims=True)
        bias_sum = bias_sum + jnp.sum(grad_normed, axis=0, keepdims=True)
        grad_in = gr.inside[rows, :] + norm_backward(hat, scale, grad_normed * gain)
        turned = grad_in.astype(bf16).T
        for at in range(start, start + TILE, piece):
            back.inside[at // piece] = turned[:, at - start : at - start + piece]
    pieces = D // SLOT
    for at, row in enumerate(
        (gain_sum, bias_sum, sums.inside[0:1, :], sums.inside[1:2, :])
    ):
        for part in range(pieces):
            small[at * pieces + part : at * pieces + part + 1, :] = row[
                :, part * SLOT : (part + 1) * SLOT
            ]
    made[...] = dot_tn(normed.get()[...], grads[:, :lanes]).astype(bf16)
    tail = small[...].astype(bf16)
    if pair:
        _, rows_count, size, _ = narrow[0].inside.shape
        for row in range(rows_count):
            for out, half in ((narrow[0], scalars[0][0]), (narrow[1], 1 - scalars[0][0])):
                start = pl.multiple_of((2 * row + half) * size, size)
                out.inside[0, row] = made[pl.ds(start, size), :]
                out.inside[0, row, :48, 3 * width :] = tail
        narrow[1].send()
        narrow[0].send()
    else:
        narrow[0].inside[...] = made[...]
        narrow[0].inside[:48, 3 * width :] = tail
        narrow[0].send()
    back.send()


def own_sum_kernel(parts, count, scalars, ins, outs, scratch):
    mine = outs[0].inside
    tails, small = scratch
    width = D // parts
    size = ins[0].inside.shape[1]
    half = size // 2
    last = ins[count]
    span = last.outside.shape[1] - 3 * half
    last.start(source=last.outside.at[:, pl.ds(span, 3 * half), :], target=tails)
    total = ins[0].get()[0].astype(f32)
    for one in ins[1:count]:
        total = total + one.get()[0].astype(f32)
    mine[:size, : 3 * width] = total[:, : 3 * width].astype(bf16)
    pieces = D // SLOT
    small[...] = jnp.zeros(small.shape, f32)
    for at in range(4):
        for part in range(pieces):
            row = at * pieces + part
            small[at : at + 1, part * SLOT : (part + 1) * SLOT] = total[
                row : row + 1, 3 * width :
            ]
    mine[size:, :] = small[...].astype(bf16)
    last.get()
    out = tails[0].astype(f32)
    for part in range(1, parts):
        out = out + tails[part].astype(f32)
    out = out.astype(bf16)
    start = 3 * width
    mine[:half, start : start + 128] = out[:half]
    mine[:half, start + 128 :] = out[half : 2 * half, :64]
    mine[half:size, start : start + 64] = out[half : 2 * half, 64:]
    mine[half:size, start + 64 :] = out[2 * half :]
    outs[0].send()


def output_kernel(scalars, ins, outs, scratch):
    got = ins[0].get()
    parts, _, piece = got.shape
    width = D // parts
    total = got[0, :D].astype(f32)
    for part in range(1, parts):
        total = total + got[part, :D].astype(f32)
    for at in range(parts):
        outs[0].inside[:, at * piece : (at + 1) * piece] = total[
            at * width : (at + 1) * width
        ].astype(bf16)
    outs[0].send()


def finish_kernel(scalars, ins, outs, scratch):
    grad_in, vectors = outs
    (small,) = scratch
    size = ins[1].outside.shape[1] - 16
    ins[1].start(source=ins[1].outside.at[:, pl.ds(size, 16), :], target=small)
    back = ins[0].get()
    total = back[0].astype(f32)
    for at in range(1, back.shape[0]):
        total = total + back[at].astype(f32)
    grad_in.inside[...] = total.T.astype(bf16)
    grad_in.send()
    ins[1].get()
    sums = small[0].astype(f32)
    for at in range(1, small.shape[0]):
        sums = sums + small[at].astype(f32)
    vectors.inside[...] = sums[:4]
    vectors.send()


def spread_kernel(count, table, where, *refs):
    blocks, outs = refs[:count], refs[-4:]
    for step, members in enumerate(table):

        @pl.when(pl.program_id(0) == step)
        def _():
            part = 0
            for at in members:
                for own in range(blocks[at].shape[0]):
                    total = 4 * blocks[at].shape[0] * len(members)
                    width = 4 * D // total
                    for grad in range(4):
                        outs[grad][:, part * width : (part + 1) * width] = blocks[at][
                            own, :, grad * width : (grad + 1) * width
                        ].astype(f32)
                    part += 1


def spread(row_seq, steps, earlier=None):
    count = sum(len(blocks) for _, _, blocks in steps)
    size = steps[0][2][0].shape[1]
    table, at = [], 0
    for _, _, blocks in steps:
        table.append(tuple(range(at, at + len(blocks))))
        at += len(blocks)
    received = [block for _, _, blocks in steps for block in blocks]
    kept = [] if earlier is None else list(earlier)

    def place(i, w):
        row, seq = jnp.int32(0), jnp.int32(0)
        for step, (row_step, seq_step, _) in enumerate(steps):
            row = jnp.where(i == step, row_step, row)
            seq = jnp.where(i == step, seq_step, seq)
        return (2 * (w[0] ^ row) + (w[1] ^ seq), 0)

    return pl.pallas_call(
        functools.partial(spread_kernel, count, table),
        out_shape=(jax.ShapeDtypeStruct((D, D), f32),) * 4,
        grid_spec=pltpu.PrefetchScalarGridSpec(
            num_scalar_prefetch=1,
            grid=(len(steps),),
            in_specs=[
                pl.BlockSpec(block.shape, lambda i, w: (0, 0, 0)) for block in received
            ]
            + [pl.BlockSpec(memory_space=pl.ANY)] * len(kept),
            out_specs=(pl.BlockSpec((size, D), place),) * 4,
        ),
        input_output_aliases={1 + count + at: at for at in range(len(kept))},
        compiler_params=pltpu.CompilerParams(vmem_limit_bytes=SMALL_LIMIT),
        cost_estimate=pl.CostEstimate(flops=0, bytes_accessed=0, transcendentals=0),
    )(row_seq, *received, *kept)


def spread_ffn_kernel(count, where, *refs):
    blocks, outs = refs[:count], refs[count:]
    size = outs[0].shape[0]
    for at in range(count):

        @pl.when(pl.program_id(0) == at)
        def _():
            outs[0][...] = blocks[at][:size, :].astype(f32)
            outs[1][...] = blocks[at][size:, :].astype(f32)


def spread_ffn(row_seq, mine, other):
    received = [*mine, *other]
    count = len(received)
    rows_count = len(mine)
    size = received[0].shape[0] // 2
    whole = pl.BlockSpec((2 * size, D), lambda i, w: (0, 0))

    def place(i, w):
        return (2 * (w[0] ^ (i % rows_count)) + (w[1] ^ (i // rows_count)), 0)

    return pl.pallas_call(
        functools.partial(spread_ffn_kernel, count),
        out_shape=(jax.ShapeDtypeStruct((D, D), f32),) * 2,
        grid_spec=pltpu.PrefetchScalarGridSpec(
            num_scalar_prefetch=1,
            grid=(count,),
            in_specs=[whole] * count,
            out_specs=(pl.BlockSpec((size, D), place),) * 2,
        ),
        compiler_params=pltpu.CompilerParams(vmem_limit_bytes=SMALL_LIMIT),
        cost_estimate=pl.CostEstimate(flops=0, bytes_accessed=0, transcendentals=0),
    )(row_seq, *received)


def broadcast_exchange(value, axis):
    count = lax.axis_size(axis)
    return lax.all_to_all(
        jnp.broadcast_to(value[None], (count,) + value.shape), axis, 0, 0, tiled=False
    )


def swap(value):
    return lax.ppermute(value, "seq", [(0, 1), (1, 0)])


def trade(value, axis, step):
    return lax.ppermute(value, axis, [(a, a ^ step) for a in range(lax.axis_size(axis))])


def features_kernel(heads, scalars, ins, outs, scratch):
    docs = ins[0].get()[...]
    feats = outs[0].inside
    _, length, _ = feats.shape
    position = lax.broadcasted_iota(jnp.int32, (1, length), 1)
    feature = lax.broadcasted_iota(jnp.int32, (FEATS, length), 0)
    for h in range(heads):
        head = scalars[0][0] * heads + h
        hit = None
        base = 0
        for part, dilation in zip(segment_parts, dilations, strict=True):
            seg_width = length * part // 16
            inside = lax.rem(
                lax.rem(position, seg_width) + dilation - lax.rem(head, dilation), dilation
            )
            key = base + lax.div(position, seg_width) * DOCS + docs
            key = jnp.where(inside == 0, key, -1)
            found = feature == key
            hit = found if hit is None else hit | found
            base += DOCS * (16 // part)
        feats[h] = jnp.where(hit, 1.0, 0.0).T.astype(bf16)
        outs[0].send(h)


def shape(*dims, kind=bf16):
    return jax.ShapeDtypeStruct(dims, kind)


def per_device(
    block_input,
    doc_ids,
    ln1_gain,
    ln1_bias,
    w_query,
    w_key,
    w_value,
    w_out,
    ln2_gain,
    ln2_bias,
    w_up,
    w_down,
    cotangent,
):
    span = block_input.shape[1]
    rows_count = lax.axis_size("row")
    seq_count = lax.axis_size("seq")
    parts = lax.axis_size("pat")
    row_index = lax.axis_index("row")
    seq_index = lax.axis_index("seq")
    pat_index = lax.axis_index("pat")
    pair = seq_count == 2
    heads = HEADS // parts
    width = D // parts
    quarter = span // parts
    size = D // (rows_count * seq_count) if pair else D
    here = seq_index.astype(jnp.int32)[None]
    row_here = row_index.astype(jnp.int32)[None]
    part_here = pat_index.astype(jnp.int32)[None]
    x = block_input[0]

    c_own = cotangent[0].T
    c_parts = [c_own] + [trade(c_own, "pat", s) for s in range(1, parts)]
    (feats,) = staged_call(
        functools.partial(features_kernel, heads),
        [part_here],
        [doc_ids],
        (shape(heads, doc_ids.shape[1], FEATS),),
    )

    def window(scalars):
        return scalars[0][0] * width // 128 * 128

    normed, q, kv, own = staged_call(
        functools.partial(project_kernel, parts),
        [part_here],
        [x, ln1_gain, ln1_bias, w_query, w_key, w_value],
        (shape(span, D), shape(span, width), shape(span, 2 * width), shape(D, D)),
        windows={3: window, 4: window, 5: window},
    )

    kv_far = swap(kv) if pair else lax.all_gather(kv, "seq", axis=0, tiled=True)
    far_rows = kv_far.shape[0]

    mixed, mixed_t, lse = staged_call(
        functools.partial(attention_kernel, heads, span),
        [here],
        [q, kv, feats, kv_far],
        (shape(width, span), shape(width, span, kind=f32), shape(8, span, kind=f32)),
        scratch=[
            pltpu.VMEM((heads, span, width), bf16),
            pltpu.VMEM((span, width), bf16),
            pltpu.VMEM((width, span), bf16),
            pltpu.VMEM((far_rows, width), bf16),
            pltpu.VMEM((far_rows // span, width, span), bf16),
        ],
    )
    mixed, *c_parts = lax.optimization_barrier((mixed, *c_parts))
    mixed4 = lax.all_gather(mixed, "pat")

    wide_shapes = (shape(3, rows_count, size, D),) * 2 if pair else (shape(3, D, D),)
    gm, gr, sums, ffn, *wide = staged_call(
        functools.partial(middle_kernel, pair),
        [here, part_here],
        [mixed4, x, w_out, ln2_gain, ln2_bias, w_up, w_down, *c_parts],
        (
            shape(parts, width, span),
            shape(span, D, kind=f32),
            shape(8, D, kind=f32),
            shape(parts, parts * width + (3 * size // 2 if pair else 0), quarter),
            *wide_shapes,
        ),
        scratch=[pltpu.VMEM((span, D), bf16)] * 5
        + [
            pltpu.VMEM((span, D), f32),
            pltpu.VMEM((D, D), bf16),
            pltpu.VMEM((parts, width, span), bf16),
        ],
        late=parts,
    )
    gm_parts = lax.all_to_all(gm, "pat", 0, 0, tiled=True)

    if pair:
        keep, send = wide
        ordered = staged_call(
            add_kernel, [row_here], [keep, swap(send)], (shape(3, size, D),) * rows_count,
            limit=SMALL_LIMIT,
        )
        received = [ordered[0]] + [trade(ordered[s], "row", s) for s in range(1, rows_count)]
        gm_parts, *_ = lax.optimization_barrier((gm_parts, received[1], received[2]))

    gq, gkv, gkv_far = staged_call(
        functools.partial(attention_back_kernel, heads, span),
        [here],
        [gm_parts, q, mixed_t, lse, kv, feats, kv_far],
        (
            shape(span, width),
            shape(span, 2 * width, kind=f32),
            shape(far_rows, 2 * width),
        ),
        scratch=[
            pltpu.VMEM((heads, span, width), bf16),
            pltpu.VMEM((heads, span, width), bf16),
            pltpu.VMEM((8, span), f32),
            pltpu.VMEM((span, heads * span), bf16),
            pltpu.VMEM((span, heads * span), bf16),
            pltpu.VMEM((span, width), bf16),
            pltpu.VMEM((span, width), bf16),
            pltpu.VMEM((width, span), bf16),
            pltpu.VMEM((width, span), f32),
        ],
    )

    if pair:
        gkv_more = swap(gkv_far)
        ffn_own, ffn = staged_call(
            functools.partial(row_sum_kernel, parts),
            [],
            [*received, ffn],
            (shape(2 * size, D), shape(*ffn.shape)),
            scratch=[pltpu.VMEM((parts, 3 * size // 2, quarter), bf16)],
            limit=SMALL_LIMIT,
            late=1,
            aliases=((rows_count, 1),),
        )
        ffn_parts = lax.all_to_all(ffn, "pat", 0, 0, tiled=True)
    else:
        gkv_more = lax.psum_scatter(gkv_far, "seq", scatter_dimension=0, tiled=True)
        ffn_parts = lax.all_to_all(ffn, "pat", 0, 0, tiled=True)

    lanes = 3 * width + SLOT
    narrow_shapes = (shape(1, rows_count, size, lanes),) * 2 if pair else (shape(D, lanes),)
    back, *narrow = staged_call(
        functools.partial(last_kernel, parts, pair),
        [here],
        [gq, normed, gkv, own, x, ln1_gain, gr, sums, gkv_more],
        (shape(parts, parts * width, quarter), *narrow_shapes),
        scratch=[
            pltpu.VMEM((span, D), bf16),
            pltpu.VMEM((48, SLOT), f32),
            pltpu.VMEM((D, lanes), bf16),
        ],
    )

    if pair:
        keep, send = narrow
        ordered = staged_call(
            add_kernel, [row_here], [keep, swap(send)], (shape(1, size, lanes),) * rows_count,
            limit=SMALL_LIMIT,
        )
        received = [ordered[0]] + [trade(ordered[s], "row", s) for s in range(1, rows_count)]
        ffn_own, *received = lax.optimization_barrier((ffn_own, *received))
        ffn_mine = [ffn_own] + [trade(ffn_own, "row", s) for s in range(1, rows_count)]
        (mine,) = staged_call(
            functools.partial(own_sum_kernel, parts, rows_count),
            [],
            [*received, ffn_parts],
            (shape(size + 16, D),),
            scratch=[
                pltpu.VMEM((parts, 3 * size // 2, quarter), bf16),
                pltpu.VMEM((16, D), f32),
            ],
            limit=SMALL_LIMIT,
            late=1,
        )
        gathered = lax.all_gather(mine, "pat")
        back, gathered, *ffn_mine = lax.optimization_barrier((back, gathered, *ffn_mine))
        back_parts = lax.all_to_all(back, "pat", 0, 0, tiled=True)
        ffn_other = [swap(value) for value in ffn_mine]
        row_seq = jnp.stack([row_index, seq_index]).astype(jnp.int32)
        grad_down, grad_up = spread_ffn(row_seq, ffn_mine, ffn_other)
        a, b = gathered[: parts // 2, :size], gathered[parts // 2 :, :size]
        a1, b2 = trade(a, "row", 1), trade(b, "row", 2)
        b1, a2 = trade(b, "row", 1), trade(a, "row", 2)
        a3, b3 = trade(a1, "row", 2), trade(b2, "row", 1)
        early = [(a, b), (a1, b1), (a2, b2)]
        steps = [(at, 0, pieces) for at, pieces in enumerate(early)] + [
            (at, 1, [swap(piece) for piece in pieces]) for at, pieces in enumerate(early)
        ]
        grads = spread(row_seq, steps)
        far3, near3, *_ = lax.optimization_barrier((a3, b3, grads[0], grad_up))
        grads = spread(row_seq, [(3, 0, (a3, b3)), (3, 1, (swap(far3), swap(near3)))], grads)
    else:
        axes = ("row", "seq")
        back_parts = lax.all_to_all(back, "pat", 0, 0, tiled=True)
        wide_sum = lax.psum(wide[0], axes)
        grad_down, grad_up = wide_sum[0].astype(f32), wide_sum[1].astype(f32)
        grad_out = lax.psum(wide_sum[2], "pat").astype(f32)
        gathered = lax.all_gather(lax.psum(narrow[0], axes), "pat")
        small = gathered[:, :48, 3 * width :].reshape(parts, 4, D)
        small = jnp.pad(small, ((0, 0), (0, 12), (0, 0)))
        grads = [
            gathered[:, :, at * width : (at + 1) * width]
            .astype(f32)
            .transpose(1, 0, 2)
            .reshape(D, D)
            for at in range(3)
        ] + [grad_out]
    (out_t,) = staged_call(
        output_kernel, [], [ffn_parts], (shape(width, span),), limit=SMALL_LIMIT
    )
    grad_in, vectors = staged_call(
        finish_kernel,
        [],
        [back_parts, gathered if pair else small],
        (shape(quarter, D), shape(4, D, kind=f32)),
        scratch=[pltpu.VMEM((parts, 16, D), bf16)],
        limit=SMALL_LIMIT,
        late=1,
    )
    return (
        out_t.T[None],
        grad_in[None],
        vectors[0],
        vectors[1],
        grads[0],
        grads[1],
        grads[2],
        grads[3],
        vectors[2],
        vectors[3],
        grad_up,
        grad_down,
    )


def solution(mesh):
    placed = (
        P("row", "seq", None),
        P("row", None),
        P(),
        P(),
        P(),
        P(),
        P(),
        P(),
        P(),
        P(),
        P(None, "pat"),
        P("pat", None),
        P("row", "seq", "pat"),
    )
    return jax.shard_map(
        per_device,
        mesh=mesh,
        in_specs=placed,
        out_specs=(
            P("row", "seq", "pat"),
            P("row", ("seq", "pat"), None),
            P(),
            P(),
            P(),
            P(),
            P(),
            P(),
            P(),
            P(),
            P(None, "pat"),
            P("pat", None),
        ),
        check_vma=False,
    )
```

```python
import functools

import jax
import jax.numpy as jnp
from jax import lax
from jax.experimental import pallas as pl
from jax.experimental.pallas import tpu as pltpu
from jax.sharding import PartitionSpec as P

D = 768
HEADS = 12
HDIM = 64

epsilon = 1e-05
masked_low = -1e30
segment_parts = (1, 2, 4, 8, 16)
dilations = (1, 2, 4, 6, 12)
DOCS = 3
FEATS = 128
TILE = 256
VMEM_LIMIT = 60 * 1024 * 1024
SMALL_LIMIT = 20 * 1024 * 1024
COPIES = 64
f32 = jnp.float32
bf16 = jnp.bfloat16


def dot(a, b):
    return lax.dot_general(a, b, (((1,), (0,)), ((), ())), preferred_element_type=f32)


def dot_nt(a, b):
    return lax.dot_general(a, b, (((1,), (1,)), ((), ())), preferred_element_type=f32)


def dot_tn(a, b):
    return lax.dot_general(a, b, (((0,), (0,)), ((), ())), preferred_element_type=f32)


class Staged:
    def __init__(self, outside, inside, sems, free):
        self.outside, self.inside, self.sems, self.free = outside, inside, sems, free
        self.pending = []

    def start(self, source=None, target=None):
        copy = pltpu.make_async_copy(
            self.outside if source is None else source,
            self.inside if target is None else target,
            self.sems.at[next(self.free)],
        )
        copy.start()
        self.pending.append(copy)

    def get(self):
        for copy in self.pending:
            copy.wait()
        self.pending = []
        return self.inside

    def put(self, source, target):
        copy = pltpu.make_async_copy(source, target, self.sems.at[next(self.free)])
        copy.start()
        self.pending.append(copy)

    def send(self, at=...):
        copy = pltpu.make_async_copy(
            self.inside.at[at], self.outside.at[at], self.sems.at[next(self.free)]
        )
        copy.start()
        self.pending.append(copy)


def staged_call(body, scalars, arrays, outs, scratch=(), windows=None, limit=VMEM_LIMIT, late=0, aliases=(), bare=(), flops=0):
    windows = windows or {}
    n_scalar, n_in, n_out = len(scalars), len(arrays), len(outs)

    def kernel(*refs):
        scalar_refs, refs = refs[:n_scalar], refs[n_scalar:]
        outside, refs = refs[: n_in + n_out], refs[n_in + n_out :]
        inside, refs = refs[: n_in + n_out], refs[n_in + n_out :]
        sems, rest = refs[0], refs[1:]
        free = iter(range(COPIES))
        every = [Staged(o, i, sems, free) for o, i in zip(outside, inside, strict=True)]
        ins, results = every[:n_in], every[n_in:]
        for at, one in enumerate(ins[: n_in - late]):
            if at in windows:
                start = windows[at](scalar_refs)
                size = one.inside.shape[-1]
                one.start(one.outside.at[:, pl.ds(pl.multiple_of(start, 128), size)])
            else:
                one.start()
        body(scalar_refs, ins, results, rest)
        for one in ins + results:
            one.get()

    def buffer(at, array):
        dims = array.shape
        if at >= n_in - late:
            return pltpu.VMEM((16, 128), array.dtype)
        if at in windows:
            dims = (*dims[:-1], 256)
        return pltpu.VMEM(dims, array.dtype)

    return pl.pallas_call(
        kernel,
        out_shape=tuple(outs),
        in_specs=[pl.BlockSpec(memory_space=pltpu.SMEM)] * n_scalar
        + [pl.BlockSpec(memory_space=pl.ANY)] * n_in,
        out_specs=(pl.BlockSpec(memory_space=pltpu.HBM),) * n_out,
        scratch_shapes=[buffer(at, a) for at, a in enumerate(arrays)]
        + [
            pltpu.VMEM((16, 128) if at in bare else o.shape, o.dtype)
            for at, o in enumerate(outs)
        ]
        + [pltpu.SemaphoreType.DMA((COPIES,))]
        + list(scratch),
        input_output_aliases={n_scalar + a: o for a, o in aliases},
        compiler_params=pltpu.CompilerParams(vmem_limit_bytes=limit),
        cost_estimate=pl.CostEstimate(flops=flops, bytes_accessed=0, transcendentals=0),
    )(*scalars, *arrays)


def normalise(values):
    center = values - jnp.mean(values, axis=-1, keepdims=True)
    scale = lax.rsqrt(jnp.mean(center * center, axis=-1, keepdims=True) + epsilon)
    return center * scale, scale


def norm_backward(hat, scale, grad):
    return scale * (
        grad
        - jnp.mean(grad, axis=-1, keepdims=True)
        - hat * jnp.mean(grad * hat, axis=-1, keepdims=True)
    )


def project_kernel(parts, scalars, ins, outs, scratch):
    x, gain, bias, *weights = ins
    normed, q, kv, own = outs
    width = D // parts
    where = scalars[0]
    own.inside[:, 3 * width :] = jnp.zeros((D, D - 3 * width), bf16)
    gain = gain.get()[...].reshape(1, D)
    bias = bias.get()[...].reshape(1, D)
    x.get()
    span = x.inside.shape[0]
    for start in range(0, span, TILE):
        rows = slice(start, start + TILE)
        hat, _ = normalise(x.inside[rows, :].astype(f32))
        normed.inside[rows, :] = (hat * gain + bias).astype(bf16)
    normed.send()
    for w in weights:
        w.get()
    for odd in range(2):

        @pl.when(where[0] % 2 == odd)
        def _():
            for at, w in enumerate(weights):
                own.inside[:, at * width : (at + 1) * width] = w.inside[
                    :, odd * 64 : odd * 64 + width
                ]

    own.send()
    for start in range(0, span, TILE):
        rows = slice(start, start + TILE)
        made = dot(normed.inside[rows, :], own.inside[:, : 3 * width]).astype(bf16)
        q.inside[rows, :] = (made[:, :width].astype(f32) * HDIM**-0.5).astype(bf16)
        kv.inside[rows, :] = made[:, width:]
    kv.send()
    q.send()


def head_mask(heads, width):
    lane = lax.broadcasted_iota(jnp.int32, (1, width), 1)
    return [((lane >= h * HDIM) & (lane < (h + 1) * HDIM)).astype(bf16) for h in range(heads)]


def attention_kernel(heads, span, scalars, ins, outs, scratch):
    where = scalars[0]
    q, kv, feats, kv_far = (one.get() for one in ins)
    mixed_low, mixed_t, lse = (one.inside for one in outs)
    q_head, k, v_t, kf, vf_t, tops, totals = scratch
    width = heads * HDIM
    masks = head_mask(heads, width)
    for h in range(heads):
        q_head[h] = q[...] * masks[h]
    k[...] = kv[:, :width]
    v_t[...] = kv[:, width:].T
    far = kv_far.shape[0] // span

    def turn(j, _):
        rows = pl.ds(pl.multiple_of(j * span, span), span)
        kf[rows, :] = kv_far[rows, :width]
        vf_t[j] = kv_far[rows, width:].T
        return 0

    mine = where[0]
    lax.fori_loop(0, jnp.minimum(mine, far), turn, 0)
    own_start = pl.multiple_of(mine * span, span)
    lse[...] = jnp.zeros(lse.shape, f32)
    pairs = [(start, h) for start in range(0, span, TILE) for h in range(heads)]

    def part(start, h, k_rows, f_rows, v_rows, causal):
        counts = dot_nt(f_rows, feats[h, pl.ds(own_start + start, TILE), :])
        if causal:
            at_k = lax.broadcasted_iota(jnp.int32, counts.shape, 0)
            at_q = lax.broadcasted_iota(jnp.int32, counts.shape, 1) + start
            counts = jnp.where(at_k <= at_q, counts, 0.0)
        scores = dot_nt(k_rows, q_head[h, start : start + TILE, :])
        scores = jnp.where(counts > 0, scores, masked_low)
        return counts, scores, v_rows

    for at, (start, h) in enumerate(pairs):
        size = start + TILE
        head_rows = slice(h * HDIM, (h + 1) * HDIM)
        counts, scores, v_rows = part(
            start,
            h,
            k[:size, :],
            feats[h, pl.ds(own_start, size), :],
            v_t[head_rows, :size],
            True,
        )
        top = jnp.max(scores, axis=0, keepdims=True)
        weights = counts * jnp.exp(scores - top)
        tops[at : at + 1, :] = top
        totals[at : at + 1, :] = jnp.sum(weights, axis=0, keepdims=True)
        mixed_t[head_rows, start : start + TILE] = dot(v_rows, weights.astype(bf16))

    def far_step(j, _):
        rows = pl.ds(pl.multiple_of(j * span, span), span)
        for at, (start, h) in enumerate(pairs):
            head_rows = slice(h * HDIM, (h + 1) * HDIM)
            counts, scores, v_rows = part(
                start, h, kf[rows, :], feats[h, rows, :], vf_t[j, head_rows, :], False
            )
            top = tops[at : at + 1, :]
            new_top = jnp.maximum(top, jnp.max(scores, axis=0, keepdims=True))
            weights = counts * jnp.exp(scores - new_top)
            factor = jnp.exp(top - new_top)
            tops[at : at + 1, :] = new_top
            totals[at : at + 1, :] = totals[at : at + 1, :] * factor + jnp.sum(
                weights, axis=0, keepdims=True
            )
            mixed_t[head_rows, start : start + TILE] = mixed_t[
                head_rows, start : start + TILE
            ] * factor + dot(v_rows, weights.astype(bf16))
        return 0

    lax.fori_loop(0, mine, far_step, 0)
    for at, (start, h) in enumerate(pairs):
        head_rows = slice(h * HDIM, (h + 1) * HDIM)
        total = totals[at : at + 1, :]
        done = mixed_t[head_rows, start : start + TILE] / total
        mixed_t[head_rows, start : start + TILE] = done
        mixed_low[head_rows, start : start + TILE] = done.astype(bf16)
        lse[h : h + 1, start : start + TILE] = tops[at : at + 1, :] + jnp.log(total)
    for one in outs:
        one.send()


def attention_back_kernel(heads, span, scalars, ins, outs, scratch):
    where = scalars[0]
    parts, q, mixed_t, lse, kv, feats, kv_far = (one.get() for one in ins)
    grad_q, grad_kv, grad_far = (one.inside for one in outs)
    q_head, g_head, dots, probs, slopes, k, v, k_t, gq_t = scratch
    width = heads * HDIM
    masks = head_mask(heads, width)
    mine = where[0]
    far = kv_far.shape[0] // span
    total = parts[0].astype(f32)
    for part in range(1, parts.shape[0]):
        total = total + parts[part].astype(f32)
    low_t = total.astype(bf16)
    low = low_t.T
    for h in range(heads):
        q_head[h] = q[...] * masks[h]
        g_head[h] = low * masks[h]
    product = low_t.astype(f32) * mixed_t[...]
    for h in range(heads):
        dots[h : h + 1, :] = jnp.sum(product[h * HDIM : (h + 1) * HDIM], axis=0, keepdims=True)
    own_start = pl.multiple_of(mine * span, span)

    def block(h, start, size, f_rows, low_from):
        tile = slice(start, start + TILE)
        counts = dot_nt(f_rows, feats[h, pl.ds(own_start + start, TILE), :])
        if low_from is not None:
            at_k = lax.broadcasted_iota(jnp.int32, counts.shape, 0)
            at_q = lax.broadcasted_iota(jnp.int32, counts.shape, 1) + low_from
            counts = jnp.where(at_k <= at_q, counts, 0.0)
        scores = jnp.where(counts > 0, dot_nt(k[:size, :], q_head[h, tile, :]), masked_low)
        prob = counts * jnp.exp(scores - lse[h : h + 1, tile])
        grad_prob = dot_nt(v[:size, :], g_head[h, tile, :])
        slope = prob * (grad_prob - dots[h : h + 1, tile])
        columns = slice(h * span + start, h * span + start + TILE)
        probs[:size, columns] = prob.astype(bf16)
        slopes[:size, columns] = slope.astype(bf16)
        if size < span:
            probs[size:, columns] = jnp.zeros((span - size, TILE), bf16)
            slopes[size:, columns] = jnp.zeros((span - size, TILE), bf16)

    def finish():
        k_t[...] = k[...].T
        grad_v_rows = dot(probs[...], g_head[...].reshape(heads * span, width))
        grad_k_rows = dot(slopes[...], q_head[...].reshape(heads * span, width))
        terms = [
            dot(k_t[h * HDIM : (h + 1) * HDIM, :], slopes[:, h * span : (h + 1) * span])
            for h in range(heads)
        ]
        return grad_k_rows, grad_v_rows, terms

    k[...] = kv[:, :width]
    v[...] = kv[:, width:]
    for start in range(0, span, TILE):
        for h in range(heads):
            size = start + TILE
            block(h, start, size, feats[h, pl.ds(own_start, size), :], start)
    grad_k_rows, grad_v_rows, terms = finish()
    grad_kv[:, :width] = grad_k_rows
    grad_kv[:, width:] = grad_v_rows
    outs[1].send()
    for h in range(heads):
        gq_t[h * HDIM : (h + 1) * HDIM, :] = terms[h]

    def far_block(j, _):
        rows = pl.ds(pl.multiple_of(j * span, span), span)
        k[...] = kv_far[rows, :width]
        v[...] = kv_far[rows, width:]
        for start in range(0, span, TILE):
            for h in range(heads):
                block(h, start, span, feats[h, rows, :], None)
        grad_k_rows, grad_v_rows, terms = finish()
        grad_far[rows, :width] = grad_k_rows.astype(bf16)
        grad_far[rows, width:] = grad_v_rows.astype(bf16)
        for h in range(heads):
            gq_t[h * HDIM : (h + 1) * HDIM, :] += terms[h]
        return 0

    used = jnp.minimum(mine, far)
    lax.fori_loop(0, used, far_block, 0)

    def clear(j, _):
        grad_far[pl.ds(pl.multiple_of(j * span, span), span), :] = jnp.zeros((span, 2 * width), bf16)
        return 0

    lax.fori_loop(used, far, clear, 0)
    outs[2].send()
    grad_q[...] = (gq_t[...] * HDIM**-0.5).T.astype(bf16)
    outs[0].send()


def middle_kernel(scalars, ins, outs, scratch):
    mixed4, x, w_out, gain, bias, w_up, w_down, *c_parts = ins
    gm, sums, act, gh, branch, low, c, resids = outs
    (c4,) = scratch
    parts, width, span = mixed4.inside.shape
    for step, one in enumerate(c_parts):
        one.start(target=c4.at[scalars[0][0] ^ step])
    mixed_t = mixed4.get()[...].reshape(D, span)
    x.get(), w_out.get()
    gain = gain.get()[...].reshape(1, D)
    bias = bias.get()[...].reshape(1, D)
    gain_sum = jnp.zeros((1, D), f32)
    bias_sum = jnp.zeros((1, D), f32)
    for start in range(0, span, TILE):
        rows = slice(start, start + TILE)
        resid = x.inside[rows, :].astype(f32) + dot_tn(mixed_t[:, rows], w_out.inside[...])
        resids.inside[rows, :] = resid.astype(bf16)
        hat, scale = normalise(resid)
        normed = (hat * gain + bias).astype(bf16)
        low.inside[rows, :] = normed
        w_up.get()
        hidden = dot(normed, w_up.inside[...])
        bell = 0.5 + 0.5 * lax.erf(hidden * (0.5**0.5))
        act.inside[rows, :] = (hidden * bell).astype(bf16)
        slope = bell + hidden * jnp.exp(-0.5 * hidden * hidden) * 0.3989422804014327
        if start == 0:
            w_down.get()
            for one in c_parts:
                one.get()
            for part in range(parts):
                c.inside[:, part * width : (part + 1) * width] = c4[part].T
            c.send()
        c_rows = c.inside[rows, :]
        grad_hidden = (slope * dot_nt(c_rows, w_down.inside[...])).astype(bf16)
        gh.inside[rows, :] = grad_hidden
        grad_normed = dot_nt(grad_hidden, w_up.inside[...])
        gain_sum = gain_sum + jnp.sum(grad_normed * hat, axis=0, keepdims=True)
        bias_sum = bias_sum + jnp.sum(grad_normed, axis=0, keepdims=True)
        grad_resid = norm_backward(hat, scale, grad_normed * gain) + c_rows.astype(f32) * (
            1.0 / parts
        )
        grad_low = grad_resid.astype(bf16)
        branch.inside[rows, :] = grad_low
        for one in (act, low, gh, resids, branch):
            one.send(pl.ds(start, TILE))
        for part in range(parts):
            gm.inside[part, :, rows] = dot_nt(
                w_out.inside[part * width : (part + 1) * width, :], grad_low
            ).astype(bf16)
    sums.inside[0:1, :] = gain_sum
    sums.inside[1:2, :] = bias_sum
    gm.send()
    sums.send()


def weights_kernel(pair, scalars, ins, outs, scratch):
    act, c, low, gh, mixed4, branch, w_down, resids = ins
    ffn, *wide = outs
    (made,) = scratch
    parts, width, span = mixed4.inside.shape
    chunk = span // parts
    where = scalars[0]

    def out_product():
        mixed_t = mixed4.get()[...].reshape(D, span)
        return dot(mixed_t, branch.get()[...])

    products = (
        lambda: dot_tn(act.get()[...], c.get()[...]),
        lambda: dot_tn(low.get()[...], gh.get()[...]),
        out_product,
    )
    for at, product in enumerate(products):
        if not pair:
            wide[0].inside[at] = product().astype(bf16)
            continue
        made[...] = product().astype(bf16)
        rows_count = wide[0].inside.shape[1]
        size = D // (2 * rows_count)
        for row in range(rows_count):
            for out, half in ((wide[0].inside.at[at], where[0]), (wide[1 + at].inside, 1 - where[0])):
                start = pl.multiple_of((2 * row + half) * size, size)
                out[row] = made[pl.ds(start, size), :]
        wide[1 + at].send()
        wide[0].send(at)
    if not pair:
        wide[0].send()
    w_down.get(), resids.get()
    for start in range(0, span, TILE):
        rows = slice(start, start + TILE)
        out = dot(act.inside[rows, :], w_down.inside[...]) + resids.inside[rows, :].astype(f32) * (
            1.0 / parts
        )
        out_t = out.astype(bf16).T
        for part in range(parts):
            for at in range(start, start + TILE, chunk):
                ffn.inside[part, at // chunk * width : (at // chunk + 1) * width, :] = out_t[
                    part * width : (part + 1) * width, at - start : at - start + chunk
                ]
    ffn.send()


def add_kernel(scalars, ins, outs, scratch):
    keep, *more = ins
    keep.get()
    for group, one in enumerate(more):
        one.get()
        for at, out in enumerate(outs):
            block = scalars[0][0] ^ at
            out.inside[group] = (
                keep.inside[group, block].astype(f32) + one.inside[block].astype(f32)
            ).astype(bf16)
    for out in outs[1:] + outs[:1]:
        out.send()


def row_sum_kernel(parts, scalars, ins, outs, scratch):
    ffn_own, *out_parts = outs
    (rows,) = scratch
    total = ins[0].get()[...].astype(f32)
    for one in ins[1:]:
        total = total + one.get()[...].astype(f32)
    total = total.astype(bf16)
    size = total.shape[1]
    half = size // 2
    width = D // parts
    for own in range(parts):

        @pl.when(scalars[0][0] == own)
        def _():
            for step, out in enumerate(out_parts):
                part = own ^ step
                columns = slice(part * width, (part + 1) * width)
                out.inside[:, :width] = total[2, :half, columns]
                out.inside[:, width:] = total[2, half:, columns]

    for one in out_parts[::-1]:
        one.send()
    rows[...] = total[:2].reshape(2 * size, D)
    for row in range(ffn_own.outside.shape[0]):
        ffn_own.put(rows, ffn_own.outside.at[row])


SLOT = 64


def last_kernel(parts, pair, scalars, ins, outs, scratch):
    gq, normed, gkv, own, x, gain, gr, sums, gkv_more = ins
    back, *narrow = outs
    grads, small, made = scratch
    width = D // parts
    span = x.inside.shape[0]
    piece = span // parts
    lanes = 3 * width + SLOT
    grads[:, :width] = gq.get()[...]
    grads[:, 3 * width :] = jnp.zeros((span, D - 3 * width), bf16)
    gkv.get(), gkv_more.get()
    grads[:, width : 3 * width] = (
        gkv.inside[...] + gkv_more.inside[...].astype(f32)
    ).astype(bf16)
    own.get(), x.get(), gr.get(), sums.get()
    gain = gain.get()[...].reshape(1, D)
    gain_sum = jnp.zeros((1, D), f32)
    bias_sum = jnp.zeros((1, D), f32)
    for start in range(0, span, TILE):
        rows = slice(start, start + TILE)
        hat, scale = normalise(x.inside[rows, :].astype(f32))
        grad_normed = dot_nt(grads[rows, :], own.inside[...])
        gain_sum = gain_sum + jnp.sum(grad_normed * hat, axis=0, keepdims=True)
        bias_sum = bias_sum + jnp.sum(grad_normed, axis=0, keepdims=True)
        grad_in = gr.inside[rows, :].astype(f32) + norm_backward(hat, scale, grad_normed * gain)
        turned = grad_in.astype(bf16).T
        for at in range(start, start + TILE, piece):
            back.inside[at // piece] = turned[:, at - start : at - start + piece]
    pieces = D // SLOT
    for at, row in enumerate(
        (gain_sum, bias_sum, sums.inside[0:1, :], sums.inside[1:2, :])
    ):
        for part in range(pieces):
            small[at * pieces + part : at * pieces + part + 1, :] = row[
                :, part * SLOT : (part + 1) * SLOT
            ]
    made[...] = dot_tn(normed.get()[...], grads[:, :lanes]).astype(bf16)
    tail = small[...].astype(bf16)
    if pair:
        rows_count, size, _ = narrow[1].inside.shape
        for row in range(rows_count):
            for out, half in (
                (narrow[0].inside.at[0], scalars[0][0]),
                (narrow[1].inside, 1 - scalars[0][0]),
            ):
                start = pl.multiple_of((2 * row + half) * size, size)
                out[row] = made[pl.ds(start, size), :]
                out[row, :48, 3 * width :] = tail
        narrow[1].send()
        narrow[0].send()
    else:
        narrow[0].inside[...] = made[...]
        narrow[0].inside[:48, 3 * width :] = tail
        narrow[0].send()
    back.send()


def own_sum_kernel(parts, count, scalars, ins, outs, scratch):
    mine = outs[0].inside
    (small,) = scratch
    width = D // parts
    size = ins[0].inside.shape[1]
    half = size // 2
    out = ins[count].get()[...].astype(f32)
    for one in ins[count + 1 :]:
        out = out + one.get()[...].astype(f32)
    mine[:half, 3 * width :] = out[:, :width].astype(bf16)
    mine[half:size, 3 * width :] = out[:, width:].astype(bf16)
    total = ins[0].get()[0].astype(f32)
    for one in ins[1:count]:
        total = total + one.get()[0].astype(f32)
    mine[:size, : 3 * width] = total[:, : 3 * width].astype(bf16)
    pieces = D // SLOT
    small[...] = jnp.zeros(small.shape, f32)
    for at in range(4):
        for part in range(pieces):
            row = at * pieces + part
            small[at : at + 1, part * SLOT : (part + 1) * SLOT] = total[
                row : row + 1, 3 * width :
            ]
    mine[size:, :] = small[...].astype(bf16)
    outs[0].send()


def output_kernel(scalars, ins, outs, scratch):
    got = ins[0].get()
    parts, _, piece = got.shape
    width = D // parts
    total = got[0, :D].astype(f32)
    for part in range(1, parts):
        total = total + got[part, :D].astype(f32)
    for at in range(parts):
        outs[0].inside[:, at * piece : (at + 1) * piece] = total[
            at * width : (at + 1) * width
        ].astype(bf16)
    outs[0].send()


def finish_kernel(scalars, ins, outs, scratch):
    grad_in, vectors = outs
    (small,) = scratch
    size = ins[1].outside.shape[1] - 16
    ins[1].start(source=ins[1].outside.at[:, pl.ds(size, 16), :], target=small)
    back = ins[0].get()
    total = back[0].astype(f32)
    for at in range(1, back.shape[0]):
        total = total + back[at].astype(f32)
    grad_in.inside[...] = total.T.astype(bf16)
    grad_in.send()
    ins[1].get()
    sums = small[0].astype(f32)
    for at in range(1, small.shape[0]):
        sums = sums + small[at].astype(f32)
    vectors.inside[...] = sums[:4]
    vectors.send()


def spread_kernel(steps, scalars, ins, outs, scratch):
    (buffer,) = scratch
    row, seq = scalars
    size = buffer.shape[2]
    at = 0
    for step, (row_step, seq_step, count) in enumerate(steps):
        part = 0
        for one in ins[at : at + count]:
            got = one.get()
            for own in range(got.shape[0]):
                width = D // (got.shape[0] * count)
                columns = slice(part * width, (part + 1) * width)
                for grad in range(4):
                    buffer[grad, step, :, columns] = got[
                        own, :, grad * width : (grad + 1) * width
                    ].astype(f32)
                part += 1
        at += count
        start = pl.multiple_of((2 * (row[0] ^ row_step) + (seq[0] ^ seq_step)) * size, size)
        for grad in range(4):
            out = outs[grad]
            out.put(buffer.at[grad, step], out.outside.at[pl.ds(start, size), :])


def spread(row_here, here, steps, earlier=(), flops=0):
    count = sum(len(blocks) for _, _, blocks in steps)
    size = steps[0][2][0].shape[1]
    received = [block for _, _, blocks in steps for block in blocks]
    return staged_call(
        functools.partial(spread_kernel, [(a, b, len(c)) for a, b, c in steps]),
        [row_here, here],
        [*received, *earlier],
        (shape(D, D, kind=f32),) * 4,
        scratch=[pltpu.VMEM((4, len(steps), size, D), f32)],
        limit=SMALL_LIMIT,
        late=len(earlier),
        aliases=tuple((count + at, at) for at in range(len(earlier))),
        bare=range(4),
        flops=flops,
    )


def spread_ffn_kernel(scalars, ins, outs, scratch):
    (buffer,) = scratch
    size = buffer.shape[2]
    for half, one in enumerate(ins):
        got = one.get()
        for row in range(got.shape[0]):
            start = pl.multiple_of((2 * row + (scalars[0][0] ^ half)) * size, size)
            for grad, out in enumerate(outs):
                place = buffer.at[grad, half * got.shape[0] + row]
                place[...] = got[row, grad * size : (grad + 1) * size, :].astype(f32)
                out.put(place, out.outside.at[pl.ds(start, size), :])


def broadcast_exchange(value, axis):
    count = lax.axis_size(axis)
    return lax.all_to_all(
        jnp.broadcast_to(value[None], (count,) + value.shape), axis, 0, 0, tiled=False
    )


def swap(value):
    return lax.ppermute(value, "seq", [(0, 1), (1, 0)])


def trade(value, axis, step):
    return lax.ppermute(value, axis, [(a, a ^ step) for a in range(lax.axis_size(axis))])


def features_kernel(heads, scalars, ins, outs, scratch):
    docs = ins[0].get()[...]
    feats = outs[0].inside
    _, length, _ = feats.shape
    position = lax.broadcasted_iota(jnp.int32, (1, length), 1)
    feature = lax.broadcasted_iota(jnp.int32, (FEATS, length), 0)
    for h in range(heads):
        head = scalars[0][0] * heads + h
        hit = None
        base = 0
        for part, dilation in zip(segment_parts, dilations, strict=True):
            seg_width = length * part // 16
            inside = lax.rem(
                lax.rem(position, seg_width) + dilation - lax.rem(head, dilation), dilation
            )
            key = base + lax.div(position, seg_width) * DOCS + docs
            key = jnp.where(inside == 0, key, -1)
            found = feature == key
            hit = found if hit is None else hit | found
            base += DOCS * (16 // part)
        feats[h] = jnp.where(hit, 1.0, 0.0).T.astype(bf16)
        outs[0].send(h)


def shape(*dims, kind=bf16):
    return jax.ShapeDtypeStruct(dims, kind)


def per_device(
    block_input,
    doc_ids,
    ln1_gain,
    ln1_bias,
    w_query,
    w_key,
    w_value,
    w_out,
    ln2_gain,
    ln2_bias,
    w_up,
    w_down,
    cotangent,
):
    span = block_input.shape[1]
    rows_count = lax.axis_size("row")
    seq_count = lax.axis_size("seq")
    parts = lax.axis_size("pat")
    row_index = lax.axis_index("row")
    seq_index = lax.axis_index("seq")
    pat_index = lax.axis_index("pat")
    pair = seq_count == 2
    heads = HEADS // parts
    width = D // parts
    quarter = span // parts
    size = D // (rows_count * seq_count) if pair else D
    here = seq_index.astype(jnp.int32)[None]
    row_here = row_index.astype(jnp.int32)[None]
    part_here = pat_index.astype(jnp.int32)[None]
    x = block_input[0]

    c_own = cotangent[0].T
    c_parts = [c_own] + [trade(c_own, "pat", s) for s in range(1, parts)]
    (feats,) = staged_call(
        functools.partial(features_kernel, heads),
        [part_here],
        [doc_ids],
        (shape(heads, doc_ids.shape[1], FEATS),),
        flops=1 << 42,
    )

    def window(scalars):
        return scalars[0][0] * width // 128 * 128

    normed, q, kv, own = staged_call(
        functools.partial(project_kernel, parts),
        [part_here],
        [x, ln1_gain, ln1_bias, w_query, w_key, w_value],
        (shape(span, D), shape(span, width), shape(span, 2 * width), shape(D, D)),
        windows={3: window, 4: window, 5: window},
    )

    kv_far = swap(kv) if pair else lax.all_gather(kv, "seq", axis=0, tiled=True)
    far_rows = kv_far.shape[0]

    mixed, mixed_t, lse = staged_call(
        functools.partial(attention_kernel, heads, span),
        [here],
        [q, kv, feats, kv_far],
        (shape(width, span), shape(width, span, kind=f32), shape(8, span, kind=f32)),
        scratch=[
            pltpu.VMEM((heads, span, width), bf16),
            pltpu.VMEM((span, width), bf16),
            pltpu.VMEM((width, span), bf16),
            pltpu.VMEM((far_rows, width), bf16),
            pltpu.VMEM((far_rows // span, width, span), bf16),
            pltpu.VMEM((heads * span // TILE + 8, TILE), f32),
            pltpu.VMEM((heads * span // TILE + 8, TILE), f32),
        ],
    )
    mixed, *c_parts = lax.optimization_barrier((mixed, *c_parts))
    mixed4 = lax.all_gather(mixed, "pat")

    wide_shapes = (shape(3, D, D),)
    if pair:
        wide_shapes = (shape(3, rows_count, size, D),) + (shape(rows_count, size, D),) * 3
    gm, sums, act, gh, branch, low, c, resids = staged_call(
        middle_kernel,
        [part_here],
        [mixed4, x, w_out, ln2_gain, ln2_bias, w_up, w_down, *c_parts],
        (shape(parts, width, span), shape(8, D, kind=f32)) + (shape(span, D),) * 6,
        scratch=[pltpu.VMEM((parts, width, span), bf16)],
        late=parts,
    )
    gm_parts = lax.all_to_all(gm, "pat", 0, 0, tiled=True)
    ffn, *wide = staged_call(
        functools.partial(weights_kernel, pair),
        [here],
        [act, c, low, gh, mixed4, branch, w_down, resids],
        (shape(parts, parts * width, quarter), *wide_shapes),
        scratch=[pltpu.VMEM((D, D), bf16)],
        flops=1 << 42,
    )

    if pair:
        keep, *sends = wide
        ordered = staged_call(
            add_kernel,
            [row_here],
            [keep, *[swap(send) for send in sends]],
            (shape(3, size, D),) * rows_count,
            limit=SMALL_LIMIT,
        )
        wide_parts = [ordered[0]] + [trade(ordered[s], "row", s) for s in range(1, rows_count)]

    ffn, _ = lax.optimization_barrier((ffn, gm_parts))
    ffn_parts = lax.all_to_all(ffn, "pat", 0, 0, tiled=True)
    (out_t,) = staged_call(
        output_kernel,
        [],
        [ffn_parts],
        (shape(width, span),),
        limit=SMALL_LIMIT,
        flops=1 << 42,
    )
    gq, gkv, gkv_far = staged_call(
        functools.partial(attention_back_kernel, heads, span),
        [here],
        [gm_parts, q, mixed_t, lse, kv, feats, kv_far],
        (
            shape(span, width),
            shape(span, 2 * width, kind=f32),
            shape(far_rows, 2 * width),
        ),
        scratch=[
            pltpu.VMEM((heads, span, width), bf16),
            pltpu.VMEM((heads, span, width), bf16),
            pltpu.VMEM((8, span), f32),
            pltpu.VMEM((span, heads * span), bf16),
            pltpu.VMEM((span, heads * span), bf16),
            pltpu.VMEM((span, width), bf16),
            pltpu.VMEM((span, width), bf16),
            pltpu.VMEM((width, span), bf16),
            pltpu.VMEM((width, span), f32),
        ],
        flops=1 << 42,
    )

    if pair:
        gkv_more = swap(gkv_far)
        ffn_own, *out_parts = staged_call(
            functools.partial(row_sum_kernel, parts),
            [part_here],
            wide_parts,
            (shape(rows_count, 2 * size, D),) + (shape(size // 2, 2 * width),) * parts,
            scratch=[pltpu.VMEM((2 * size, D), bf16)],
            limit=SMALL_LIMIT,
            bare=(0,),
        )
        out_parts = [out_parts[0]] + [trade(out_parts[s], "pat", s) for s in range(1, parts)]
    else:
        gkv_more = lax.psum_scatter(gkv_far, "seq", scatter_dimension=0, tiled=True)

    lanes = 3 * width + SLOT
    narrow_shapes = (shape(1, rows_count, size, lanes), shape(rows_count, size, lanes)) if pair else (shape(D, lanes),)
    back, *narrow = staged_call(
        functools.partial(last_kernel, parts, pair),
        [here],
        [gq, normed, gkv, own, x, ln1_gain, branch, sums, gkv_more],
        (shape(parts, parts * width, quarter), *narrow_shapes),
        scratch=[
            pltpu.VMEM((span, D), bf16),
            pltpu.VMEM((48, SLOT), f32),
            pltpu.VMEM((D, lanes), bf16),
        ],
    )

    if pair:
        keep, send = narrow
        send, *_ = lax.optimization_barrier((send, *wide_parts[1:]))
        ordered = staged_call(
            add_kernel, [row_here], [keep, swap(send)], (shape(1, size, lanes),) * rows_count,
            limit=SMALL_LIMIT,
        )
        received = [ordered[0]] + [trade(ordered[s], "row", s) for s in range(1, rows_count)]
        received[3], _ = lax.optimization_barrier((received[3], out_t))
        (mine,) = staged_call(
            functools.partial(own_sum_kernel, parts, rows_count),
            [],
            [*received, *out_parts],
            (shape(size + 16, D),),
            scratch=[pltpu.VMEM((16, D), f32)],
            limit=SMALL_LIMIT,
        )
        gathered = lax.all_gather(mine, "pat")
        ffn_own, *_ = lax.optimization_barrier(
            (ffn_own, ffn_parts, *received[1:], *out_parts[1:])
        )
        ffn_mine = lax.all_to_all(ffn_own, "row", 0, 0, tiled=True)
        gathered, ffn_mine, back = lax.optimization_barrier((gathered, ffn_mine, back))
        back_parts = lax.all_to_all(back, "pat", 0, 0, tiled=True)
        grad_down, grad_up = staged_call(
            spread_ffn_kernel,
            [here],
            [ffn_mine, swap(ffn_mine)],
            (shape(D, D, kind=f32),) * 2,
            scratch=[pltpu.VMEM((2, 2 * rows_count, size, D), f32)],
            limit=SMALL_LIMIT,
            bare=range(2),
        )
        own = gathered[:, :size]
        near = [own] + [trade(own, "row", s) for s in range(1, rows_count)]
        grads = spread(
            row_here,
            here,
            [(s, 0, (near[s],)) for s in range(rows_count - 1)]
            + [(s, 1, (swap(near[s]),)) for s in range(rows_count - 1)],
        )
        far, *_ = lax.optimization_barrier((near[-1], grads[0], grad_up))
        grads = spread(
            row_here,
            here,
            [(rows_count - 1, 0, (near[-1],)), (rows_count - 1, 1, (swap(far),))],
            grads,
        )
    else:
        axes = ("row", "seq")
        back_parts = lax.all_to_all(back, "pat", 0, 0, tiled=True)
        wide_sum = lax.psum(wide[0], axes)
        grad_down, grad_up = wide_sum[0].astype(f32), wide_sum[1].astype(f32)
        grad_out = lax.psum(wide_sum[2], "pat").astype(f32)
        gathered = lax.all_gather(lax.psum(narrow[0], axes), "pat")
        small = gathered[:, :48, 3 * width :].reshape(parts, 4, D)
        small = jnp.pad(small, ((0, 0), (0, 12), (0, 0)))
        grads = [
            gathered[:, :, at * width : (at + 1) * width]
            .astype(f32)
            .transpose(1, 0, 2)
            .reshape(D, D)
            for at in range(3)
        ] + [grad_out]
    grad_in, vectors = staged_call(
        finish_kernel,
        [],
        [back_parts, gathered if pair else small],
        (shape(quarter, D), shape(4, D, kind=f32)),
        scratch=[pltpu.VMEM((parts, 16, D), bf16)],
        limit=SMALL_LIMIT,
        late=1,
    )
    return (
        out_t.T[None],
        grad_in[None],
        vectors[0],
        vectors[1],
        grads[0],
        grads[1],
        grads[2],
        grads[3],
        vectors[2],
        vectors[3],
        grad_up,
        grad_down,
    )


def solution(mesh):
    placed = (
        P("row", "seq", None),
        P("row", None),
        P(),
        P(),
        P(),
        P(),
        P(),
        P(),
        P(),
        P(),
        P(None, "pat"),
        P("pat", None),
        P("row", "seq", "pat"),
    )
    return jax.shard_map(
        per_device,
        mesh=mesh,
        in_specs=placed,
        out_specs=(
            P("row", "seq", "pat"),
            P("row", ("seq", "pat"), None),
            P(),
            P(),
            P(),
            P(),
            P(),
            P(),
            P(),
            P(),
            P(None, "pat"),
            P("pat", None),
        ),
        check_vma=False,
    )
```

```python
import functools

import jax
import jax.numpy as jnp
from jax import lax
from jax.experimental import pallas as pl
from jax.experimental.pallas import tpu as pltpu
from jax.sharding import PartitionSpec as P

D = 768
HEADS = 12
HDIM = 64

epsilon = 1e-05
masked_low = -1e30
segment_parts = (1, 2, 4, 8, 16)
dilations = (1, 2, 4, 6, 12)
DOCS = 3
FEATS = 128
TILE = 256
VMEM_LIMIT = 60 * 1024 * 1024
SMALL_LIMIT = 20 * 1024 * 1024
COPIES = 64
f32 = jnp.float32
bf16 = jnp.bfloat16


def dot(a, b):
    return lax.dot_general(a, b, (((1,), (0,)), ((), ())), preferred_element_type=f32)


def dot_nt(a, b):
    return lax.dot_general(a, b, (((1,), (1,)), ((), ())), preferred_element_type=f32)


def dot_tn(a, b):
    return lax.dot_general(a, b, (((0,), (0,)), ((), ())), preferred_element_type=f32)


class Staged:
    def __init__(self, outside, inside, sems, free):
        self.outside, self.inside, self.sems, self.free = outside, inside, sems, free
        self.pending = []

    def start(self, source=None, target=None):
        copy = pltpu.make_async_copy(
            self.outside if source is None else source,
            self.inside if target is None else target,
            self.sems.at[next(self.free)],
        )
        copy.start()
        self.pending.append(copy)

    def get(self):
        for copy in self.pending:
            copy.wait()
        self.pending = []
        return self.inside

    def put(self, source, target):
        copy = pltpu.make_async_copy(source, target, self.sems.at[next(self.free)])
        copy.start()
        self.pending.append(copy)

    def send(self, at=...):
        copy = pltpu.make_async_copy(
            self.inside.at[at], self.outside.at[at], self.sems.at[next(self.free)]
        )
        copy.start()
        self.pending.append(copy)


def staged_call(body, scalars, arrays, outs, scratch=(), windows=None, limit=VMEM_LIMIT, late=0, aliases=(), bare=(), flops=0):
    windows = windows or {}
    n_scalar, n_in, n_out = len(scalars), len(arrays), len(outs)

    def kernel(*refs):
        scalar_refs, refs = refs[:n_scalar], refs[n_scalar:]
        outside, refs = refs[: n_in + n_out], refs[n_in + n_out :]
        inside, refs = refs[: n_in + n_out], refs[n_in + n_out :]
        sems, rest = refs[0], refs[1:]
        free = iter(range(COPIES))
        every = [Staged(o, i, sems, free) for o, i in zip(outside, inside, strict=True)]
        ins, results = every[:n_in], every[n_in:]
        for at, one in enumerate(ins[: n_in - late]):
            if at in windows:
                start = windows[at](scalar_refs)
                size = one.inside.shape[-1]
                one.start(one.outside.at[:, pl.ds(pl.multiple_of(start, 128), size)])
            else:
                one.start()
        body(scalar_refs, ins, results, rest)
        for one in ins + results:
            one.get()

    def buffer(at, array):
        dims = array.shape
        if at >= n_in - late:
            return pltpu.VMEM((16, 128), array.dtype)
        if at in windows:
            dims = (*dims[:-1], 256)
        return pltpu.VMEM(dims, array.dtype)

    return pl.pallas_call(
        kernel,
        out_shape=tuple(outs),
        in_specs=[pl.BlockSpec(memory_space=pltpu.SMEM)] * n_scalar
        + [pl.BlockSpec(memory_space=pl.ANY)] * n_in,
        out_specs=(pl.BlockSpec(memory_space=pltpu.HBM),) * n_out,
        scratch_shapes=[buffer(at, a) for at, a in enumerate(arrays)]
        + [
            pltpu.VMEM((16, 128) if at in bare else o.shape, o.dtype)
            for at, o in enumerate(outs)
        ]
        + [pltpu.SemaphoreType.DMA((COPIES,))]
        + list(scratch),
        input_output_aliases={n_scalar + a: o for a, o in aliases},
        compiler_params=pltpu.CompilerParams(vmem_limit_bytes=limit),
        cost_estimate=pl.CostEstimate(flops=flops, bytes_accessed=0, transcendentals=0),
    )(*scalars, *arrays)


def normalise(values):
    center = values - jnp.mean(values, axis=-1, keepdims=True)
    scale = lax.rsqrt(jnp.mean(center * center, axis=-1, keepdims=True) + epsilon)
    return center * scale, scale


def norm_backward(hat, scale, grad):
    return scale * (
        grad
        - jnp.mean(grad, axis=-1, keepdims=True)
        - hat * jnp.mean(grad * hat, axis=-1, keepdims=True)
    )


def make_features(heads, part, docs, feats):
    _, length, _ = feats.inside.shape
    position = lax.broadcasted_iota(jnp.int32, (1, length), 1)
    feature = lax.broadcasted_iota(jnp.int32, (FEATS, length), 0)
    for h in range(heads):
        head = part * heads + h
        hit = None
        base = 0
        for size, dilation in zip(segment_parts, dilations, strict=True):
            seg_width = length * size // 16
            inside = lax.rem(
                lax.rem(position, seg_width) + dilation - lax.rem(head, dilation), dilation
            )
            key = base + lax.div(position, seg_width) * DOCS + docs
            key = jnp.where(inside == 0, key, -1)
            found = feature == key
            hit = found if hit is None else hit | found
            base += DOCS * (16 // size)
        feats.inside[h] = jnp.where(hit, 1.0, 0.0).T.astype(bf16)
        feats.send(h)


def project_kernel(parts, pair, scalars, ins, outs, scratch):
    x, docs, gain, bias, *weights = ins[:7]
    normed, q, kv, own, feats = outs[:5]
    width = D // parts
    where = scalars[0]
    own.inside[:, 3 * width :] = jnp.zeros((D, D - 3 * width), bf16)
    gain = gain.get()[...].reshape(1, D)
    bias = bias.get()[...].reshape(1, D)
    x.get()
    span = x.inside.shape[0]
    for start in range(0, span, TILE):
        rows = slice(start, start + TILE)
        hat, _ = normalise(x.inside[rows, :].astype(f32))
        normed.inside[rows, :] = (hat * gain + bias).astype(bf16)
    normed.send()
    for w in weights:
        w.get()
    for odd in range(2):

        @pl.when(where[0] % 2 == odd)
        def _():
            for at, w in enumerate(weights):
                own.inside[:, at * width : (at + 1) * width] = w.inside[
                    :, odd * 64 : odd * 64 + width
                ]

    own.send()
    for start in range(0, span, TILE):
        rows = slice(start, start + TILE)
        made = dot(normed.inside[rows, :], own.inside[:, : 3 * width]).astype(bf16)
        q.inside[rows, :] = (made[:, :width].astype(f32) * HDIM**-0.5).astype(bf16)
        kv.inside[rows, :] = made[:, width:]
    kv.send()
    q.send()
    if pair:
        x_far = ins[7].get()

        @pl.when(scalars[1][0] > 0)
        def _():
            for start in range(0, span, TILE):
                rows = slice(start, start + TILE)
                hat, _ = normalise(x_far[rows, :].astype(f32))
                low = (hat * gain + bias).astype(bf16)
                outs[5].inside[rows, :] = dot(low, own.inside[:, width : 3 * width]).astype(bf16)

        outs[5].send()
    make_features(feats.inside.shape[0], where[0], docs.get()[...], feats)


def head_mask(heads, width):
    lane = lax.broadcasted_iota(jnp.int32, (1, width), 1)
    return [((lane >= h * HDIM) & (lane < (h + 1) * HDIM)).astype(bf16) for h in range(heads)]


def attention_kernel(heads, span, scalars, ins, outs, scratch):
    where = scalars[0]
    q, kv, feats, kv_far = (one.get() for one in ins)
    mixed_low, mixed_t, lse = (one.inside for one in outs)
    q_head, k, v_t, kf, vf_t, tops, totals = scratch
    width = heads * HDIM
    masks = head_mask(heads, width)
    for h in range(heads):
        q_head[h] = q[...] * masks[h]
    k[...] = kv[:, :width]
    v_t[...] = kv[:, width:].T
    far = kv_far.shape[0] // span

    def turn(j, _):
        rows = pl.ds(pl.multiple_of(j * span, span), span)
        kf[rows, :] = kv_far[rows, :width]
        vf_t[j] = kv_far[rows, width:].T
        return 0

    mine = where[0]
    lax.fori_loop(0, jnp.minimum(mine, far), turn, 0)
    own_start = pl.multiple_of(mine * span, span)
    lse[...] = jnp.zeros(lse.shape, f32)
    pairs = [(start, h) for start in range(0, span, TILE) for h in range(heads)]

    def part(start, h, k_rows, f_rows, v_rows, causal):
        counts = dot_nt(f_rows, feats[h, pl.ds(own_start + start, TILE), :])
        if causal:
            at_k = lax.broadcasted_iota(jnp.int32, counts.shape, 0)
            at_q = lax.broadcasted_iota(jnp.int32, counts.shape, 1) + start
            counts = jnp.where(at_k <= at_q, counts, 0.0)
        scores = dot_nt(k_rows, q_head[h, start : start + TILE, :])
        scores = jnp.where(counts > 0, scores, masked_low)
        return counts, scores, v_rows

    for at, (start, h) in enumerate(pairs):
        size = start + TILE
        head_rows = slice(h * HDIM, (h + 1) * HDIM)
        counts, scores, v_rows = part(
            start,
            h,
            k[:size, :],
            feats[h, pl.ds(own_start, size), :],
            v_t[head_rows, :size],
            True,
        )
        top = jnp.max(scores, axis=0, keepdims=True)
        weights = counts * jnp.exp(scores - top)
        tops[at : at + 1, :] = top
        totals[at : at + 1, :] = jnp.sum(weights, axis=0, keepdims=True)
        mixed_t[head_rows, start : start + TILE] = dot(v_rows, weights.astype(bf16))

    def far_step(j, _):
        rows = pl.ds(pl.multiple_of(j * span, span), span)
        for at, (start, h) in enumerate(pairs):
            head_rows = slice(h * HDIM, (h + 1) * HDIM)
            counts, scores, v_rows = part(
                start, h, kf[rows, :], feats[h, rows, :], vf_t[j, head_rows, :], False
            )
            top = tops[at : at + 1, :]
            new_top = jnp.maximum(top, jnp.max(scores, axis=0, keepdims=True))
            weights = counts * jnp.exp(scores - new_top)
            factor = jnp.exp(top - new_top)
            tops[at : at + 1, :] = new_top
            totals[at : at + 1, :] = totals[at : at + 1, :] * factor + jnp.sum(
                weights, axis=0, keepdims=True
            )
            mixed_t[head_rows, start : start + TILE] = mixed_t[
                head_rows, start : start + TILE
            ] * factor + dot(v_rows, weights.astype(bf16))
        return 0

    lax.fori_loop(0, mine, far_step, 0)
    for at, (start, h) in enumerate(pairs):
        head_rows = slice(h * HDIM, (h + 1) * HDIM)
        total = totals[at : at + 1, :]
        done = mixed_t[head_rows, start : start + TILE] / total
        mixed_t[head_rows, start : start + TILE] = done
        mixed_low[head_rows, start : start + TILE] = done.astype(bf16)
        lse[h : h + 1, start : start + TILE] = tops[at : at + 1, :] + jnp.log(total)
    for one in outs:
        one.send()


def count_rows(f_rows, f_tile, low_from):
    counts = dot_nt(f_rows, f_tile)
    if low_from is not None:
        at_k = lax.broadcasted_iota(jnp.int32, counts.shape, 0)
        at_q = lax.broadcasted_iota(jnp.int32, counts.shape, 1) + low_from
        counts = jnp.where(at_k <= at_q, counts, 0.0)
    return counts


def attention_back_kernel(heads, span, scalars, ins, outs, scratch):
    where = scalars[0]
    parts, q, mixed_t, lse, kv, feats, kv_far = (one.get() for one in ins)
    grad_q, grad_kv, grad_far = (one.inside for one in outs)
    q_head, g_head, dots, probs, slopes, k, v, k_t, gq_t = scratch
    width = heads * HDIM
    masks = head_mask(heads, width)
    mine = where[0]
    far = kv_far.shape[0] // span
    total = parts[0].astype(f32)
    for part in range(1, parts.shape[0]):
        total = total + parts[part].astype(f32)
    low_t = total.astype(bf16)
    low = low_t.T
    for h in range(heads):
        q_head[h] = q[...] * masks[h]
        g_head[h] = low * masks[h]
    product = low_t.astype(f32) * mixed_t[...]
    for h in range(heads):
        dots[h : h + 1, :] = jnp.sum(product[h * HDIM : (h + 1) * HDIM], axis=0, keepdims=True)
    own_start = pl.multiple_of(mine * span, span)

    def block(h, start, size, rows, diagonal):
        tile = slice(start, start + TILE)
        columns = slice(h * span + start, h * span + start + TILE)
        f_rows = feats[h, pl.ds(own_start, size) if diagonal else rows, :]
        f_tile = feats[h, pl.ds(own_start + start, TILE), :]
        counts = count_rows(f_rows, f_tile, start if diagonal else None)
        scores = jnp.where(counts > 0, dot_nt(k[:size, :], q_head[h, tile, :]), masked_low)
        prob = counts * jnp.exp(scores - lse[h : h + 1, tile])
        grad_prob = dot_nt(v[:size, :], g_head[h, tile, :])
        slope = prob * (grad_prob - dots[h : h + 1, tile])
        probs[:size, columns] = prob.astype(bf16)
        slopes[:size, columns] = slope.astype(bf16)
        if size < span:
            probs[size:, columns] = jnp.zeros((span - size, TILE), bf16)
            slopes[size:, columns] = jnp.zeros((span - size, TILE), bf16)

    def finish():
        k_t[...] = k[...].T
        grad_v_rows = dot(probs[...], g_head[...].reshape(heads * span, width))
        grad_k_rows = dot(slopes[...], q_head[...].reshape(heads * span, width))
        terms = [
            dot(k_t[h * HDIM : (h + 1) * HDIM, :], slopes[:, h * span : (h + 1) * span])
            for h in range(heads)
        ]
        return grad_k_rows, grad_v_rows, terms

    k[...] = kv[:, :width]
    v[...] = kv[:, width:]
    for start in range(0, span, TILE):
        for h in range(heads):
            size = start + TILE
            block(h, start, size, None, True)
    grad_k_rows, grad_v_rows, terms = finish()
    grad_kv[:, :width] = grad_k_rows
    grad_kv[:, width:] = grad_v_rows
    outs[1].send()
    for h in range(heads):
        gq_t[h * HDIM : (h + 1) * HDIM, :] = terms[h]

    def far_block(j, _):
        rows = pl.ds(pl.multiple_of(j * span, span), span)
        k[...] = kv_far[rows, :width]
        v[...] = kv_far[rows, width:]
        for start in range(0, span, TILE):
            for h in range(heads):
                block(h, start, span, rows, False)
        grad_k_rows, grad_v_rows, terms = finish()
        grad_far[rows, :width] = grad_k_rows.astype(bf16)
        grad_far[rows, width:] = grad_v_rows.astype(bf16)
        for h in range(heads):
            gq_t[h * HDIM : (h + 1) * HDIM, :] += terms[h]
        return 0

    used = jnp.minimum(mine, far)
    lax.fori_loop(0, used, far_block, 0)

    def clear(j, _):
        grad_far[pl.ds(pl.multiple_of(j * span, span), span), :] = jnp.zeros((span, 2 * width), bf16)
        return 0

    lax.fori_loop(used, far, clear, 0)
    outs[2].send()
    grad_q[...] = (gq_t[...] * HDIM**-0.5).T.astype(bf16)
    outs[0].send()


def middle_kernel(scalars, ins, outs, scratch):
    mixed4, x, w_out, gain, bias, w_up, w_down, *c_parts = ins
    gm, sums, act, gh, branch, low, c, resids = outs
    (c4,) = scratch
    parts, width, span = mixed4.inside.shape
    for step, one in enumerate(c_parts):
        one.start(target=c4.at[scalars[0][0] ^ step])
    mixed_t = mixed4.get()[...].reshape(D, span)
    x.get(), w_out.get()
    gain = gain.get()[...].reshape(1, D)
    bias = bias.get()[...].reshape(1, D)
    gain_sum = jnp.zeros((1, D), f32)
    bias_sum = jnp.zeros((1, D), f32)
    for start in range(0, span, span):
        rows = slice(start, start + span)
        resid = x.inside[rows, :].astype(f32) + dot_tn(mixed_t[:, rows], w_out.inside[...])
        resids.inside[rows, :] = resid.astype(bf16)
        hat, scale = normalise(resid)
        normed = (hat * gain + bias).astype(bf16)
        low.inside[rows, :] = normed
        w_up.get()
        hidden = dot(normed, w_up.inside[...])
        bell = 0.5 + 0.5 * lax.erf(hidden * (0.5**0.5))
        act.inside[rows, :] = (hidden * bell).astype(bf16)
        slope = bell + hidden * jnp.exp(-0.5 * hidden * hidden) * 0.3989422804014327
        if start == 0:
            w_down.get()
            for one in c_parts:
                one.get()
            for part in range(parts):
                c.inside[:, part * width : (part + 1) * width] = c4[part].T
            c.send()
        c_rows = c.inside[rows, :]
        grad_hidden = (slope * dot_nt(c_rows, w_down.inside[...])).astype(bf16)
        gh.inside[rows, :] = grad_hidden
        grad_normed = dot_nt(grad_hidden, w_up.inside[...])
        gain_sum = gain_sum + jnp.sum(grad_normed * hat, axis=0, keepdims=True)
        bias_sum = bias_sum + jnp.sum(grad_normed, axis=0, keepdims=True)
        grad_resid = norm_backward(hat, scale, grad_normed * gain) + c_rows.astype(f32) * (
            1.0 / parts
        )
        grad_low = grad_resid.astype(bf16)
        branch.inside[rows, :] = grad_low
        for one in (act, low, gh, resids, branch):
            one.send(pl.ds(start, span))
        for part in range(parts):
            gm.inside[part, :, rows] = dot_nt(
                w_out.inside[part * width : (part + 1) * width, :], grad_low
            ).astype(bf16)
    sums.inside[0:1, :] = gain_sum
    sums.inside[1:2, :] = bias_sum
    gm.send()
    sums.send()


def weights_kernel(pair, scalars, ins, outs, scratch):
    act, c, low, gh, mixed4, branch, w_down, resids = ins
    ffn, *wide = outs
    (made,) = scratch
    parts, width, span = mixed4.inside.shape
    chunk = span // parts
    where = scalars[0]

    def out_product():
        mixed_t = mixed4.get()[...].reshape(D, span)
        return dot(mixed_t, branch.get()[...])

    products = (
        lambda: dot_tn(act.get()[...], c.get()[...]),
        lambda: dot_tn(low.get()[...], gh.get()[...]),
        out_product,
    )
    for at, product in enumerate(products):
        if not pair:
            wide[0].inside[at] = product().astype(bf16)
            continue
        made[...] = product().astype(bf16)
        rows_count = wide[0].inside.shape[1]
        size = D // (2 * rows_count)
        for row in range(rows_count):
            for out, half in ((wide[0].inside.at[at], where[0]), (wide[1 + at].inside, 1 - where[0])):
                start = pl.multiple_of((2 * row + half) * size, size)
                out[row] = made[pl.ds(start, size), :]
        wide[1 + at].send()
        wide[0].send(at)
    if not pair:
        wide[0].send()
    w_down.get(), resids.get()
    for start in range(0, span, TILE):
        rows = slice(start, start + TILE)
        out = dot(act.inside[rows, :], w_down.inside[...]) + resids.inside[rows, :].astype(f32) * (
            1.0 / parts
        )
        out_t = out.astype(bf16).T
        for part in range(parts):
            for at in range(start, start + TILE, chunk):
                ffn.inside[part, at // chunk * width : (at // chunk + 1) * width, :] = out_t[
                    part * width : (part + 1) * width, at - start : at - start + chunk
                ]
    ffn.send()


def add_kernel(scalars, ins, outs, scratch):
    keep, *more = ins
    keep.get()
    for group, one in enumerate(more):
        one.get()
        for at, out in enumerate(outs):
            block = scalars[0][0] ^ at
            out.inside[group] = (
                keep.inside[group, block].astype(f32) + one.inside[block].astype(f32)
            ).astype(bf16)
    for out in outs[1:] + outs[:1]:
        out.send()


def row_sum_kernel(parts, scalars, ins, outs, scratch):
    ffn_own, *out_parts = outs
    (rows,) = scratch
    total = ins[0].get()[...].astype(f32)
    for one in ins[1:]:
        total = total + one.get()[...].astype(f32)
    total = total.astype(bf16)
    size = total.shape[1]
    half = size // 2
    width = D // parts
    for own in range(parts):

        @pl.when(scalars[0][0] == own)
        def _():
            for step, out in enumerate(out_parts):
                part = own ^ step
                columns = slice(part * width, (part + 1) * width)
                out.inside[:, :width] = total[2, :half, columns]
                out.inside[:, width:] = total[2, half:, columns]

    for one in out_parts[::-1]:
        one.send()
    rows[...] = total[:2].reshape(2 * size, D)
    for row in range(ffn_own.outside.shape[0]):
        ffn_own.put(rows, ffn_own.outside.at[row])


SLOT = 64


def last_kernel(parts, pair, scalars, ins, outs, scratch):
    gq, normed, gkv, own, x, gain, gr, sums, gkv_more = ins
    back, *narrow = outs
    grads, small, made = scratch
    width = D // parts
    span = x.inside.shape[0]
    piece = span // parts
    lanes = 3 * width + SLOT
    grads[:, :width] = gq.get()[...]
    grads[:, 3 * width :] = jnp.zeros((span, D - 3 * width), bf16)
    gkv.get(), gkv_more.get()
    grads[:, width : 3 * width] = (
        gkv.inside[...] + gkv_more.inside[...].astype(f32)
    ).astype(bf16)
    own.get(), x.get(), gr.get(), sums.get()
    gain = gain.get()[...].reshape(1, D)
    gain_sum = jnp.zeros((1, D), f32)
    bias_sum = jnp.zeros((1, D), f32)
    for start in range(0, span, TILE):
        rows = slice(start, start + TILE)
        hat, scale = normalise(x.inside[rows, :].astype(f32))
        grad_normed = dot_nt(grads[rows, :], own.inside[...])
        gain_sum = gain_sum + jnp.sum(grad_normed * hat, axis=0, keepdims=True)
        bias_sum = bias_sum + jnp.sum(grad_normed, axis=0, keepdims=True)
        grad_in = gr.inside[rows, :].astype(f32) + norm_backward(hat, scale, grad_normed * gain)
        turned = grad_in.astype(bf16).T
        for at in range(start, start + TILE, piece):
            back.inside[at // piece] = turned[:, at - start : at - start + piece]
    pieces = D // SLOT
    for at, row in enumerate(
        (gain_sum, bias_sum, sums.inside[0:1, :], sums.inside[1:2, :])
    ):
        for part in range(pieces):
            small[at * pieces + part : at * pieces + part + 1, :] = row[
                :, part * SLOT : (part + 1) * SLOT
            ]
    made[...] = dot_tn(normed.get()[...], grads[:, :lanes]).astype(bf16)
    tail = small[...].astype(bf16)
    if pair:
        rows_count, size, _ = narrow[1].inside.shape
        for row in range(rows_count):
            for out, half in (
                (narrow[0].inside.at[0], scalars[0][0]),
                (narrow[1].inside, 1 - scalars[0][0]),
            ):
                start = pl.multiple_of((2 * row + half) * size, size)
                out[row] = made[pl.ds(start, size), :]
                out[row, :48, 3 * width :] = tail
        narrow[1].send()
        narrow[0].send()
    else:
        narrow[0].inside[...] = made[...]
        narrow[0].inside[:48, 3 * width :] = tail
        narrow[0].send()
    back.send()


def own_sum_kernel(parts, count, scalars, ins, outs, scratch):
    mine = outs[0].inside
    (small,) = scratch
    width = D // parts
    size = ins[0].inside.shape[1]
    half = size // 2
    out = ins[count].get()[...].astype(f32)
    for one in ins[count + 1 :]:
        out = out + one.get()[...].astype(f32)
    mine[:half, 3 * width :] = out[:, :width].astype(bf16)
    mine[half:size, 3 * width :] = out[:, width:].astype(bf16)
    total = ins[0].get()[0].astype(f32)
    for one in ins[1:count]:
        total = total + one.get()[0].astype(f32)
    mine[:size, : 3 * width] = total[:, : 3 * width].astype(bf16)
    pieces = D // SLOT
    small[...] = jnp.zeros(small.shape, f32)
    for at in range(4):
        for part in range(pieces):
            row = at * pieces + part
            small[at : at + 1, part * SLOT : (part + 1) * SLOT] = total[
                row : row + 1, 3 * width :
            ]
    mine[size:, :] = small[...].astype(bf16)
    outs[0].send()


def output_kernel(scalars, ins, outs, scratch):
    got = ins[0].get()
    parts, _, piece = got.shape
    width = D // parts
    total = got[0, :D].astype(f32)
    for part in range(1, parts):
        total = total + got[part, :D].astype(f32)
    for at in range(parts):
        outs[0].inside[:, at * piece : (at + 1) * piece] = total[
            at * width : (at + 1) * width
        ].astype(bf16)
    outs[0].send()


def finish_kernel(scalars, ins, outs, scratch):
    grad_in, *vectors = outs
    (small,) = scratch
    size = ins[1].outside.shape[1] - 16
    ins[1].start(source=ins[1].outside.at[:, pl.ds(size, 16), :], target=small)
    back = ins[0].get()
    total = back[0].astype(f32)
    for at in range(1, back.shape[0]):
        total = total + back[at].astype(f32)
    grad_in.inside[...] = total.T.astype(bf16)
    grad_in.send()
    ins[1].get()
    sums = small[0].astype(f32)
    for at in range(1, small.shape[0]):
        sums = sums + small[at].astype(f32)
    for at, vector in enumerate(vectors):
        vector.inside[...] = sums[at]
        vector.send()


def spread_kernel(steps, scalars, ins, outs, scratch):
    (buffer,) = scratch
    row, seq = scalars
    size = buffer.shape[2]
    at = 0
    for step, (row_step, seq_step, count) in enumerate(steps):
        part = 0
        for one in ins[at : at + count]:
            got = one.get()
            for own in range(got.shape[0]):
                width = D // (got.shape[0] * count)
                columns = slice(part * width, (part + 1) * width)
                for grad in range(4):
                    buffer[grad, step, :, columns] = got[
                        own, :, grad * width : (grad + 1) * width
                    ].astype(f32)
                part += 1
        at += count
        start = pl.multiple_of((2 * (row[0] ^ row_step) + (seq[0] ^ seq_step)) * size, size)
        for grad in range(4):
            out = outs[grad]
            out.put(buffer.at[grad, step], out.outside.at[pl.ds(start, size), :])


def spread(row_here, here, steps, earlier=(), flops=0):
    count = sum(len(blocks) for _, _, blocks in steps)
    size = steps[0][2][0].shape[1]
    received = [block for _, _, blocks in steps for block in blocks]
    return staged_call(
        functools.partial(spread_kernel, [(a, b, len(c)) for a, b, c in steps]),
        [row_here, here],
        [*received, *earlier],
        (shape(D, D, kind=f32),) * 4,
        scratch=[pltpu.VMEM((4, len(steps), size, D), f32)],
        limit=SMALL_LIMIT,
        late=len(earlier),
        aliases=tuple((count + at, at) for at in range(len(earlier))),
        bare=range(4),
        flops=flops,
    )


def spread_ffn_kernel(scalars, ins, outs, scratch):
    (buffer,) = scratch
    size = buffer.shape[2]
    for half, one in enumerate(ins):
        got = one.get()
        for row in range(got.shape[0]):
            start = pl.multiple_of((2 * row + (scalars[0][0] ^ half)) * size, size)
            for grad, out in enumerate(outs):
                place = buffer.at[grad, half * got.shape[0] + row]
                place[...] = got[row, grad * size : (grad + 1) * size, :].astype(f32)
                out.put(place, out.outside.at[pl.ds(start, size), :])


def broadcast_exchange(value, axis):
    count = lax.axis_size(axis)
    return lax.all_to_all(
        jnp.broadcast_to(value[None], (count,) + value.shape), axis, 0, 0, tiled=False
    )


def swap(value):
    return lax.ppermute(value, "seq", [(0, 1), (1, 0)])


def trade(value, axis, step):
    return lax.ppermute(value, axis, [(a, a ^ step) for a in range(lax.axis_size(axis))])


def shape(*dims, kind=bf16):
    return jax.ShapeDtypeStruct(dims, kind)


def per_device(
    block_input,
    doc_ids,
    ln1_gain,
    ln1_bias,
    w_query,
    w_key,
    w_value,
    w_out,
    ln2_gain,
    ln2_bias,
    w_up,
    w_down,
    cotangent,
):
    span = block_input.shape[1]
    rows_count = lax.axis_size("row")
    seq_count = lax.axis_size("seq")
    parts = lax.axis_size("pat")
    row_index = lax.axis_index("row")
    seq_index = lax.axis_index("seq")
    pat_index = lax.axis_index("pat")
    pair = seq_count == 2
    heads = HEADS // parts
    width = D // parts
    quarter = span // parts
    size = D // (rows_count * seq_count) if pair else D
    here = seq_index.astype(jnp.int32)[None]
    row_here = row_index.astype(jnp.int32)[None]
    part_here = pat_index.astype(jnp.int32)[None]
    x = block_input[0]

    c_own = cotangent[0].T
    c_parts = [c_own] + [trade(c_own, "pat", s) for s in range(1, parts)]
    def window(scalars):
        return scalars[0][0] * width // 128 * 128

    far_shapes = (shape(span, 2 * width),) if pair else ()
    normed, q, kv, own, feats, *far = staged_call(
        functools.partial(project_kernel, parts, pair),
        [part_here, here],
        [x, doc_ids, ln1_gain, ln1_bias, w_query, w_key, w_value] + ([swap(x)] if pair else []),
        (
            shape(span, D),
            shape(span, width),
            shape(span, 2 * width),
            shape(D, D),
            shape(heads, doc_ids.shape[1], FEATS),
            *far_shapes,
        ),
        windows={4: window, 5: window, 6: window},
        flops=1 << 42,
    )

    kv_far = far[0] if pair else lax.all_gather(kv, "seq", axis=0, tiled=True)
    far_rows = kv_far.shape[0]

    mixed, mixed_t, lse = staged_call(
        functools.partial(attention_kernel, heads, span),
        [here],
        [q, kv, feats, kv_far],
        (shape(width, span), shape(width, span, kind=f32), shape(8, span, kind=f32)),
        scratch=[
            pltpu.VMEM((heads, span, width), bf16),
            pltpu.VMEM((span, width), bf16),
            pltpu.VMEM((width, span), bf16),
            pltpu.VMEM((far_rows, width), bf16),
            pltpu.VMEM((far_rows // span, width, span), bf16),
            pltpu.VMEM((heads * span // TILE + 8, TILE), f32),
            pltpu.VMEM((heads * span // TILE + 8, TILE), f32),
        ],
    )
    mixed, *c_parts = lax.optimization_barrier((mixed, *c_parts))
    mixed4 = lax.all_gather(mixed, "pat")

    wide_shapes = (shape(3, D, D),)
    if pair:
        wide_shapes = (shape(3, rows_count, size, D),) + (shape(rows_count, size, D),) * 3
    gm, sums, act, gh, branch, low, c, resids = staged_call(
        middle_kernel,
        [part_here],
        [mixed4, x, w_out, ln2_gain, ln2_bias, w_up, w_down, *c_parts],
        (shape(parts, width, span), shape(8, D, kind=f32)) + (shape(span, D),) * 6,
        scratch=[pltpu.VMEM((parts, width, span), bf16)],
        late=parts,
    )
    gm_parts = lax.all_to_all(gm, "pat", 0, 0, tiled=True)
    ffn, *wide = staged_call(
        functools.partial(weights_kernel, pair),
        [here],
        [act, c, low, gh, mixed4, branch, w_down, resids],
        (shape(parts, parts * width, quarter), *wide_shapes),
        scratch=[pltpu.VMEM((D, D), bf16)],
        flops=1 << 42,
    )

    if pair:
        keep, *sends = wide
        ordered = staged_call(
            add_kernel,
            [row_here],
            [keep, *[swap(send) for send in sends]],
            (shape(3, size, D),) * rows_count,
            limit=SMALL_LIMIT,
        )
        wide_parts = [ordered[0]] + [trade(ordered[s], "row", s) for s in range(1, rows_count)]

    ffn, _ = lax.optimization_barrier((ffn, gm_parts))
    ffn_parts = lax.all_to_all(ffn, "pat", 0, 0, tiled=True)
    (out_t,) = staged_call(
        output_kernel,
        [],
        [ffn_parts],
        (shape(width, span),),
        limit=SMALL_LIMIT,
        flops=1 << 42,
    )
    gq, gkv, gkv_far = staged_call(
        functools.partial(attention_back_kernel, heads, span),
        [here],
        [gm_parts, q, mixed_t, lse, kv, feats, kv_far],
        (
            shape(span, width),
            shape(span, 2 * width, kind=f32),
            shape(far_rows, 2 * width),
        ),
        scratch=[
            pltpu.VMEM((heads, span, width), bf16),
            pltpu.VMEM((heads, span, width), bf16),
            pltpu.VMEM((8, span), f32),
            pltpu.VMEM((span, heads * span), bf16),
            pltpu.VMEM((span, heads * span), bf16),
            pltpu.VMEM((span, width), bf16),
            pltpu.VMEM((span, width), bf16),
            pltpu.VMEM((width, span), bf16),
            pltpu.VMEM((width, span), f32),
        ],
        flops=1 << 42,
    )

    if pair:
        gkv_more = swap(gkv_far)
        ffn_own, *out_parts = staged_call(
            functools.partial(row_sum_kernel, parts),
            [part_here],
            wide_parts,
            (shape(rows_count, 2 * size, D),) + (shape(size // 2, 2 * width),) * parts,
            scratch=[pltpu.VMEM((2 * size, D), bf16)],
            limit=SMALL_LIMIT,
            bare=(0,),
        )
        out_parts = [out_parts[0]] + [trade(out_parts[s], "pat", s) for s in range(1, parts)]
    else:
        gkv_more = lax.psum_scatter(gkv_far, "seq", scatter_dimension=0, tiled=True)

    lanes = 3 * width + SLOT
    narrow_shapes = (shape(1, rows_count, size, lanes), shape(rows_count, size, lanes)) if pair else (shape(D, lanes),)
    back, *narrow = staged_call(
        functools.partial(last_kernel, parts, pair),
        [here],
        [gq, normed, gkv, own, x, ln1_gain, branch, sums, gkv_more],
        (shape(parts, parts * width, quarter), *narrow_shapes),
        scratch=[
            pltpu.VMEM((span, D), bf16),
            pltpu.VMEM((48, SLOT), f32),
            pltpu.VMEM((D, lanes), bf16),
        ],
    )

    if pair:
        keep, send = narrow
        send, *_ = lax.optimization_barrier((send, *wide_parts[1:]))
        ordered = staged_call(
            add_kernel, [row_here], [keep, swap(send)], (shape(1, size, lanes),) * rows_count,
            limit=65000 << 10,
        )
        received = [ordered[0]] + [trade(ordered[s], "row", s) for s in range(1, rows_count)]
        received[3], _ = lax.optimization_barrier((received[3], out_t))
        (mine,) = staged_call(
            functools.partial(own_sum_kernel, parts, rows_count),
            [],
            [*received, *out_parts],
            (shape(size + 16, D),),
            scratch=[pltpu.VMEM((16, D), f32)],
            limit=SMALL_LIMIT,
        )
        gathered = lax.all_gather(mine, "pat")
        ffn_own, *_ = lax.optimization_barrier(
            (ffn_own, ffn_parts, *received[1:], *out_parts[1:])
        )
        ffn_mine = lax.all_to_all(ffn_own, "row", 0, 0, tiled=True)
        gathered, ffn_mine, back = lax.optimization_barrier((gathered, ffn_mine, back))
        back_parts = lax.all_to_all(back, "pat", 0, 0, tiled=True)
        grad_down, grad_up = staged_call(
            spread_ffn_kernel,
            [here],
            [ffn_mine, swap(ffn_mine)],
            (shape(D, D, kind=f32),) * 2,
            scratch=[pltpu.VMEM((2, 2 * rows_count, size, D), f32)],
            limit=SMALL_LIMIT,
            bare=range(2),
        )
        own = gathered[:, :size]
        near1, near2 = trade(own, "row", 1), trade(own, "row", 2)
        far = (trade(near1[: parts // 2], "row", 2), trade(near2[parts // 2 :], "row", 1))
        grads = spread(
            row_here,
            here,
            [(0, 0, (own,)), (1, 0, (near1,)), (2, 0, (near2,))]
            + [(0, 1, (swap(own),)), (1, 1, (swap(near1),)), (2, 1, (swap(near2),))],
        )
        sent = lax.optimization_barrier((*far, grads[0], grad_up))[:2]
        grads = spread(
            row_here,
            here,
            [(3, 0, far), (3, 1, tuple(swap(value) for value in sent))],
            grads,
        )
    else:
        axes = ("row", "seq")
        back_parts = lax.all_to_all(back, "pat", 0, 0, tiled=True)
        wide_sum = lax.psum(wide[0], axes)
        grad_down, grad_up = wide_sum[0].astype(f32), wide_sum[1].astype(f32)
        grad_out = lax.psum(wide_sum[2], "pat").astype(f32)
        gathered = lax.all_gather(lax.psum(narrow[0], axes), "pat")
        small = gathered[:, :48, 3 * width :].reshape(parts, 4, D)
        small = jnp.pad(small, ((0, 0), (0, 12), (0, 0)))
        grads = [
            gathered[:, :, at * width : (at + 1) * width]
            .astype(f32)
            .transpose(1, 0, 2)
            .reshape(D, D)
            for at in range(3)
        ] + [grad_out]
    grad_in, *vectors = staged_call(
        finish_kernel,
        [],
        [back_parts, gathered if pair else small],
        (shape(quarter, D),) + (shape(D, kind=f32),) * 4,
        scratch=[pltpu.VMEM((parts, 16, D), bf16)],
        limit=SMALL_LIMIT,
        late=1,
    )
    return (
        out_t.T[None],
        grad_in[None],
        vectors[0],
        vectors[1],
        grads[0],
        grads[1],
        grads[2],
        grads[3],
        vectors[2],
        vectors[3],
        grad_up,
        grad_down,
    )


def solution(mesh):
    placed = (
        P("row", "seq", None),
        P("row", None),
        P(),
        P(),
        P(),
        P(),
        P(),
        P(),
        P(),
        P(),
        P(None, "pat"),
        P("pat", None),
        P("row", "seq", "pat"),
    )
    return jax.shard_map(
        per_device,
        mesh=mesh,
        in_specs=placed,
        out_specs=(
            P("row", "seq", "pat"),
            P("row", ("seq", "pat"), None),
            P(),
            P(),
            P(),
            P(),
            P(),
            P(),
            P(),
            P(),
            P(None, "pat"),
            P("pat", None),
        ),
        check_vma=False,
    )
```

```python
import functools

import jax
import jax.numpy as jnp
from jax import lax
from jax.experimental import pallas as pl
from jax.experimental.pallas import tpu as pltpu
from jax.sharding import PartitionSpec as P

D = 768
HEADS = 12
HDIM = 64

epsilon = 1e-05
masked_low = -1e30
segment_parts = (1, 2, 4, 8, 16)
dilations = (1, 2, 4, 6, 12)
DOCS = 3
FEATS = 128
TILE = 256
VMEM_LIMIT = 60 * 1024 * 1024
SMALL_LIMIT = 20 * 1024 * 1024
COPIES = 64
f32 = jnp.float32
bf16 = jnp.bfloat16


def dot(a, b):
    return lax.dot_general(a, b, (((1,), (0,)), ((), ())), preferred_element_type=f32)


def dot_nt(a, b):
    return lax.dot_general(a, b, (((1,), (1,)), ((), ())), preferred_element_type=f32)


def dot_tn(a, b):
    return lax.dot_general(a, b, (((0,), (0,)), ((), ())), preferred_element_type=f32)


class Staged:
    def __init__(self, outside, inside, sems, free):
        self.outside, self.inside, self.sems, self.free = outside, inside, sems, free
        self.pending = []

    def start(self, source=None, target=None):
        copy = pltpu.make_async_copy(
            self.outside if source is None else source,
            self.inside if target is None else target,
            self.sems.at[next(self.free)],
        )
        copy.start()
        self.pending.append(copy)

    def get(self):
        for copy in self.pending:
            copy.wait()
        self.pending = []
        return self.inside

    def put(self, source, target):
        copy = pltpu.make_async_copy(source, target, self.sems.at[next(self.free)])
        copy.start()
        self.pending.append(copy)

    def send(self, at=...):
        copy = pltpu.make_async_copy(
            self.inside.at[at], self.outside.at[at], self.sems.at[next(self.free)]
        )
        copy.start()
        self.pending.append(copy)


def staged_call(body, scalars, arrays, outs, scratch=(), windows=None, limit=VMEM_LIMIT, late=0, aliases=(), bare=(), flops=0):
    windows = windows or {}
    n_scalar, n_in, n_out = len(scalars), len(arrays), len(outs)

    def kernel(*refs):
        scalar_refs, refs = refs[:n_scalar], refs[n_scalar:]
        outside, refs = refs[: n_in + n_out], refs[n_in + n_out :]
        inside, refs = refs[: n_in + n_out], refs[n_in + n_out :]
        sems, rest = refs[0], refs[1:]
        free = iter(range(COPIES))
        every = [Staged(o, i, sems, free) for o, i in zip(outside, inside, strict=True)]
        ins, results = every[:n_in], every[n_in:]
        for at, one in enumerate(ins[: n_in - late]):
            if at in windows:
                start = windows[at](scalar_refs)
                size = one.inside.shape[-1]
                one.start(one.outside.at[:, pl.ds(pl.multiple_of(start, 128), size)])
            else:
                one.start()
        body(scalar_refs, ins, results, rest)
        for one in ins + results:
            one.get()

    def buffer(at, array):
        dims = array.shape
        if at >= n_in - late:
            return pltpu.VMEM((16, 128), array.dtype)
        if at in windows:
            dims = (*dims[:-1], 256)
        return pltpu.VMEM(dims, array.dtype)

    return pl.pallas_call(
        kernel,
        out_shape=tuple(outs),
        in_specs=[pl.BlockSpec(memory_space=pltpu.SMEM)] * n_scalar
        + [pl.BlockSpec(memory_space=pl.ANY)] * n_in,
        out_specs=(pl.BlockSpec(memory_space=pltpu.HBM),) * n_out,
        scratch_shapes=[buffer(at, a) for at, a in enumerate(arrays)]
        + [
            pltpu.VMEM((16, 128) if at in bare else o.shape, o.dtype)
            for at, o in enumerate(outs)
        ]
        + [pltpu.SemaphoreType.DMA((COPIES,))]
        + list(scratch),
        input_output_aliases={n_scalar + a: o for a, o in aliases},
        compiler_params=pltpu.CompilerParams(vmem_limit_bytes=limit),
        cost_estimate=pl.CostEstimate(flops=flops, bytes_accessed=0, transcendentals=0),
    )(*scalars, *arrays)


def normalise(values):
    center = values - jnp.mean(values, axis=-1, keepdims=True)
    scale = lax.rsqrt(jnp.mean(center * center, axis=-1, keepdims=True) + epsilon)
    return center * scale, scale


def norm_backward(hat, scale, grad):
    return scale * (
        grad
        - jnp.mean(grad, axis=-1, keepdims=True)
        - hat * jnp.mean(grad * hat, axis=-1, keepdims=True)
    )


def make_features(heads, part, docs, feats):
    _, length, _ = feats.inside.shape
    position = lax.broadcasted_iota(jnp.int32, (1, length), 1)
    feature = lax.broadcasted_iota(jnp.int32, (FEATS, length), 0)
    for h in range(heads):
        head = part * heads + h
        hit = None
        base = 0
        for size, dilation in zip(segment_parts, dilations, strict=True):
            seg_width = length * size // 16
            inside = lax.rem(
                lax.rem(position, seg_width) + dilation - lax.rem(head, dilation), dilation
            )
            key = base + lax.div(position, seg_width) * DOCS + docs
            key = jnp.where(inside == 0, key, -1)
            found = feature == key
            hit = found if hit is None else hit | found
            base += DOCS * (16 // size)
        feats.inside[h] = jnp.where(hit, 1.0, 0.0).T.astype(bf16)
        feats.send(h)


def project_kernel(parts, pair, scalars, ins, outs, scratch):
    x, docs, gain, bias, *weights = ins[:7]
    normed, q, kv, own, feats = outs[:5]
    width = D // parts
    where = scalars[0]
    own.inside[:, 3 * width :] = jnp.zeros((D, D - 3 * width), bf16)
    gain = gain.get()[...].reshape(1, D)
    bias = bias.get()[...].reshape(1, D)
    x.get()
    span = x.inside.shape[0]
    for start in range(0, span, TILE):
        rows = slice(start, start + TILE)
        hat, _ = normalise(x.inside[rows, :].astype(f32))
        normed.inside[rows, :] = (hat * gain + bias).astype(bf16)
    normed.send()
    for w in weights:
        w.get()
    for odd in range(2):

        @pl.when(where[0] % 2 == odd)
        def _():
            for at, w in enumerate(weights):
                own.inside[:, at * width : (at + 1) * width] = w.inside[
                    :, odd * 64 : odd * 64 + width
                ]

    own.send()
    for start in range(0, span, TILE):
        rows = slice(start, start + TILE)
        made = dot(normed.inside[rows, :], own.inside[:, : 3 * width]).astype(bf16)
        q.inside[rows, :] = (made[:, :width].astype(f32) * HDIM**-0.5).astype(bf16)
        kv.inside[rows, :] = made[:, width:]
    kv.send()
    q.send()
    if pair:
        x_far = ins[7].get()

        @pl.when(scalars[1][0] > 0)
        def _():
            for start in range(0, span, TILE):
                rows = slice(start, start + TILE)
                hat, _ = normalise(x_far[rows, :].astype(f32))
                low = (hat * gain + bias).astype(bf16)
                outs[5].inside[rows, :] = dot(low, own.inside[:, width : 3 * width]).astype(bf16)

        outs[5].send()
    make_features(feats.inside.shape[0], where[0], docs.get()[...], feats)


def head_mask(heads, width):
    lane = lax.broadcasted_iota(jnp.int32, (1, width), 1)
    return [((lane >= h * HDIM) & (lane < (h + 1) * HDIM)).astype(bf16) for h in range(heads)]


def attention_kernel(heads, span, scalars, ins, outs, scratch):
    where = scalars[0]
    q, kv, feats, kv_far = (one.get() for one in ins)
    mixed_low, mixed_t, lse = (one.inside for one in outs)
    q_head, k, v_t, kf, vf_t, tops, totals = scratch
    width = heads * HDIM
    masks = head_mask(heads, width)
    for h in range(heads):
        q_head[h] = q[...] * masks[h]
    k[...] = kv[:, :width]
    v_t[...] = kv[:, width:].T
    far = kv_far.shape[0] // span

    def turn(j, _):
        rows = pl.ds(pl.multiple_of(j * span, span), span)
        kf[rows, :] = kv_far[rows, :width]
        vf_t[j] = kv_far[rows, width:].T
        return 0

    mine = where[0]
    lax.fori_loop(0, jnp.minimum(mine, far), turn, 0)
    own_start = pl.multiple_of(mine * span, span)
    lse[...] = jnp.zeros(lse.shape, f32)
    pairs = [(start, h) for start in range(0, span, TILE) for h in range(heads)]

    def part(start, h, k_rows, f_rows, v_rows, causal):
        counts = dot_nt(f_rows, feats[h, pl.ds(own_start + start, TILE), :])
        if causal:
            at_k = lax.broadcasted_iota(jnp.int32, counts.shape, 0)
            at_q = lax.broadcasted_iota(jnp.int32, counts.shape, 1) + start
            counts = jnp.where(at_k <= at_q, counts, 0.0)
        scores = dot_nt(k_rows, q_head[h, start : start + TILE, :])
        scores = jnp.where(counts > 0, scores, masked_low)
        return counts, scores, v_rows

    for at, (start, h) in enumerate(pairs):
        size = start + TILE
        head_rows = slice(h * HDIM, (h + 1) * HDIM)
        counts, scores, v_rows = part(
            start,
            h,
            k[:size, :],
            feats[h, pl.ds(own_start, size), :],
            v_t[head_rows, :size],
            True,
        )
        top = jnp.max(scores, axis=0, keepdims=True)
        weights = counts * jnp.exp(scores - top)
        tops[at : at + 1, :] = top
        totals[at : at + 1, :] = jnp.sum(weights, axis=0, keepdims=True)
        mixed_t[head_rows, start : start + TILE] = dot(v_rows, weights.astype(bf16))

    def far_step(j, _):
        rows = pl.ds(pl.multiple_of(j * span, span), span)
        for at, (start, h) in enumerate(pairs):
            head_rows = slice(h * HDIM, (h + 1) * HDIM)
            counts, scores, v_rows = part(
                start, h, kf[rows, :], feats[h, rows, :], vf_t[j, head_rows, :], False
            )
            top = tops[at : at + 1, :]
            new_top = jnp.maximum(top, jnp.max(scores, axis=0, keepdims=True))
            weights = counts * jnp.exp(scores - new_top)
            factor = jnp.exp(top - new_top)
            tops[at : at + 1, :] = new_top
            totals[at : at + 1, :] = totals[at : at + 1, :] * factor + jnp.sum(
                weights, axis=0, keepdims=True
            )
            mixed_t[head_rows, start : start + TILE] = mixed_t[
                head_rows, start : start + TILE
            ] * factor + dot(v_rows, weights.astype(bf16))
        return 0

    lax.fori_loop(0, mine, far_step, 0)
    for at, (start, h) in enumerate(pairs):
        head_rows = slice(h * HDIM, (h + 1) * HDIM)
        total = totals[at : at + 1, :]
        done = mixed_t[head_rows, start : start + TILE] / total
        mixed_t[head_rows, start : start + TILE] = done
        mixed_low[head_rows, start : start + TILE] = done.astype(bf16)
        lse[h : h + 1, start : start + TILE] = tops[at : at + 1, :] + jnp.log(total)
    for one in outs:
        one.send()


def count_rows(f_rows, f_tile, low_from):
    counts = dot_nt(f_rows, f_tile)
    if low_from is not None:
        at_k = lax.broadcasted_iota(jnp.int32, counts.shape, 0)
        at_q = lax.broadcasted_iota(jnp.int32, counts.shape, 1) + low_from
        counts = jnp.where(at_k <= at_q, counts, 0.0)
    return counts


def attention_back_kernel(heads, span, scalars, ins, outs, scratch):
    where = scalars[0]
    parts, q, mixed_t, lse, kv, feats, kv_far = (one.get() for one in ins)
    grad_q, grad_kv, grad_far = (one.inside for one in outs)
    q_head, g_head, dots, probs, slopes, k, v, k_t, gq_t = scratch
    width = heads * HDIM
    masks = head_mask(heads, width)
    mine = where[0]
    far = kv_far.shape[0] // span
    total = parts[0].astype(f32)
    for part in range(1, parts.shape[0]):
        total = total + parts[part].astype(f32)
    low_t = total.astype(bf16)
    low = low_t.T
    for h in range(heads):
        q_head[h] = q[...] * masks[h]
        g_head[h] = low * masks[h]
    product = low_t.astype(f32) * mixed_t[...]
    for h in range(heads):
        dots[h : h + 1, :] = jnp.sum(product[h * HDIM : (h + 1) * HDIM], axis=0, keepdims=True)
    own_start = pl.multiple_of(mine * span, span)

    def block(h, start, size, rows, diagonal):
        tile = slice(start, start + TILE)
        columns = slice(h * span + start, h * span + start + TILE)
        f_rows = feats[h, pl.ds(own_start, size) if diagonal else rows, :]
        f_tile = feats[h, pl.ds(own_start + start, TILE), :]
        counts = count_rows(f_rows, f_tile, start if diagonal else None)
        scores = jnp.where(counts > 0, dot_nt(k[:size, :], q_head[h, tile, :]), masked_low)
        prob = counts * jnp.exp(scores - lse[h : h + 1, tile])
        grad_prob = dot_nt(v[:size, :], g_head[h, tile, :])
        slope = prob * (grad_prob - dots[h : h + 1, tile])
        probs[:size, columns] = prob.astype(bf16)
        slopes[:size, columns] = slope.astype(bf16)
        if size < span:
            probs[size:, columns] = jnp.zeros((span - size, TILE), bf16)
            slopes[size:, columns] = jnp.zeros((span - size, TILE), bf16)

    def finish():
        k_t[...] = k[...].T
        grad_v_rows = dot(probs[...], g_head[...].reshape(heads * span, width))
        grad_k_rows = dot(slopes[...], q_head[...].reshape(heads * span, width))
        terms = [
            dot(k_t[h * HDIM : (h + 1) * HDIM, :], slopes[:, h * span : (h + 1) * span])
            for h in range(heads)
        ]
        return grad_k_rows, grad_v_rows, terms

    k[...] = kv[:, :width]
    v[...] = kv[:, width:]
    for start in range(0, span, TILE):
        for h in range(heads):
            size = start + TILE
            block(h, start, size, None, True)
    grad_k_rows, grad_v_rows, terms = finish()
    grad_kv[:, :width] = grad_k_rows
    grad_kv[:, width:] = grad_v_rows
    outs[1].send()
    for h in range(heads):
        gq_t[h * HDIM : (h + 1) * HDIM, :] = terms[h]

    def far_block(j, _):
        rows = pl.ds(pl.multiple_of(j * span, span), span)
        k[...] = kv_far[rows, :width]
        v[...] = kv_far[rows, width:]
        for start in range(0, span, TILE):
            for h in range(heads):
                block(h, start, span, rows, False)
        grad_k_rows, grad_v_rows, terms = finish()
        grad_far[rows, :width] = grad_k_rows.astype(bf16)
        grad_far[rows, width:] = grad_v_rows.astype(bf16)
        for h in range(heads):
            gq_t[h * HDIM : (h + 1) * HDIM, :] += terms[h]
        return 0

    used = jnp.minimum(mine, far)
    lax.fori_loop(0, used, far_block, 0)

    def clear(j, _):
        grad_far[pl.ds(pl.multiple_of(j * span, span), span), :] = jnp.zeros((span, 2 * width), bf16)
        return 0

    lax.fori_loop(used, far, clear, 0)
    outs[2].send()
    grad_q[...] = (gq_t[...] * HDIM**-0.5).T.astype(bf16)
    outs[0].send()


def middle_kernel(scalars, ins, outs, scratch):
    mixed4, x, w_out, gain, bias, w_up, w_down, *c_parts = ins
    gm, sums, act, gh, branch, low, c, resids = outs
    (c4,) = scratch
    parts, width, span = mixed4.inside.shape
    for step, one in enumerate(c_parts):
        one.start(target=c4.at[scalars[0][0] ^ step])
    mixed_t = mixed4.get()[...].reshape(D, span)
    x.get(), w_out.get()
    gain = gain.get()[...].reshape(1, D)
    bias = bias.get()[...].reshape(1, D)
    gain_sum = jnp.zeros((1, D), f32)
    bias_sum = jnp.zeros((1, D), f32)
    for start in range(0, span, span):
        rows = slice(start, start + span)
        resid = x.inside[rows, :].astype(f32) + dot_tn(mixed_t[:, rows], w_out.inside[...])
        resids.inside[rows, :] = resid.astype(bf16)
        hat, scale = normalise(resid)
        normed = (hat * gain + bias).astype(bf16)
        low.inside[rows, :] = normed
        w_up.get()
        hidden = dot(normed, w_up.inside[...])
        bell = 0.5 + 0.5 * lax.erf(hidden * (0.5**0.5))
        act.inside[rows, :] = (hidden * bell).astype(bf16)
        slope = bell + hidden * jnp.exp(-0.5 * hidden * hidden) * 0.3989422804014327
        if start == 0:
            w_down.get()
            for one in c_parts:
                one.get()
            for part in range(parts):
                c.inside[:, part * width : (part + 1) * width] = c4[part].T
            c.send()
        c_rows = c.inside[rows, :]
        grad_hidden = (slope * dot_nt(c_rows, w_down.inside[...])).astype(bf16)
        gh.inside[rows, :] = grad_hidden
        grad_normed = dot_nt(grad_hidden, w_up.inside[...])
        gain_sum = gain_sum + jnp.sum(grad_normed * hat, axis=0, keepdims=True)
        bias_sum = bias_sum + jnp.sum(grad_normed, axis=0, keepdims=True)
        grad_resid = norm_backward(hat, scale, grad_normed * gain) + c_rows.astype(f32) * (
            1.0 / parts
        )
        grad_low = grad_resid.astype(bf16)
        branch.inside[rows, :] = grad_low
        for one in (act, low, gh, resids, branch):
            one.send(pl.ds(start, span))
        for part in range(parts):
            gm.inside[part, :, rows] = dot_nt(
                w_out.inside[part * width : (part + 1) * width, :], grad_low
            ).astype(bf16)
    sums.inside[0:1, :] = gain_sum
    sums.inside[1:2, :] = bias_sum
    gm.send()
    sums.send()


def weights_kernel(pair, scalars, ins, outs, scratch):
    act, c, low, gh, mixed4, branch, w_down, resids = ins
    ffn, *wide = outs
    (made,) = scratch
    parts, width, span = mixed4.inside.shape
    chunk = span // parts
    where = scalars[0]

    def out_product():
        mixed_t = mixed4.get()[...].reshape(D, span)
        return dot(mixed_t, branch.get()[...])

    products = (
        lambda: dot_tn(act.get()[...], c.get()[...]),
        lambda: dot_tn(low.get()[...], gh.get()[...]),
        out_product,
    )
    for at, product in enumerate(products):
        if not pair:
            wide[0].inside[at] = product().astype(bf16)
            continue
        made[...] = product().astype(bf16)
        rows_count = wide[0].inside.shape[1]
        size = D // (2 * rows_count)
        for row in range(rows_count):
            for out, half in ((wide[0].inside.at[at], where[0]), (wide[1 + at].inside, 1 - where[0])):
                start = pl.multiple_of((2 * row + half) * size, size)
                out[row] = made[pl.ds(start, size), :]
        wide[1 + at].send()
        wide[0].send(at)
    if not pair:
        wide[0].send()
    w_down.get(), resids.get()
    for start in range(0, span, TILE):
        rows = slice(start, start + TILE)
        out = dot(act.inside[rows, :], w_down.inside[...]) + resids.inside[rows, :].astype(f32) * (
            1.0 / parts
        )
        out_t = out.astype(bf16).T
        for part in range(parts):
            for at in range(start, start + TILE, chunk):
                ffn.inside[part, at // chunk * width : (at // chunk + 1) * width, :] = out_t[
                    part * width : (part + 1) * width, at - start : at - start + chunk
                ]
    ffn.send()


def add_kernel(scalars, ins, outs, scratch):
    keep, *more = ins
    keep.get()
    for group, one in enumerate(more):
        one.get()
        for at, out in enumerate(outs):
            block = scalars[0][0] ^ at
            out.inside[group] = (
                keep.inside[group, block].astype(f32) + one.inside[block].astype(f32)
            ).astype(bf16)
    for out in outs[1:] + outs[:1]:
        out.send()


def row_sum_kernel(parts, scalars, ins, outs, scratch):
    ffn_own, out_parts = outs
    (rows,) = scratch
    total = ins[0].get()[...].astype(f32)
    for one in ins[1:]:
        total = total + one.get()[...].astype(f32)
    total = total.astype(bf16)
    size = total.shape[1]
    half = size // 2
    width = D // parts
    for part in range(parts):
        columns = slice(part * width, (part + 1) * width)
        out_parts.inside[part, :, :width] = total[2, :half, columns]
        out_parts.inside[part, :, width:] = total[2, half:, columns]
    out_parts.send()
    rows[...] = total[:2].reshape(2 * size, D)
    for row in range(ffn_own.outside.shape[0]):
        ffn_own.put(rows, ffn_own.outside.at[row])


SLOT = 64


def last_kernel(parts, pair, scalars, ins, outs, scratch):
    gq, normed, gkv, own, x, gain, gr, sums, gkv_more = ins
    back, *narrow = outs
    grads, small, made = scratch
    width = D // parts
    span = x.inside.shape[0]
    piece = span // parts
    lanes = 3 * width + SLOT
    grads[:, :width] = gq.get()[...]
    grads[:, 3 * width :] = jnp.zeros((span, D - 3 * width), bf16)
    gkv.get(), gkv_more.get()
    grads[:, width : 3 * width] = (
        gkv.inside[...] + gkv_more.inside[...].astype(f32)
    ).astype(bf16)
    own.get(), x.get(), gr.get(), sums.get()
    gain = gain.get()[...].reshape(1, D)
    gain_sum = jnp.zeros((1, D), f32)
    bias_sum = jnp.zeros((1, D), f32)
    for start in range(0, span, TILE):
        rows = slice(start, start + TILE)
        hat, scale = normalise(x.inside[rows, :].astype(f32))
        grad_normed = dot_nt(grads[rows, :], own.inside[...])
        gain_sum = gain_sum + jnp.sum(grad_normed * hat, axis=0, keepdims=True)
        bias_sum = bias_sum + jnp.sum(grad_normed, axis=0, keepdims=True)
        grad_in = gr.inside[rows, :].astype(f32) + norm_backward(hat, scale, grad_normed * gain)
        turned = grad_in.astype(bf16).T
        for at in range(start, start + TILE, piece):
            back.inside[at // piece] = turned[:, at - start : at - start + piece]
    pieces = D // SLOT
    for at, row in enumerate(
        (gain_sum, bias_sum, sums.inside[0:1, :], sums.inside[1:2, :])
    ):
        for part in range(pieces):
            small[at * pieces + part : at * pieces + part + 1, :] = row[
                :, part * SLOT : (part + 1) * SLOT
            ]
    made[...] = dot_tn(normed.get()[...], grads[:, :lanes]).astype(bf16)
    tail = small[...].astype(bf16)
    if pair:
        rows_count, size, _ = narrow[1].inside.shape
        for row in range(rows_count):
            for out, half in (
                (narrow[0].inside.at[0], scalars[0][0]),
                (narrow[1].inside, 1 - scalars[0][0]),
            ):
                start = pl.multiple_of((2 * row + half) * size, size)
                out[row] = made[pl.ds(start, size), :]
                out[row, :48, 3 * width :] = tail
        narrow[1].send()
        narrow[0].send()
    else:
        narrow[0].inside[...] = made[...]
        narrow[0].inside[:48, 3 * width :] = tail
        narrow[0].send()
    back.send()


def own_sum_kernel(parts, count, scalars, ins, outs, scratch):
    mine = outs[0].inside
    (small,) = scratch
    width = D // parts
    size = ins[0].inside.shape[1]
    half = size // 2
    out = ins[count].get()[0].astype(f32)
    for part in range(1, parts):
        out = out + ins[count].inside[part].astype(f32)
    mine[:half, 3 * width :] = out[:, :width].astype(bf16)
    mine[half:size, 3 * width :] = out[:, width:].astype(bf16)
    total = ins[0].get()[0].astype(f32)
    for one in ins[1:count]:
        total = total + one.get()[0].astype(f32)
    mine[:size, : 3 * width] = total[:, : 3 * width].astype(bf16)
    pieces = D // SLOT
    small[...] = jnp.zeros(small.shape, f32)
    for at in range(4):
        for part in range(pieces):
            row = at * pieces + part
            small[at : at + 1, part * SLOT : (part + 1) * SLOT] = total[
                row : row + 1, 3 * width :
            ]
    mine[size:, :] = small[...].astype(bf16)
    outs[0].send()


def output_kernel(scalars, ins, outs, scratch):
    got = ins[0].get()
    parts, _, piece = got.shape
    width = D // parts
    total = got[0, :D].astype(f32)
    for part in range(1, parts):
        total = total + got[part, :D].astype(f32)
    for at in range(parts):
        outs[0].inside[:, at * piece : (at + 1) * piece] = total[
            at * width : (at + 1) * width
        ].astype(bf16)
    outs[0].send()


def finish_kernel(scalars, ins, outs, scratch):
    grad_in, *vectors = outs
    (small,) = scratch
    size = ins[1].outside.shape[1] - 16
    ins[1].start(source=ins[1].outside.at[:, pl.ds(size, 16), :], target=small)
    back = ins[0].get()
    total = back[0].astype(f32)
    for at in range(1, back.shape[0]):
        total = total + back[at].astype(f32)
    grad_in.inside[...] = total.T.astype(bf16)
    grad_in.send()
    ins[1].get()
    sums = small[0].astype(f32)
    for at in range(1, small.shape[0]):
        sums = sums + small[at].astype(f32)
    for at, vector in enumerate(vectors):
        vector.inside[...] = sums[at]
        vector.send()


def spread_kernel(steps, scalars, ins, outs, scratch):
    (buffer,) = scratch
    row, seq = scalars
    size = buffer.shape[2]
    at = 0
    for step, (row_step, seq_step, count) in enumerate(steps):
        part = 0
        for one in ins[at : at + count]:
            got = one.get()
            for own in range(got.shape[0]):
                width = D // (got.shape[0] * count)
                columns = slice(part * width, (part + 1) * width)
                for grad in range(4):
                    buffer[grad, step, :, columns] = got[
                        own, :, grad * width : (grad + 1) * width
                    ].astype(f32)
                part += 1
        at += count
        start = pl.multiple_of((2 * (row[0] ^ row_step) + (seq[0] ^ seq_step)) * size, size)
        for grad in range(4):
            out = outs[grad]
            out.put(buffer.at[grad, step], out.outside.at[pl.ds(start, size), :])


def spread(row_here, here, steps, earlier=(), flops=0):
    count = sum(len(blocks) for _, _, blocks in steps)
    size = steps[0][2][0].shape[1]
    received = [block for _, _, blocks in steps for block in blocks]
    return staged_call(
        functools.partial(spread_kernel, [(a, b, len(c)) for a, b, c in steps]),
        [row_here, here],
        [*received, *earlier],
        (shape(D, D, kind=f32),) * 4,
        scratch=[pltpu.VMEM((4, len(steps), size, D), f32)],
        limit=SMALL_LIMIT,
        late=len(earlier),
        aliases=tuple((count + at, at) for at in range(len(earlier))),
        bare=range(4),
        flops=flops,
    )


def spread_ffn_kernel(scalars, ins, outs, scratch):
    (buffer,) = scratch
    size = buffer.shape[2]
    for half, one in enumerate(ins):
        got = one.get()
        for row in range(got.shape[0]):
            start = pl.multiple_of((2 * row + (scalars[0][0] ^ half)) * size, size)
            for grad, out in enumerate(outs):
                place = buffer.at[grad, half * got.shape[0] + row]
                place[...] = got[row, grad * size : (grad + 1) * size, :].astype(f32)
                out.put(place, out.outside.at[pl.ds(start, size), :])


def broadcast_exchange(value, axis):
    count = lax.axis_size(axis)
    return lax.all_to_all(
        jnp.broadcast_to(value[None], (count,) + value.shape), axis, 0, 0, tiled=False
    )


def swap(value):
    return lax.ppermute(value, "seq", [(0, 1), (1, 0)])


def trade(value, axis, step):
    return lax.ppermute(value, axis, [(a, a ^ step) for a in range(lax.axis_size(axis))])


def shape(*dims, kind=bf16):
    return jax.ShapeDtypeStruct(dims, kind)


def per_device(
    block_input,
    doc_ids,
    ln1_gain,
    ln1_bias,
    w_query,
    w_key,
    w_value,
    w_out,
    ln2_gain,
    ln2_bias,
    w_up,
    w_down,
    cotangent,
):
    span = block_input.shape[1]
    rows_count = lax.axis_size("row")
    seq_count = lax.axis_size("seq")
    parts = lax.axis_size("pat")
    row_index = lax.axis_index("row")
    seq_index = lax.axis_index("seq")
    pat_index = lax.axis_index("pat")
    pair = seq_count == 2
    heads = HEADS // parts
    width = D // parts
    quarter = span // parts
    size = D // (rows_count * seq_count) if pair else D
    here = seq_index.astype(jnp.int32)[None]
    row_here = row_index.astype(jnp.int32)[None]
    part_here = pat_index.astype(jnp.int32)[None]
    x = block_input[0]

    c_own = cotangent[0].T
    c_parts = [c_own] + [trade(c_own, "pat", s) for s in range(1, parts)]
    def window(scalars):
        return scalars[0][0] * width // 128 * 128

    far_shapes = (shape(span, 2 * width),) if pair else ()
    normed, q, kv, own, feats, *far = staged_call(
        functools.partial(project_kernel, parts, pair),
        [part_here, here],
        [x, doc_ids, ln1_gain, ln1_bias, w_query, w_key, w_value] + ([swap(x)] if pair else []),
        (
            shape(span, D),
            shape(span, width),
            shape(span, 2 * width),
            shape(D, D),
            shape(heads, doc_ids.shape[1], FEATS),
            *far_shapes,
        ),
        windows={4: window, 5: window, 6: window},
        flops=1 << 42,
    )

    kv_far = far[0] if pair else lax.all_gather(kv, "seq", axis=0, tiled=True)
    far_rows = kv_far.shape[0]

    mixed, mixed_t, lse = staged_call(
        functools.partial(attention_kernel, heads, span),
        [here],
        [q, kv, feats, kv_far],
        (shape(width, span), shape(width, span, kind=f32), shape(8, span, kind=f32)),
        scratch=[
            pltpu.VMEM((heads, span, width), bf16),
            pltpu.VMEM((span, width), bf16),
            pltpu.VMEM((width, span), bf16),
            pltpu.VMEM((far_rows, width), bf16),
            pltpu.VMEM((far_rows // span, width, span), bf16),
            pltpu.VMEM((heads * span // TILE + 8, TILE), f32),
            pltpu.VMEM((heads * span // TILE + 8, TILE), f32),
        ],
    )
    mixed, *c_parts = lax.optimization_barrier((mixed, *c_parts))
    mixed4 = lax.all_gather(mixed, "pat")

    wide_shapes = (shape(3, D, D),)
    if pair:
        wide_shapes = (shape(3, rows_count, size, D),) + (shape(rows_count, size, D),) * 3
    gm, sums, act, gh, branch, low, c, resids = staged_call(
        middle_kernel,
        [part_here],
        [mixed4, x, w_out, ln2_gain, ln2_bias, w_up, w_down, *c_parts],
        (shape(parts, width, span), shape(8, D, kind=f32)) + (shape(span, D),) * 6,
        scratch=[pltpu.VMEM((parts, width, span), bf16)],
        late=parts,
    )
    gm_parts = lax.all_to_all(gm, "pat", 0, 0, tiled=True)
    ffn, *wide = staged_call(
        functools.partial(weights_kernel, pair),
        [here],
        [act, c, low, gh, mixed4, branch, w_down, resids],
        (shape(parts, parts * width, quarter), *wide_shapes),
        scratch=[pltpu.VMEM((D, D), bf16)],
        flops=1 << 42,
    )

    if pair:
        keep, *sends = wide
        ordered = staged_call(
            add_kernel,
            [row_here],
            [keep, *[swap(send) for send in sends]],
            (shape(3, size, D),) * rows_count,
            limit=SMALL_LIMIT,
        )
        wide_parts = [ordered[0]] + [trade(ordered[s], "row", s) for s in range(1, rows_count)]

    ffn, _ = lax.optimization_barrier((ffn, gm_parts))
    ffn_parts = lax.all_to_all(ffn, "pat", 0, 0, tiled=True)
    (out_t,) = staged_call(
        output_kernel,
        [],
        [ffn_parts],
        (shape(width, span),),
        limit=SMALL_LIMIT,
        flops=1 << 42,
    )
    gq, gkv, gkv_far = staged_call(
        functools.partial(attention_back_kernel, heads, span),
        [here],
        [gm_parts, q, mixed_t, lse, kv, feats, kv_far],
        (
            shape(span, width),
            shape(span, 2 * width, kind=f32),
            shape(far_rows, 2 * width),
        ),
        scratch=[
            pltpu.VMEM((heads, span, width), bf16),
            pltpu.VMEM((heads, span, width), bf16),
            pltpu.VMEM((8, span), f32),
            pltpu.VMEM((span, heads * span), bf16),
            pltpu.VMEM((span, heads * span), bf16),
            pltpu.VMEM((span, width), bf16),
            pltpu.VMEM((span, width), bf16),
            pltpu.VMEM((width, span), bf16),
            pltpu.VMEM((width, span), f32),
        ],
        flops=1 << 42,
    )

    if pair:
        gkv_more = swap(gkv_far)
        ffn_own, out_parts = staged_call(
            functools.partial(row_sum_kernel, parts),
            [],
            wide_parts,
            (shape(rows_count, 2 * size, D), shape(parts, size // 2, 2 * width)),
            scratch=[pltpu.VMEM((2 * size, D), bf16)],
            limit=SMALL_LIMIT,
            bare=(0,),
        )
        out_parts, _ = lax.optimization_barrier((out_parts, ffn_parts))
        out_parts = lax.all_to_all(out_parts, "pat", 0, 0, tiled=True)
    else:
        gkv_more = lax.psum_scatter(gkv_far, "seq", scatter_dimension=0, tiled=True)

    lanes = 3 * width + SLOT
    narrow_shapes = (shape(1, rows_count, size, lanes), shape(rows_count, size, lanes)) if pair else (shape(D, lanes),)
    back, *narrow = staged_call(
        functools.partial(last_kernel, parts, pair),
        [here],
        [gq, normed, gkv, own, x, ln1_gain, branch, sums, gkv_more],
        (shape(parts, parts * width, quarter), *narrow_shapes),
        scratch=[
            pltpu.VMEM((span, D), bf16),
            pltpu.VMEM((48, SLOT), f32),
            pltpu.VMEM((D, lanes), bf16),
        ],
    )

    if pair:
        keep, send = narrow
        send, *_ = lax.optimization_barrier((send, *wide_parts[1:]))
        keep, _ = lax.optimization_barrier((keep, ffn_own))
        ordered = staged_call(
            add_kernel, [row_here], [keep, swap(send)], (shape(1, size, lanes),) * rows_count,
            limit=65000 << 10,
        )
        received = [ordered[0]] + [trade(ordered[s], "row", s) for s in range(1, rows_count)]
        received[3], _ = lax.optimization_barrier((received[3], out_t))
        (mine,) = staged_call(
            functools.partial(own_sum_kernel, parts, rows_count),
            [],
            [*received, out_parts],
            (shape(size + 16, D),),
            scratch=[pltpu.VMEM((16, D), f32)],
            limit=SMALL_LIMIT,
        )
        gathered = lax.all_gather(mine, "pat")
        ffn_own, *_ = lax.optimization_barrier(
            (ffn_own, out_parts, *received[1:])
        )
        ffn_mine = lax.all_to_all(ffn_own, "row", 0, 0, tiled=True)
        gathered, ffn_mine, back = lax.optimization_barrier((gathered, ffn_mine, back))
        back_parts = lax.all_to_all(back, "pat", 0, 0, tiled=True)
        grad_down, grad_up = staged_call(
            spread_ffn_kernel,
            [here],
            [ffn_mine, swap(ffn_mine)],
            (shape(D, D, kind=f32),) * 2,
            scratch=[pltpu.VMEM((2, 2 * rows_count, size, D), f32)],
            limit=SMALL_LIMIT,
            bare=range(2),
        )
        own = gathered[:, :size]
        near1, near2 = trade(own, "row", 1), trade(own, "row", 2)
        far = (trade(near1[: parts // 2], "row", 2), trade(near2[parts // 2 :], "row", 1))
        grads = spread(
            row_here,
            here,
            [(0, 0, (own,)), (1, 0, (near1,)), (2, 0, (near2,))]
            + [(0, 1, (swap(own),)), (1, 1, (swap(near1),)), (2, 1, (swap(near2),))],
        )
        sent = lax.optimization_barrier((*far, grads[0], grad_up))[:2]
        grads = spread(
            row_here,
            here,
            [(3, 0, far), (3, 1, tuple(swap(value) for value in sent))],
            grads,
        )
    else:
        axes = ("row", "seq")
        back_parts = lax.all_to_all(back, "pat", 0, 0, tiled=True)
        wide_sum = lax.psum(wide[0], axes)
        grad_down, grad_up = wide_sum[0].astype(f32), wide_sum[1].astype(f32)
        grad_out = lax.psum(wide_sum[2], "pat").astype(f32)
        gathered = lax.all_gather(lax.psum(narrow[0], axes), "pat")
        small = gathered[:, :48, 3 * width :].reshape(parts, 4, D)
        small = jnp.pad(small, ((0, 0), (0, 12), (0, 0)))
        grads = [
            gathered[:, :, at * width : (at + 1) * width]
            .astype(f32)
            .transpose(1, 0, 2)
            .reshape(D, D)
            for at in range(3)
        ] + [grad_out]
    if pair:
        back_parts, _ = lax.optimization_barrier((back_parts, grads[0]))
    grad_in, *vectors = staged_call(
        finish_kernel,
        [],
        [back_parts, gathered if pair else small],
        (shape(quarter, D),) + (shape(D, kind=f32),) * 4,
        scratch=[pltpu.VMEM((parts, 16, D), bf16)],
        limit=SMALL_LIMIT,
        late=1,
    )
    return (
        out_t.T[None],
        grad_in[None],
        vectors[0],
        vectors[1],
        grads[0],
        grads[1],
        grads[2],
        grads[3],
        vectors[2],
        vectors[3],
        grad_up,
        grad_down,
    )


def solution(mesh):
    placed = (
        P("row", "seq", None),
        P("row", None),
        P(),
        P(),
        P(),
        P(),
        P(),
        P(),
        P(),
        P(),
        P(None, "pat"),
        P("pat", None),
        P("row", "seq", "pat"),
    )
    return jax.shard_map(
        per_device,
        mesh=mesh,
        in_specs=placed,
        out_specs=(
            P("row", "seq", "pat"),
            P("row", ("seq", "pat"), None),
            P(),
            P(),
            P(),
            P(),
            P(),
            P(),
            P(),
            P(),
            P(None, "pat"),
            P("pat", None),
        ),
        check_vma=False,
    )
```

```python
import functools

import jax
import jax.numpy as jnp
from jax import lax
from jax.experimental import pallas as pl
from jax.experimental.pallas import tpu as pltpu
from jax.sharding import PartitionSpec as P

D = 768
HEADS = 12
HDIM = 64

epsilon = 1e-05
masked_low = -1e30
segment_parts = (1, 2, 4, 8, 16)
dilations = (1, 2, 4, 6, 12)
DOCS = 3
FEATS = 128
TILE = 256
VMEM_LIMIT = 60 * 1024 * 1024
SMALL_LIMIT = 20 * 1024 * 1024
COPIES = 64
f32 = jnp.float32
bf16 = jnp.bfloat16


def dot(a, b):
    return lax.dot_general(a, b, (((1,), (0,)), ((), ())), preferred_element_type=f32)


def dot_nt(a, b):
    return lax.dot_general(a, b, (((1,), (1,)), ((), ())), preferred_element_type=f32)


def dot_tn(a, b):
    return lax.dot_general(a, b, (((0,), (0,)), ((), ())), preferred_element_type=f32)


class Staged:
    def __init__(self, outside, inside, sems, free):
        self.outside, self.inside, self.sems, self.free = outside, inside, sems, free
        self.pending = []

    def start(self, source=None, target=None):
        copy = pltpu.make_async_copy(
            self.outside if source is None else source,
            self.inside if target is None else target,
            self.sems.at[next(self.free)],
        )
        copy.start()
        self.pending.append(copy)

    def get(self):
        for copy in self.pending:
            copy.wait()
        self.pending = []
        return self.inside

    def put(self, source, target):
        copy = pltpu.make_async_copy(source, target, self.sems.at[next(self.free)])
        copy.start()
        self.pending.append(copy)

    def send(self, at=...):
        copy = pltpu.make_async_copy(
            self.inside.at[at], self.outside.at[at], self.sems.at[next(self.free)]
        )
        copy.start()
        self.pending.append(copy)


def staged_call(body, scalars, arrays, outs, scratch=(), windows=None, limit=VMEM_LIMIT, late=0, aliases=(), bare=(), flops=0):
    windows = windows or {}
    n_scalar, n_in, n_out = len(scalars), len(arrays), len(outs)

    def kernel(*refs):
        scalar_refs, refs = refs[:n_scalar], refs[n_scalar:]
        outside, refs = refs[: n_in + n_out], refs[n_in + n_out :]
        inside, refs = refs[: n_in + n_out], refs[n_in + n_out :]
        sems, rest = refs[0], refs[1:]
        free = iter(range(COPIES))
        every = [Staged(o, i, sems, free) for o, i in zip(outside, inside, strict=True)]
        ins, results = every[:n_in], every[n_in:]
        for at, one in enumerate(ins[: n_in - late]):
            if at in windows:
                start = windows[at](scalar_refs)
                size = one.inside.shape[-1]
                one.start(one.outside.at[:, pl.ds(pl.multiple_of(start, 128), size)])
            else:
                one.start()
        body(scalar_refs, ins, results, rest)
        for one in ins + results:
            one.get()

    def buffer(at, array):
        dims = array.shape
        if at >= n_in - late:
            return pltpu.VMEM((16, 128), array.dtype)
        if at in windows:
            dims = (*dims[:-1], 256)
        return pltpu.VMEM(dims, array.dtype)

    return pl.pallas_call(
        kernel,
        out_shape=tuple(outs),
        in_specs=[pl.BlockSpec(memory_space=pltpu.SMEM)] * n_scalar
        + [pl.BlockSpec(memory_space=pl.ANY)] * n_in,
        out_specs=(pl.BlockSpec(memory_space=pltpu.HBM),) * n_out,
        scratch_shapes=[buffer(at, a) for at, a in enumerate(arrays)]
        + [
            pltpu.VMEM((16, 128) if at in bare else o.shape, o.dtype)
            for at, o in enumerate(outs)
        ]
        + [pltpu.SemaphoreType.DMA((COPIES,))]
        + list(scratch),
        input_output_aliases={n_scalar + a: o for a, o in aliases},
        compiler_params=pltpu.CompilerParams(vmem_limit_bytes=limit),
        cost_estimate=pl.CostEstimate(flops=flops, bytes_accessed=0, transcendentals=0),
    )(*scalars, *arrays)


def normalise(values):
    center = values - jnp.mean(values, axis=-1, keepdims=True)
    scale = lax.rsqrt(jnp.mean(center * center, axis=-1, keepdims=True) + epsilon)
    return center * scale, scale


def norm_backward(hat, scale, grad):
    return scale * (
        grad
        - jnp.mean(grad, axis=-1, keepdims=True)
        - hat * jnp.mean(grad * hat, axis=-1, keepdims=True)
    )


def make_features(heads, part, docs, feats):
    _, length, _ = feats.inside.shape
    position = lax.broadcasted_iota(jnp.int32, (1, length), 1)
    feature = lax.broadcasted_iota(jnp.int32, (FEATS, length), 0)
    for h in range(heads):
        head = part * heads + h
        hit = None
        base = 0
        for size, dilation in zip(segment_parts, dilations, strict=True):
            seg_width = length * size // 16
            inside = lax.rem(
                lax.rem(position, seg_width) + dilation - lax.rem(head, dilation), dilation
            )
            key = base + lax.div(position, seg_width) * DOCS + docs
            key = jnp.where(inside == 0, key, -1)
            found = feature == key
            hit = found if hit is None else hit | found
            base += DOCS * (16 // size)
        feats.inside[h] = jnp.where(hit, 1.0, 0.0).T.astype(bf16)
        feats.send(h)


def project_kernel(parts, pair, scalars, ins, outs, scratch):
    x, docs, gain, bias, *weights = ins[:7]
    normed, q, kv, own, feats = outs[:5]
    width = D // parts
    where = scalars[0]
    own.inside[:, 3 * width :] = jnp.zeros((D, D - 3 * width), bf16)
    gain = gain.get()[...].reshape(1, D)
    bias = bias.get()[...].reshape(1, D)
    x.get()
    span = x.inside.shape[0]
    for start in range(0, span, TILE):
        rows = slice(start, start + TILE)
        hat, _ = normalise(x.inside[rows, :].astype(f32))
        normed.inside[rows, :] = (hat * gain + bias).astype(bf16)
    normed.send()
    for w in weights:
        w.get()
    for odd in range(2):

        @pl.when(where[0] % 2 == odd)
        def _():
            for at, w in enumerate(weights):
                own.inside[:, at * width : (at + 1) * width] = w.inside[
                    :, odd * 64 : odd * 64 + width
                ]

    own.send()
    for start in range(0, span, TILE):
        rows = slice(start, start + TILE)
        made = dot(normed.inside[rows, :], own.inside[:, : 3 * width]).astype(bf16)
        q.inside[rows, :] = (made[:, :width].astype(f32) * HDIM**-0.5).astype(bf16)
        kv.inside[rows, :] = made[:, width:]
    kv.send()
    q.send()
    if pair:
        x_far = ins[7].get()

        @pl.when(scalars[1][0] > 0)
        def _():
            for start in range(0, span, TILE):
                rows = slice(start, start + TILE)
                hat, _ = normalise(x_far[rows, :].astype(f32))
                low = (hat * gain + bias).astype(bf16)
                outs[5].inside[rows, :] = dot(low, own.inside[:, width : 3 * width]).astype(bf16)

        outs[5].send()
    make_features(feats.inside.shape[0], where[0], docs.get()[...], feats)


def head_mask(heads, width):
    lane = lax.broadcasted_iota(jnp.int32, (1, width), 1)
    return [((lane >= h * HDIM) & (lane < (h + 1) * HDIM)).astype(bf16) for h in range(heads)]


def attention_kernel(heads, span, scalars, ins, outs, scratch):
    where = scalars[0]
    q, kv, feats, kv_far = (one.get() for one in ins)
    mixed_low, mixed_t, lse = (one.inside for one in outs)
    q_head, k, v_t, kf, vf_t, tops, totals = scratch
    width = heads * HDIM
    masks = head_mask(heads, width)
    for h in range(heads):
        q_head[h] = q[...] * masks[h]
    k[...] = kv[:, :width]
    v_t[...] = kv[:, width:].T
    far = kv_far.shape[0] // span

    def turn(j, _):
        rows = pl.ds(pl.multiple_of(j * span, span), span)
        kf[rows, :] = kv_far[rows, :width]
        vf_t[j] = kv_far[rows, width:].T
        return 0

    mine = where[0]
    lax.fori_loop(0, jnp.minimum(mine, far), turn, 0)
    own_start = pl.multiple_of(mine * span, span)
    lse[...] = jnp.zeros(lse.shape, f32)
    pairs = [(start, h) for start in range(0, span, TILE) for h in range(heads)]

    def part(start, h, k_rows, f_rows, v_rows, causal):
        counts = dot_nt(f_rows, feats[h, pl.ds(own_start + start, TILE), :])
        if causal:
            at_k = lax.broadcasted_iota(jnp.int32, counts.shape, 0)
            at_q = lax.broadcasted_iota(jnp.int32, counts.shape, 1) + start
            counts = jnp.where(at_k <= at_q, counts, 0.0)
        scores = dot_nt(k_rows, q_head[h, start : start + TILE, :])
        scores = jnp.where(counts > 0, scores, masked_low)
        return counts, scores, v_rows

    for at, (start, h) in enumerate(pairs):
        size = start + TILE
        head_rows = slice(h * HDIM, (h + 1) * HDIM)
        counts, scores, v_rows = part(
            start,
            h,
            k[:size, :],
            feats[h, pl.ds(own_start, size), :],
            v_t[head_rows, :size],
            True,
        )
        top = jnp.max(scores, axis=0, keepdims=True)
        weights = counts * jnp.exp(scores - top)
        tops[at : at + 1, :] = top
        totals[at : at + 1, :] = jnp.sum(weights, axis=0, keepdims=True)
        mixed_t[head_rows, start : start + TILE] = dot(v_rows, weights.astype(bf16))

    def far_step(j, _):
        rows = pl.ds(pl.multiple_of(j * span, span), span)
        for at, (start, h) in enumerate(pairs):
            head_rows = slice(h * HDIM, (h + 1) * HDIM)
            counts, scores, v_rows = part(
                start, h, kf[rows, :], feats[h, rows, :], vf_t[j, head_rows, :], False
            )
            top = tops[at : at + 1, :]
            new_top = jnp.maximum(top, jnp.max(scores, axis=0, keepdims=True))
            weights = counts * jnp.exp(scores - new_top)
            factor = jnp.exp(top - new_top)
            tops[at : at + 1, :] = new_top
            totals[at : at + 1, :] = totals[at : at + 1, :] * factor + jnp.sum(
                weights, axis=0, keepdims=True
            )
            mixed_t[head_rows, start : start + TILE] = mixed_t[
                head_rows, start : start + TILE
            ] * factor + dot(v_rows, weights.astype(bf16))
        return 0

    lax.fori_loop(0, mine, far_step, 0)
    for at, (start, h) in enumerate(pairs):
        head_rows = slice(h * HDIM, (h + 1) * HDIM)
        total = totals[at : at + 1, :]
        done = mixed_t[head_rows, start : start + TILE] / total
        mixed_t[head_rows, start : start + TILE] = done
        mixed_low[head_rows, start : start + TILE] = done.astype(bf16)
        lse[h : h + 1, start : start + TILE] = tops[at : at + 1, :] + jnp.log(total)
    for one in outs:
        one.send()


def count_rows(f_rows, f_tile, low_from):
    counts = dot_nt(f_rows, f_tile)
    if low_from is not None:
        at_k = lax.broadcasted_iota(jnp.int32, counts.shape, 0)
        at_q = lax.broadcasted_iota(jnp.int32, counts.shape, 1) + low_from
        counts = jnp.where(at_k <= at_q, counts, 0.0)
    return counts


def attention_back_kernel(heads, span, scalars, ins, outs, scratch):
    where = scalars[0]
    parts, q, mixed_t, lse, kv, feats, kv_far = (one.get() for one in ins)
    grad_q, grad_kv, grad_far = (one.inside for one in outs)
    q_head, g_head, dots, probs, slopes, k, v, k_t, gq_t = scratch
    width = heads * HDIM
    masks = head_mask(heads, width)
    mine = where[0]
    far = kv_far.shape[0] // span
    total = parts[0].astype(f32)
    for part in range(1, parts.shape[0]):
        total = total + parts[part].astype(f32)
    low_t = total.astype(bf16)
    low = low_t.T
    for h in range(heads):
        q_head[h] = q[...] * masks[h]
        g_head[h] = low * masks[h]
    product = low_t.astype(f32) * mixed_t[...]
    for h in range(heads):
        dots[h : h + 1, :] = jnp.sum(product[h * HDIM : (h + 1) * HDIM], axis=0, keepdims=True)
    own_start = pl.multiple_of(mine * span, span)

    def block(h, start, size, rows, diagonal):
        tile = slice(start, start + TILE)
        columns = slice(h * span + start, h * span + start + TILE)
        f_rows = feats[h, pl.ds(own_start, size) if diagonal else rows, :]
        f_tile = feats[h, pl.ds(own_start + start, TILE), :]
        counts = count_rows(f_rows, f_tile, start if diagonal else None)
        scores = jnp.where(counts > 0, dot_nt(k[:size, :], q_head[h, tile, :]), masked_low)
        prob = counts * jnp.exp(scores - lse[h : h + 1, tile])
        grad_prob = dot_nt(v[:size, :], g_head[h, tile, :])
        slope = prob * (grad_prob - dots[h : h + 1, tile])
        probs[:size, columns] = prob.astype(bf16)
        slopes[:size, columns] = slope.astype(bf16)
        if size < span:
            probs[size:, columns] = jnp.zeros((span - size, TILE), bf16)
            slopes[size:, columns] = jnp.zeros((span - size, TILE), bf16)

    def finish():
        k_t[...] = k[...].T
        grad_v_rows = dot(probs[...], g_head[...].reshape(heads * span, width))
        grad_k_rows = dot(slopes[...], q_head[...].reshape(heads * span, width))
        terms = [
            dot(k_t[h * HDIM : (h + 1) * HDIM, :], slopes[:, h * span : (h + 1) * span])
            for h in range(heads)
        ]
        return grad_k_rows, grad_v_rows, terms

    k[...] = kv[:, :width]
    v[...] = kv[:, width:]
    for start in range(0, span, TILE):
        for h in range(heads):
            size = start + TILE
            block(h, start, size, None, True)
    grad_k_rows, grad_v_rows, terms = finish()
    grad_kv[:, :width] = grad_k_rows
    grad_kv[:, width:] = grad_v_rows
    outs[1].send()
    for h in range(heads):
        gq_t[h * HDIM : (h + 1) * HDIM, :] = terms[h]

    def far_block(j, _):
        rows = pl.ds(pl.multiple_of(j * span, span), span)
        k[...] = kv_far[rows, :width]
        v[...] = kv_far[rows, width:]
        for start in range(0, span, TILE):
            for h in range(heads):
                block(h, start, span, rows, False)
        grad_k_rows, grad_v_rows, terms = finish()
        grad_far[rows, :width] = grad_k_rows.astype(bf16)
        grad_far[rows, width:] = grad_v_rows.astype(bf16)
        for h in range(heads):
            gq_t[h * HDIM : (h + 1) * HDIM, :] += terms[h]
        return 0

    used = jnp.minimum(mine, far)
    lax.fori_loop(0, used, far_block, 0)

    def clear(j, _):
        grad_far[pl.ds(pl.multiple_of(j * span, span), span), :] = jnp.zeros((span, 2 * width), bf16)
        return 0

    lax.fori_loop(used, far, clear, 0)
    outs[2].send()
    grad_q[...] = (gq_t[...] * HDIM**-0.5).T.astype(bf16)
    outs[0].send()


def middle_kernel(scalars, ins, outs, scratch):
    mixed4, x, w_out, gain, bias, w_up, w_down, *c_parts = ins
    gm, sums, act, gh, branch, low, c, resids = outs
    (c4,) = scratch
    parts, width, span = mixed4.inside.shape
    for step, one in enumerate(c_parts):
        one.start(target=c4.at[scalars[0][0] ^ step])
    mixed_t = mixed4.get()[...].reshape(D, span)
    x.get(), w_out.get()
    gain = gain.get()[...].reshape(1, D)
    bias = bias.get()[...].reshape(1, D)
    gain_sum = jnp.zeros((1, D), f32)
    bias_sum = jnp.zeros((1, D), f32)
    for start in range(0, span, span):
        rows = slice(start, start + span)
        resid = x.inside[rows, :].astype(f32) + dot_tn(mixed_t[:, rows], w_out.inside[...])
        resids.inside[rows, :] = resid.astype(bf16)
        hat, scale = normalise(resid)
        normed = (hat * gain + bias).astype(bf16)
        low.inside[rows, :] = normed
        w_up.get()
        hidden = dot(normed, w_up.inside[...])
        bell = 0.5 + 0.5 * lax.erf(hidden * (0.5**0.5))
        act.inside[rows, :] = (hidden * bell).astype(bf16)
        slope = bell + hidden * jnp.exp(-0.5 * hidden * hidden) * 0.3989422804014327
        if start == 0:
            w_down.get()
            for one in c_parts:
                one.get()
            for part in range(parts):
                c.inside[:, part * width : (part + 1) * width] = c4[part].T
            c.send()
        c_rows = c.inside[rows, :]
        grad_hidden = (slope * dot_nt(c_rows, w_down.inside[...])).astype(bf16)
        gh.inside[rows, :] = grad_hidden
        grad_normed = dot_nt(grad_hidden, w_up.inside[...])
        gain_sum = gain_sum + jnp.sum(grad_normed * hat, axis=0, keepdims=True)
        bias_sum = bias_sum + jnp.sum(grad_normed, axis=0, keepdims=True)
        grad_resid = norm_backward(hat, scale, grad_normed * gain) + c_rows.astype(f32) * (
            1.0 / parts
        )
        grad_low = grad_resid.astype(bf16)
        branch.inside[rows, :] = grad_low
        for one in (act, low, gh, resids, branch):
            one.send(pl.ds(start, span))
        for part in range(parts):
            gm.inside[part, :, rows] = dot_nt(
                w_out.inside[part * width : (part + 1) * width, :], grad_low
            ).astype(bf16)
            gm.send(part)
    sums.inside[0:1, :] = gain_sum
    sums.inside[1:2, :] = bias_sum
    sums.send()


def weights_kernel(pair, scalars, ins, outs, scratch):
    act, c, low, gh, mixed4, branch, w_down, resids = ins
    ffn, *wide = outs
    (made,) = scratch
    parts, width, span = mixed4.inside.shape
    chunk = span // parts
    where = scalars[0]

    def out_product():
        mixed_t = mixed4.get()[...].reshape(D, span)
        return dot(mixed_t, branch.get()[...])

    products = (
        lambda: dot_tn(act.get()[...], c.get()[...]),
        lambda: dot_tn(low.get()[...], gh.get()[...]),
        out_product,
    )
    for at, product in enumerate(products):
        if not pair:
            wide[0].inside[at] = product().astype(bf16)
            continue
        made[...] = product().astype(bf16)
        rows_count = wide[0].inside.shape[1]
        size = D // (2 * rows_count)
        for row in range(rows_count):
            for out, half in ((wide[0].inside.at[at], where[0]), (wide[1 + at].inside, 1 - where[0])):
                start = pl.multiple_of((2 * row + half) * size, size)
                out[row] = made[pl.ds(start, size), :]
        wide[1 + at].send()
        wide[0].send(at)
    if not pair:
        wide[0].send()
    w_down.get(), resids.get()
    for start in range(0, span, TILE):
        rows = slice(start, start + TILE)
        out = dot(act.inside[rows, :], w_down.inside[...]) + resids.inside[rows, :].astype(f32) * (
            1.0 / parts
        )
        out_t = out.astype(bf16).T
        for part in range(parts):
            for at in range(start, start + TILE, chunk):
                ffn.inside[part, at // chunk * width : (at // chunk + 1) * width, :] = out_t[
                    part * width : (part + 1) * width, at - start : at - start + chunk
                ]
    ffn.send()


def add_kernel(scalars, ins, outs, scratch):
    keep, *more = ins
    keep.get()
    for group, one in enumerate(more):
        one.get()
        for at, out in enumerate(outs):
            block = scalars[0][0] ^ at
            out.inside[group] = (
                keep.inside[group, block].astype(f32) + one.inside[block].astype(f32)
            ).astype(bf16)
    for out in outs[1:] + outs[:1]:
        out.send()


def row_sum_kernel(parts, scalars, ins, outs, scratch):
    ffn_own, out_parts = outs
    (rows,) = scratch
    total = ins[0].get()[...].astype(f32)
    for one in ins[1:]:
        total = total + one.get()[...].astype(f32)
    total = total.astype(bf16)
    size = total.shape[1]
    half = size // 2
    width = D // parts
    for part in range(parts):
        columns = slice(part * width, (part + 1) * width)
        out_parts.inside[part, :, :width] = total[2, :half, columns]
        out_parts.inside[part, :, width:] = total[2, half:, columns]
    out_parts.send()
    rows[...] = total[:2].reshape(2 * size, D)
    for row in range(ffn_own.outside.shape[0]):
        ffn_own.put(rows, ffn_own.outside.at[row])


SLOT = 64


def last_kernel(parts, pair, scalars, ins, outs, scratch):
    gq, gkv, gkv_more, normed, own, x, gain, gr, sums = ins
    back, *narrow = outs
    grads, small, made = scratch
    width = D // parts
    span = x.inside.shape[0]
    piece = span // parts
    lanes = 3 * width + SLOT
    grads[:, 3 * width :] = jnp.zeros((span, D - 3 * width), bf16)
    grads[:, :width] = gq.get()[...]
    gkv.get(), gkv_more.get()
    grads[:, width : 3 * width] = (
        gkv.inside[...] + gkv_more.inside[...].astype(f32)
    ).astype(bf16)
    made[...] = dot_tn(normed.get()[...], grads[:, :lanes]).astype(bf16)
    if pair:
        rows_count, size, _ = narrow[1].inside.shape
        halves = (
            (narrow[0].inside.at[0], scalars[0][0]),
            (narrow[1].inside, 1 - scalars[0][0]),
        )
        for row in range(rows_count):
            for out, half in halves:
                start = pl.multiple_of((2 * row + half) * size, size)
                out[row] = made[pl.ds(start, size), :]
    else:
        narrow[0].inside[...] = made[...]
    own.get(), x.get(), gr.get(), sums.get()
    gain = gain.get()[...].reshape(1, D)
    gain_sum = jnp.zeros((1, D), f32)
    bias_sum = jnp.zeros((1, D), f32)
    for start in range(0, span, TILE):
        rows = slice(start, start + TILE)
        hat, scale = normalise(x.inside[rows, :].astype(f32))
        grad_normed = dot_nt(grads[rows, :], own.inside[...])
        gain_sum = gain_sum + jnp.sum(grad_normed * hat, axis=0, keepdims=True)
        bias_sum = bias_sum + jnp.sum(grad_normed, axis=0, keepdims=True)
        grad_in = gr.inside[rows, :].astype(f32) + norm_backward(hat, scale, grad_normed * gain)
        turned = grad_in.astype(bf16).T
        for at in range(start, start + TILE, piece):
            back.inside[at // piece] = turned[:, at - start : at - start + piece]
            back.send(at // piece)
    pieces = D // SLOT
    for at, row in enumerate(
        (gain_sum, bias_sum, sums.inside[0:1, :], sums.inside[1:2, :])
    ):
        for part in range(pieces):
            small[at * pieces + part : at * pieces + part + 1, :] = row[
                :, part * SLOT : (part + 1) * SLOT
            ]
    tail = small[...].astype(bf16)
    if pair:
        for row in range(rows_count):
            for out, _ in halves:
                out[row, :48, 3 * width :] = tail
        narrow[1].send()
        narrow[0].send()
    else:
        narrow[0].inside[:48, 3 * width :] = tail
        narrow[0].send()


def own_sum_kernel(parts, count, scalars, ins, outs, scratch):
    mine = outs[0].inside
    (small,) = scratch
    width = D // parts
    size = ins[0].inside.shape[1]
    half = size // 2
    out = ins[count].get()[0].astype(f32)
    for part in range(1, parts):
        out = out + ins[count].inside[part].astype(f32)
    mine[:half, 3 * width :] = out[:, :width].astype(bf16)
    mine[half:size, 3 * width :] = out[:, width:].astype(bf16)
    total = ins[0].get()[0].astype(f32)
    for one in ins[1:count]:
        total = total + one.get()[0].astype(f32)
    mine[:size, : 3 * width] = total[:, : 3 * width].astype(bf16)
    pieces = D // SLOT
    small[...] = jnp.zeros(small.shape, f32)
    for at in range(4):
        for part in range(pieces):
            row = at * pieces + part
            small[at : at + 1, part * SLOT : (part + 1) * SLOT] = total[
                row : row + 1, 3 * width :
            ]
    mine[size:, :] = small[...].astype(bf16)
    outs[0].send()


def output_kernel(scalars, ins, outs, scratch):
    got = ins[0].get()
    parts, _, piece = got.shape
    width = D // parts
    total = got[0, :D].astype(f32)
    for part in range(1, parts):
        total = total + got[part, :D].astype(f32)
    for at in range(parts):
        outs[0].inside[:, at * piece : (at + 1) * piece] = total[
            at * width : (at + 1) * width
        ].astype(bf16)
    outs[0].send()


def finish_kernel(scalars, ins, outs, scratch):
    grad_in, *vectors = outs
    (small,) = scratch
    size = ins[1].outside.shape[1] - 16
    ins[1].start(source=ins[1].outside.at[:, pl.ds(size, 16), :], target=small)
    back = ins[0].get()
    total = back[0].astype(f32)
    for at in range(1, back.shape[0]):
        total = total + back[at].astype(f32)
    grad_in.inside[...] = total.T.astype(bf16)
    grad_in.send()
    ins[1].get()
    sums = small[0].astype(f32)
    for at in range(1, small.shape[0]):
        sums = sums + small[at].astype(f32)
    for at, vector in enumerate(vectors):
        vector.inside[...] = sums[at]
        vector.send()


def spread_kernel(steps, scalars, ins, outs, scratch):
    (buffer,) = scratch
    row, seq = scalars
    size = buffer.shape[2]
    at = 0
    for step, (row_step, seq_step, count) in enumerate(steps):
        part = 0
        for one in ins[at : at + count]:
            got = one.get()
            for own in range(got.shape[0]):
                width = D // (got.shape[0] * count)
                columns = slice(part * width, (part + 1) * width)
                for grad in range(4):
                    buffer[grad, step, :, columns] = got[
                        own, :, grad * width : (grad + 1) * width
                    ].astype(f32)
                part += 1
        at += count
        start = pl.multiple_of((2 * (row[0] ^ row_step) + (seq[0] ^ seq_step)) * size, size)
        for grad in range(4):
            out = outs[grad]
            out.put(buffer.at[grad, step], out.outside.at[pl.ds(start, size), :])


def spread(row_here, here, steps, earlier=(), flops=0):
    count = sum(len(blocks) for _, _, blocks in steps)
    size = steps[0][2][0].shape[1]
    received = [block for _, _, blocks in steps for block in blocks]
    return staged_call(
        functools.partial(spread_kernel, [(a, b, len(c)) for a, b, c in steps]),
        [row_here, here],
        [*received, *earlier],
        (shape(D, D, kind=f32),) * 4,
        scratch=[pltpu.VMEM((4, len(steps), size, D), f32)],
        limit=SMALL_LIMIT,
        late=len(earlier),
        aliases=tuple((count + at, at) for at in range(len(earlier))),
        bare=range(4),
        flops=flops,
    )


def spread_ffn_kernel(scalars, ins, outs, scratch):
    (buffer,) = scratch
    size = buffer.shape[2]
    for half, one in enumerate(ins):
        got = one.get()
        for row in range(got.shape[0]):
            start = pl.multiple_of((2 * row + (scalars[0][0] ^ half)) * size, size)
            for grad, out in enumerate(outs):
                place = buffer.at[grad, half * got.shape[0] + row]
                place[...] = got[row, grad * size : (grad + 1) * size, :].astype(f32)
                out.put(place, out.outside.at[pl.ds(start, size), :])


def first_spread_kernel(steps, scalars, ins, outs, scratch):
    spread_ffn_kernel(scalars[1:], ins[:2], outs[:2], scratch[:1])
    spread_kernel(steps, scalars, ins[2:], outs[2:], scratch[1:])


def broadcast_exchange(value, axis):
    count = lax.axis_size(axis)
    return lax.all_to_all(
        jnp.broadcast_to(value[None], (count,) + value.shape), axis, 0, 0, tiled=False
    )


def swap(value):
    return lax.ppermute(value, "seq", [(0, 1), (1, 0)])


def trade(value, axis, step):
    return lax.ppermute(value, axis, [(a, a ^ step) for a in range(lax.axis_size(axis))])


def shape(*dims, kind=bf16):
    return jax.ShapeDtypeStruct(dims, kind)


def per_device(
    block_input,
    doc_ids,
    ln1_gain,
    ln1_bias,
    w_query,
    w_key,
    w_value,
    w_out,
    ln2_gain,
    ln2_bias,
    w_up,
    w_down,
    cotangent,
):
    span = block_input.shape[1]
    rows_count = lax.axis_size("row")
    seq_count = lax.axis_size("seq")
    parts = lax.axis_size("pat")
    row_index = lax.axis_index("row")
    seq_index = lax.axis_index("seq")
    pat_index = lax.axis_index("pat")
    pair = seq_count == 2
    heads = HEADS // parts
    width = D // parts
    quarter = span // parts
    size = D // (rows_count * seq_count) if pair else D
    here = seq_index.astype(jnp.int32)[None]
    row_here = row_index.astype(jnp.int32)[None]
    part_here = pat_index.astype(jnp.int32)[None]
    x = block_input[0]

    c_own = cotangent[0].T
    c_parts = [c_own] + [trade(c_own, "pat", s) for s in range(1, parts)]
    def window(scalars):
        return scalars[0][0] * width // 128 * 128

    far_shapes = (shape(span, 2 * width),) if pair else ()
    normed, q, kv, own, feats, *far = staged_call(
        functools.partial(project_kernel, parts, pair),
        [part_here, here],
        [x, doc_ids, ln1_gain, ln1_bias, w_query, w_key, w_value] + ([swap(x)] if pair else []),
        (
            shape(span, D),
            shape(span, width),
            shape(span, 2 * width),
            shape(D, D),
            shape(heads, doc_ids.shape[1], FEATS),
            *far_shapes,
        ),
        windows={4: window, 5: window, 6: window},
        flops=1 << 42,
    )

    kv_far = far[0] if pair else lax.all_gather(kv, "seq", axis=0, tiled=True)
    far_rows = kv_far.shape[0]

    mixed, mixed_t, lse = staged_call(
        functools.partial(attention_kernel, heads, span),
        [here],
        [q, kv, feats, kv_far],
        (shape(width, span), shape(width, span, kind=f32), shape(8, span, kind=f32)),
        scratch=[
            pltpu.VMEM((heads, span, width), bf16),
            pltpu.VMEM((span, width), bf16),
            pltpu.VMEM((width, span), bf16),
            pltpu.VMEM((far_rows, width), bf16),
            pltpu.VMEM((far_rows // span, width, span), bf16),
            pltpu.VMEM((heads * span // TILE + 8, TILE), f32),
            pltpu.VMEM((heads * span // TILE + 8, TILE), f32),
        ],
    )
    mixed, *c_parts = lax.optimization_barrier((mixed, *c_parts))
    mixed4 = lax.all_gather(mixed, "pat")

    wide_shapes = (shape(3, D, D),)
    if pair:
        wide_shapes = (shape(3, rows_count, size, D),) + (shape(rows_count, size, D),) * 3
    gm, sums, act, gh, branch, low, c, resids = staged_call(
        middle_kernel,
        [part_here],
        [mixed4, x, w_out, ln2_gain, ln2_bias, w_up, w_down, *c_parts],
        (shape(parts, width, span), shape(8, D, kind=f32)) + (shape(span, D),) * 6,
        scratch=[pltpu.VMEM((parts, width, span), bf16)],
        late=parts,
    )
    gm_parts = lax.all_to_all(gm, "pat", 0, 0, tiled=True)
    ffn, *wide = staged_call(
        functools.partial(weights_kernel, pair),
        [here],
        [act, c, low, gh, mixed4, branch, w_down, resids],
        (shape(parts, parts * width, quarter), *wide_shapes),
        scratch=[pltpu.VMEM((D, D), bf16)],
        flops=1 << 42,
    )

    if pair:
        keep, *sends = wide
        ordered = staged_call(
            add_kernel,
            [row_here],
            [keep, *[swap(send) for send in sends]],
            (shape(3, size, D),) * rows_count,
            limit=SMALL_LIMIT,
        )
        wide_parts = [ordered[0]] + [trade(ordered[s], "row", s) for s in range(1, rows_count)]

    ffn, _ = lax.optimization_barrier((ffn, gm_parts))
    ffn_parts = lax.all_to_all(ffn, "pat", 0, 0, tiled=True)
    (out_t,) = staged_call(
        output_kernel,
        [],
        [ffn_parts],
        (shape(width, span),),
        limit=SMALL_LIMIT,
        flops=1 << 42,
    )
    gq, gkv, gkv_far = staged_call(
        functools.partial(attention_back_kernel, heads, span),
        [here],
        [gm_parts, q, mixed_t, lse, kv, feats, kv_far],
        (
            shape(span, width),
            shape(span, 2 * width, kind=f32),
            shape(far_rows, 2 * width),
        ),
        scratch=[
            pltpu.VMEM((heads, span, width), bf16),
            pltpu.VMEM((heads, span, width), bf16),
            pltpu.VMEM((8, span), f32),
            pltpu.VMEM((span, heads * span), bf16),
            pltpu.VMEM((span, heads * span), bf16),
            pltpu.VMEM((span, width), bf16),
            pltpu.VMEM((span, width), bf16),
            pltpu.VMEM((width, span), bf16),
            pltpu.VMEM((width, span), f32),
        ],
        flops=1 << 42,
    )

    if pair:
        gkv_more = swap(gkv_far)
        ffn_own, out_parts = staged_call(
            functools.partial(row_sum_kernel, parts),
            [],
            wide_parts,
            (shape(rows_count, 2 * size, D), shape(parts, size // 2, 2 * width)),
            scratch=[pltpu.VMEM((2 * size, D), bf16)],
            limit=SMALL_LIMIT,
            bare=(0,),
        )
        out_parts, _ = lax.optimization_barrier((out_parts, ffn_parts))
        out_parts = lax.all_to_all(out_parts, "pat", 0, 0, tiled=True)
    else:
        gkv_more = lax.psum_scatter(gkv_far, "seq", scatter_dimension=0, tiled=True)

    lanes = 3 * width + SLOT
    narrow_shapes = (shape(1, rows_count, size, lanes), shape(rows_count, size, lanes)) if pair else (shape(D, lanes),)
    back, *narrow = staged_call(
        functools.partial(last_kernel, parts, pair),
        [here],
        [gq, gkv, gkv_more, normed, own, x, ln1_gain, branch, sums],
        (shape(parts, parts * width, quarter), *narrow_shapes),
        scratch=[
            pltpu.VMEM((span, D), bf16),
            pltpu.VMEM((48, SLOT), f32),
            pltpu.VMEM((D, lanes), bf16),
        ],
    )

    if pair:
        keep, send = narrow
        send, *_ = lax.optimization_barrier((send, *wide_parts[1:]))
        keep, _ = lax.optimization_barrier((keep, ffn_own))
        ordered = staged_call(
            add_kernel, [row_here], [keep, swap(send)], (shape(1, size, lanes),) * rows_count,
            limit=65000 << 10,
        )
        received = [ordered[0]] + [trade(ordered[s], "row", s) for s in range(1, rows_count)]
        received[3], _ = lax.optimization_barrier((received[3], out_t))
        (mine,) = staged_call(
            functools.partial(own_sum_kernel, parts, rows_count),
            [],
            [*received, out_parts],
            (shape(size + 16, D),),
            scratch=[pltpu.VMEM((16, D), f32)],
            limit=SMALL_LIMIT,
        )
        gathered = lax.all_gather(mine, "pat")
        ffn_own, *_ = lax.optimization_barrier(
            (ffn_own, out_parts, *received[1:])
        )
        ffn_mine = lax.all_to_all(ffn_own, "row", 0, 0, tiled=True)
        gathered, ffn_mine, back = lax.optimization_barrier((gathered, ffn_mine, back))
        back_parts = lax.all_to_all(back, "pat", 0, 0, tiled=True)
        own = gathered[:, :size]
        near1, near2 = trade(own, "row", 1), trade(own, "row", 2)
        half1, half2 = near1[: parts // 2], near2[parts // 2 :]
        far = (trade(half1, "row", 2), trade(half2, "row", 1))
        sent1, _ = lax.optimization_barrier((near1, half1))
        sent2, _ = lax.optimization_barrier((near2, half2))
        steps = [(0, 0, 1), (1, 0, 1), (2, 0, 1), (0, 1, 1), (1, 1, 1), (2, 1, 1)]
        grad_down, grad_up, *grads = staged_call(
            functools.partial(first_spread_kernel, steps),
            [row_here, here],
            [
                ffn_mine,
                swap(ffn_mine),
                own,
                near1,
                near2,
                swap(own),
                swap(sent1),
                swap(sent2),
            ],
            (shape(D, D, kind=f32),) * 6,
            scratch=[
                pltpu.VMEM((2, 2 * rows_count, size, D), f32),
                pltpu.VMEM((4, len(steps), size, D), f32),
            ],
            limit=24 << 20,
            bare=range(6),
        )
        sent = lax.optimization_barrier((*far, grads[0]))[:2]
        grads = spread(
            row_here,
            here,
            [(3, 0, far), (3, 1, tuple(swap(value) for value in sent))],
            grads,
        )
    else:
        axes = ("row", "seq")
        back_parts = lax.all_to_all(back, "pat", 0, 0, tiled=True)
        wide_sum = lax.psum(wide[0], axes)
        grad_down, grad_up = wide_sum[0].astype(f32), wide_sum[1].astype(f32)
        grad_out = lax.psum(wide_sum[2], "pat").astype(f32)
        gathered = lax.all_gather(lax.psum(narrow[0], axes), "pat")
        small = gathered[:, :48, 3 * width :].reshape(parts, 4, D)
        small = jnp.pad(small, ((0, 0), (0, 12), (0, 0)))
        grads = [
            gathered[:, :, at * width : (at + 1) * width]
            .astype(f32)
            .transpose(1, 0, 2)
            .reshape(D, D)
            for at in range(3)
        ] + [grad_out]
    if pair:
        back_parts, _ = lax.optimization_barrier((back_parts, grads[0]))
    grad_in, *vectors = staged_call(
        finish_kernel,
        [],
        [back_parts, gathered if pair else small],
        (shape(quarter, D),) + (shape(D, kind=f32),) * 4,
        scratch=[pltpu.VMEM((parts, 16, D), bf16)],
        limit=SMALL_LIMIT,
        late=1,
    )
    return (
        out_t.T[None],
        grad_in[None],
        vectors[0],
        vectors[1],
        grads[0],
        grads[1],
        grads[2],
        grads[3],
        vectors[2],
        vectors[3],
        grad_up,
        grad_down,
    )


def solution(mesh):
    placed = (
        P("row", "seq", None),
        P("row", None),
        P(),
        P(),
        P(),
        P(),
        P(),
        P(),
        P(),
        P(),
        P(None, "pat"),
        P("pat", None),
        P("row", "seq", "pat"),
    )
    return jax.shard_map(
        per_device,
        mesh=mesh,
        in_specs=placed,
        out_specs=(
            P("row", "seq", "pat"),
            P("row", ("seq", "pat"), None),
            P(),
            P(),
            P(),
            P(),
            P(),
            P(),
            P(),
            P(),
            P(None, "pat"),
            P("pat", None),
        ),
        check_vma=False,
    )
```

```python
import functools

import jax
import jax.numpy as jnp
from jax import lax
from jax.experimental import pallas as pl
from jax.experimental.pallas import tpu as pltpu
from jax.sharding import PartitionSpec as P

D = 768
HEADS = 12
HDIM = 64

epsilon = 1e-05
masked_low = -1e30
segment_parts = (1, 2, 4, 8, 16)
dilations = (1, 2, 4, 6, 12)
DOCS = 3
FEATS = 128
TILE = 256
VMEM_LIMIT = 60 * 1024 * 1024
SMALL_LIMIT = 20 * 1024 * 1024
COPIES = 64
f32 = jnp.float32
bf16 = jnp.bfloat16


def dot(a, b):
    return lax.dot_general(a, b, (((1,), (0,)), ((), ())), preferred_element_type=f32)


def dot_nt(a, b):
    return lax.dot_general(a, b, (((1,), (1,)), ((), ())), preferred_element_type=f32)


def dot_tn(a, b):
    return lax.dot_general(a, b, (((0,), (0,)), ((), ())), preferred_element_type=f32)


class Staged:
    def __init__(self, outside, inside, sems, free):
        self.outside, self.inside, self.sems, self.free = outside, inside, sems, free
        self.pending = []

    def start(self, source=None, target=None):
        copy = pltpu.make_async_copy(
            self.outside if source is None else source,
            self.inside if target is None else target,
            self.sems.at[next(self.free)],
        )
        copy.start()
        self.pending.append(copy)

    def get(self):
        for copy in self.pending:
            copy.wait()
        self.pending = []
        return self.inside

    def put(self, source, target):
        copy = pltpu.make_async_copy(source, target, self.sems.at[next(self.free)])
        copy.start()
        self.pending.append(copy)

    def send(self, at=...):
        copy = pltpu.make_async_copy(
            self.inside.at[at], self.outside.at[at], self.sems.at[next(self.free)]
        )
        copy.start()
        self.pending.append(copy)


def staged_call(body, scalars, arrays, outs, scratch=(), windows=None, limit=VMEM_LIMIT, late=0, aliases=(), bare=(), flops=0):
    windows = windows or {}
    n_scalar, n_in, n_out = len(scalars), len(arrays), len(outs)

    def kernel(*refs):
        scalar_refs, refs = refs[:n_scalar], refs[n_scalar:]
        outside, refs = refs[: n_in + n_out], refs[n_in + n_out :]
        inside, refs = refs[: n_in + n_out], refs[n_in + n_out :]
        sems, rest = refs[0], refs[1:]
        free = iter(range(COPIES))
        every = [Staged(o, i, sems, free) for o, i in zip(outside, inside, strict=True)]
        ins, results = every[:n_in], every[n_in:]
        for at, one in enumerate(ins[: n_in - late]):
            if at in windows:
                start = windows[at](scalar_refs)
                size = one.inside.shape[-1]
                one.start(one.outside.at[:, pl.ds(pl.multiple_of(start, 128), size)])
            else:
                one.start()
        body(scalar_refs, ins, results, rest)
        for one in ins + results:
            one.get()

    def buffer(at, array):
        dims = array.shape
        if at >= n_in - late:
            return pltpu.VMEM((16, 128), array.dtype)
        if at in windows:
            dims = (*dims[:-1], 256)
        return pltpu.VMEM(dims, array.dtype)

    return pl.pallas_call(
        kernel,
        out_shape=tuple(outs),
        in_specs=[pl.BlockSpec(memory_space=pltpu.SMEM)] * n_scalar
        + [pl.BlockSpec(memory_space=pl.ANY)] * n_in,
        out_specs=(pl.BlockSpec(memory_space=pltpu.HBM),) * n_out,
        scratch_shapes=[buffer(at, a) for at, a in enumerate(arrays)]
        + [
            pltpu.VMEM((16, 128) if at in bare else o.shape, o.dtype)
            for at, o in enumerate(outs)
        ]
        + [pltpu.SemaphoreType.DMA((COPIES,))]
        + list(scratch),
        input_output_aliases={n_scalar + a: o for a, o in aliases},
        compiler_params=pltpu.CompilerParams(vmem_limit_bytes=limit),
        cost_estimate=pl.CostEstimate(flops=flops, bytes_accessed=0, transcendentals=0),
    )(*scalars, *arrays)


def normalise(values):
    center = values - jnp.mean(values, axis=-1, keepdims=True)
    scale = lax.rsqrt(jnp.mean(center * center, axis=-1, keepdims=True) + epsilon)
    return center * scale, scale


def norm_backward(hat, scale, grad):
    return scale * (
        grad
        - jnp.mean(grad, axis=-1, keepdims=True)
        - hat * jnp.mean(grad * hat, axis=-1, keepdims=True)
    )


def make_features(heads, part, docs, feats):
    _, length, _ = feats.inside.shape
    position = lax.broadcasted_iota(jnp.int32, (1, length), 1)
    feature = lax.broadcasted_iota(jnp.int32, (FEATS, length), 0)
    for h in range(heads):
        head = part * heads + h
        hit = None
        base = 0
        for size, dilation in zip(segment_parts, dilations, strict=True):
            seg_width = length * size // 16
            inside = lax.rem(
                lax.rem(position, seg_width) + dilation - lax.rem(head, dilation), dilation
            )
            key = base + lax.div(position, seg_width) * DOCS + docs
            key = jnp.where(inside == 0, key, -1)
            found = feature == key
            hit = found if hit is None else hit | found
            base += DOCS * (16 // size)
        feats.inside[h] = jnp.where(hit, 1.0, 0.0).T.astype(bf16)
        feats.send(h)


def project_kernel(parts, pair, scalars, ins, outs, scratch):
    x, docs, gain, bias, *weights = ins[:7]
    normed, q, kv, own, feats = outs[:5]
    width = D // parts
    where = scalars[0]
    own.inside[:, 3 * width :] = jnp.zeros((D, D - 3 * width), bf16)
    gain = gain.get()[...].reshape(1, D)
    bias = bias.get()[...].reshape(1, D)
    x.get()
    span = x.inside.shape[0]
    for start in range(0, span, TILE):
        rows = slice(start, start + TILE)
        hat, _ = normalise(x.inside[rows, :].astype(f32))
        normed.inside[rows, :] = (hat * gain + bias).astype(bf16)
    normed.send()
    for w in weights:
        w.get()
    for odd in range(2):

        @pl.when(where[0] % 2 == odd)
        def _():
            for at, w in enumerate(weights):
                own.inside[:, at * width : (at + 1) * width] = w.inside[
                    :, odd * 64 : odd * 64 + width
                ]

    own.send()
    for start in range(0, span, TILE):
        rows = slice(start, start + TILE)
        made = dot(normed.inside[rows, :], own.inside[:, : 3 * width]).astype(bf16)
        q.inside[rows, :] = (made[:, :width].astype(f32) * HDIM**-0.5).astype(bf16)
        kv.inside[rows, :] = made[:, width:]
    kv.send()
    q.send()
    if pair:
        x_far = ins[7].get()

        @pl.when(scalars[1][0] > 0)
        def _():
            for start in range(0, span, TILE):
                rows = slice(start, start + TILE)
                hat, _ = normalise(x_far[rows, :].astype(f32))
                low = (hat * gain + bias).astype(bf16)
                outs[5].inside[rows, :] = dot(low, own.inside[:, width : 3 * width]).astype(bf16)

        outs[5].send()
    make_features(feats.inside.shape[0], where[0], docs.get()[...], feats)


def head_mask(heads, width):
    lane = lax.broadcasted_iota(jnp.int32, (1, width), 1)
    return [((lane >= h * HDIM) & (lane < (h + 1) * HDIM)).astype(bf16) for h in range(heads)]


def attention_kernel(heads, span, scalars, ins, outs, scratch):
    where = scalars[0]
    q, kv, feats, kv_far = (one.get() for one in ins)
    mixed_low, mixed_t, lse = (one.inside for one in outs)
    q_head, k, v_t, kf, vf_t, tops, totals = scratch
    width = heads * HDIM
    masks = head_mask(heads, width)
    for h in range(heads):
        q_head[h] = q[...] * masks[h]
    k[...] = kv[:, :width]
    v_t[...] = kv[:, width:].T
    far = kv_far.shape[0] // span

    def turn(j, _):
        rows = pl.ds(pl.multiple_of(j * span, span), span)
        kf[rows, :] = kv_far[rows, :width]
        vf_t[j] = kv_far[rows, width:].T
        return 0

    mine = where[0]
    lax.fori_loop(0, jnp.minimum(mine, far), turn, 0)
    own_start = pl.multiple_of(mine * span, span)
    lse[...] = jnp.zeros(lse.shape, f32)
    pairs = [(start, h) for start in range(0, span, TILE) for h in range(heads)]

    def part(start, h, k_rows, f_rows, v_rows, causal):
        counts = dot_nt(f_rows, feats[h, pl.ds(own_start + start, TILE), :])
        if causal:
            at_k = lax.broadcasted_iota(jnp.int32, counts.shape, 0)
            at_q = lax.broadcasted_iota(jnp.int32, counts.shape, 1) + start
            counts = jnp.where(at_k <= at_q, counts, 0.0)
        scores = dot_nt(k_rows, q_head[h, start : start + TILE, :])
        scores = jnp.where(counts > 0, scores, masked_low)
        return counts, scores, v_rows

    for at, (start, h) in enumerate(pairs):
        size = start + TILE
        head_rows = slice(h * HDIM, (h + 1) * HDIM)
        counts, scores, v_rows = part(
            start,
            h,
            k[:size, :],
            feats[h, pl.ds(own_start, size), :],
            v_t[head_rows, :size],
            True,
        )
        top = jnp.max(scores, axis=0, keepdims=True)
        weights = counts * jnp.exp(scores - top)
        tops[at : at + 1, :] = top
        totals[at : at + 1, :] = jnp.sum(weights, axis=0, keepdims=True)
        mixed_t[head_rows, start : start + TILE] = dot(v_rows, weights.astype(bf16))

    def far_step(j, _):
        rows = pl.ds(pl.multiple_of(j * span, span), span)
        for at, (start, h) in enumerate(pairs):
            head_rows = slice(h * HDIM, (h + 1) * HDIM)
            counts, scores, v_rows = part(
                start, h, kf[rows, :], feats[h, rows, :], vf_t[j, head_rows, :], False
            )
            top = tops[at : at + 1, :]
            new_top = jnp.maximum(top, jnp.max(scores, axis=0, keepdims=True))
            weights = counts * jnp.exp(scores - new_top)
            factor = jnp.exp(top - new_top)
            tops[at : at + 1, :] = new_top
            totals[at : at + 1, :] = totals[at : at + 1, :] * factor + jnp.sum(
                weights, axis=0, keepdims=True
            )
            mixed_t[head_rows, start : start + TILE] = mixed_t[
                head_rows, start : start + TILE
            ] * factor + dot(v_rows, weights.astype(bf16))
        return 0

    lax.fori_loop(0, mine, far_step, 0)
    for at, (start, h) in enumerate(pairs):
        head_rows = slice(h * HDIM, (h + 1) * HDIM)
        total = totals[at : at + 1, :]
        done = mixed_t[head_rows, start : start + TILE] / total
        mixed_t[head_rows, start : start + TILE] = done
        mixed_low[head_rows, start : start + TILE] = done.astype(bf16)
        lse[h : h + 1, start : start + TILE] = tops[at : at + 1, :] + jnp.log(total)
    for one in outs:
        one.send()


def count_rows(f_rows, f_tile, low_from):
    counts = dot_nt(f_rows, f_tile)
    if low_from is not None:
        at_k = lax.broadcasted_iota(jnp.int32, counts.shape, 0)
        at_q = lax.broadcasted_iota(jnp.int32, counts.shape, 1) + low_from
        counts = jnp.where(at_k <= at_q, counts, 0.0)
    return counts


def attention_back_kernel(heads, span, scalars, ins, outs, scratch):
    where = scalars[0]
    parts, q, mixed_t, lse, kv, feats, kv_far = (one.get() for one in ins)
    grad_q, grad_kv, grad_far = (one.inside for one in outs)
    q_head, g_head, dots, probs, slopes, k, v, k_t, gq_t = scratch
    width = heads * HDIM
    masks = head_mask(heads, width)
    mine = where[0]
    far = kv_far.shape[0] // span
    total = parts[0].astype(f32)
    for part in range(1, parts.shape[0]):
        total = total + parts[part].astype(f32)
    low_t = total.astype(bf16)
    low = low_t.T
    for h in range(heads):
        q_head[h] = q[...] * masks[h]
        g_head[h] = low * masks[h]
    product = low_t.astype(f32) * mixed_t[...]
    for h in range(heads):
        dots[h : h + 1, :] = jnp.sum(product[h * HDIM : (h + 1) * HDIM], axis=0, keepdims=True)
    own_start = pl.multiple_of(mine * span, span)

    def block(h, start, size, rows, diagonal):
        tile = slice(start, start + TILE)
        columns = slice(h * span + start, h * span + start + TILE)
        f_rows = feats[h, pl.ds(own_start, size) if diagonal else rows, :]
        f_tile = feats[h, pl.ds(own_start + start, TILE), :]
        counts = count_rows(f_rows, f_tile, start if diagonal else None)
        scores = jnp.where(counts > 0, dot_nt(k[:size, :], q_head[h, tile, :]), masked_low)
        prob = counts * jnp.exp(scores - lse[h : h + 1, tile])
        grad_prob = dot_nt(v[:size, :], g_head[h, tile, :])
        slope = prob * (grad_prob - dots[h : h + 1, tile])
        probs[:size, columns] = prob.astype(bf16)
        slopes[:size, columns] = slope.astype(bf16)
        if size < span:
            probs[size:, columns] = jnp.zeros((span - size, TILE), bf16)
            slopes[size:, columns] = jnp.zeros((span - size, TILE), bf16)

    def finish():
        k_t[...] = k[...].T
        grad_v_rows = dot(probs[...], g_head[...].reshape(heads * span, width))
        grad_k_rows = dot(slopes[...], q_head[...].reshape(heads * span, width))
        terms = [
            dot(k_t[h * HDIM : (h + 1) * HDIM, :], slopes[:, h * span : (h + 1) * span])
            for h in range(heads)
        ]
        return grad_k_rows, grad_v_rows, terms

    k[...] = kv[:, :width]
    v[...] = kv[:, width:]
    for start in range(0, span, TILE):
        for h in range(heads):
            size = start + TILE
            block(h, start, size, None, True)
    grad_k_rows, grad_v_rows, terms = finish()
    grad_kv[:, :width] = grad_k_rows
    grad_kv[:, width:] = grad_v_rows
    outs[1].send()
    for h in range(heads):
        gq_t[h * HDIM : (h + 1) * HDIM, :] = terms[h]

    def far_block(j, _):
        rows = pl.ds(pl.multiple_of(j * span, span), span)
        k[...] = kv_far[rows, :width]
        v[...] = kv_far[rows, width:]
        for start in range(0, span, TILE):
            for h in range(heads):
                block(h, start, span, rows, False)
        grad_k_rows, grad_v_rows, terms = finish()
        grad_far[rows, :width] = grad_k_rows.astype(bf16)
        grad_far[rows, width:] = grad_v_rows.astype(bf16)
        for h in range(heads):
            gq_t[h * HDIM : (h + 1) * HDIM, :] += terms[h]
        return 0

    used = jnp.minimum(mine, far)
    lax.fori_loop(0, used, far_block, 0)

    def clear(j, _):
        grad_far[pl.ds(pl.multiple_of(j * span, span), span), :] = jnp.zeros((span, 2 * width), bf16)
        return 0

    lax.fori_loop(used, far, clear, 0)
    outs[2].send()
    grad_q[...] = (gq_t[...] * HDIM**-0.5).T.astype(bf16)
    outs[0].send()


def middle_kernel(scalars, ins, outs, scratch):
    mixed4, x, w_out, gain, bias, w_up, w_down, *c_parts = ins
    gm, sums, act, gh, branch, low, c, resids = outs
    (c4,) = scratch
    parts, width, span = mixed4.inside.shape
    for step, one in enumerate(c_parts):
        one.start(target=c4.at[scalars[0][0] ^ step])
    mixed_t = mixed4.get()[...].reshape(D, span)
    x.get(), w_out.get()
    gain = gain.get()[...].reshape(1, D)
    bias = bias.get()[...].reshape(1, D)
    gain_sum = jnp.zeros((1, D), f32)
    bias_sum = jnp.zeros((1, D), f32)
    for start in range(0, span, span):
        rows = slice(start, start + span)
        resid = x.inside[rows, :].astype(f32) + dot_tn(mixed_t[:, rows], w_out.inside[...])
        resids.inside[rows, :] = resid.astype(bf16)
        hat, scale = normalise(resid)
        normed = (hat * gain + bias).astype(bf16)
        low.inside[rows, :] = normed
        w_up.get()
        hidden = dot(normed, w_up.inside[...])
        bell = 0.5 + 0.5 * lax.erf(hidden * (0.5**0.5))
        act.inside[rows, :] = (hidden * bell).astype(bf16)
        slope = bell + hidden * jnp.exp(-0.5 * hidden * hidden) * 0.3989422804014327
        if start == 0:
            w_down.get()
            for one in c_parts:
                one.get()
            for part in range(parts):
                c.inside[:, part * width : (part + 1) * width] = c4[part].T
            c.send()
        c_rows = c.inside[rows, :]
        grad_hidden = (slope * dot_nt(c_rows, w_down.inside[...])).astype(bf16)
        gh.inside[rows, :] = grad_hidden
        grad_normed = dot_nt(grad_hidden, w_up.inside[...])
        gain_sum = gain_sum + jnp.sum(grad_normed * hat, axis=0, keepdims=True)
        bias_sum = bias_sum + jnp.sum(grad_normed, axis=0, keepdims=True)
        grad_resid = norm_backward(hat, scale, grad_normed * gain) + c_rows.astype(f32) * (
            1.0 / parts
        )
        grad_low = grad_resid.astype(bf16)
        branch.inside[rows, :] = grad_low
        for one in (act, low, gh, resids, branch):
            one.send(pl.ds(start, span))
        for part in range(parts):
            gm.inside[part, :, rows] = dot_nt(
                w_out.inside[part * width : (part + 1) * width, :], grad_low
            ).astype(bf16)
            gm.send(part)
    sums.inside[0:1, :] = gain_sum
    sums.inside[1:2, :] = bias_sum
    sums.send()


def weights_kernel(pair, scalars, ins, outs, scratch):
    act, c, low, gh, mixed4, branch, w_down, resids = ins
    ffn, *wide = outs
    (made,) = scratch
    parts, width, span = mixed4.inside.shape
    chunk = span // parts
    where = scalars[0]

    def out_product():
        mixed_t = mixed4.get()[...].reshape(D, span)
        return dot(mixed_t, branch.get()[...])

    products = (
        lambda: dot_tn(act.get()[...], c.get()[...]),
        lambda: dot_tn(low.get()[...], gh.get()[...]),
        out_product,
    )
    for at, product in enumerate(products):
        if not pair:
            wide[0].inside[at] = product().astype(bf16)
            continue
        made[...] = product().astype(bf16)
        rows_count = wide[0].inside.shape[1]
        size = D // (2 * rows_count)
        for row in range(rows_count):
            for out, half in ((wide[0].inside.at[at], where[0]), (wide[1 + at].inside, 1 - where[0])):
                start = pl.multiple_of((2 * row + half) * size, size)
                out[row] = made[pl.ds(start, size), :]
        wide[1 + at].send()
        wide[0].send(at)
    if not pair:
        wide[0].send()
    w_down.get(), resids.get()
    for start in range(0, span, TILE):
        rows = slice(start, start + TILE)
        out = dot(act.inside[rows, :], w_down.inside[...]) + resids.inside[rows, :].astype(f32) * (
            1.0 / parts
        )
        out_t = out.astype(bf16).T
        for part in range(parts):
            for at in range(start, start + TILE, chunk):
                ffn.inside[part, at // chunk * width : (at // chunk + 1) * width, :] = out_t[
                    part * width : (part + 1) * width, at - start : at - start + chunk
                ]
    ffn.send()


def add_kernel(scalars, ins, outs, scratch):
    keep, *more = ins
    keep.get()
    for group, one in enumerate(more):
        one.get()
        for at, out in enumerate(outs):
            block = scalars[0][0] ^ at
            out.inside[group] = (
                keep.inside[group, block].astype(f32) + one.inside[block].astype(f32)
            ).astype(bf16)
        for out in outs[1:] + outs[:1]:
            out.send(group)


def row_sum_kernel(parts, scalars, ins, outs, scratch):
    ffn_own, out_parts = outs
    (rows,) = scratch
    total = ins[0].get()[...].astype(f32)
    for one in ins[1:]:
        total = total + one.get()[...].astype(f32)
    total = total.astype(bf16)
    size = total.shape[1]
    half = size // 2
    width = D // parts
    for part in range(parts):
        columns = slice(part * width, (part + 1) * width)
        out_parts.inside[part, :, :width] = total[2, :half, columns]
        out_parts.inside[part, :, width:] = total[2, half:, columns]
    out_parts.send()
    rows[...] = total[:2].reshape(2 * size, D)
    for row in range(ffn_own.outside.shape[0]):
        ffn_own.put(rows, ffn_own.outside.at[row])


SLOT = 64


def last_kernel(parts, pair, scalars, ins, outs, scratch):
    gq, gkv, gkv_more, normed, own, x, gain, gr, sums = ins
    back, *narrow = outs
    grads, small, made = scratch
    width = D // parts
    span = x.inside.shape[0]
    piece = span // parts
    lanes = 3 * width + SLOT
    grads[:, 3 * width :] = jnp.zeros((span, D - 3 * width), bf16)
    grads[:, :width] = gq.get()[...]
    gkv.get(), gkv_more.get()
    grads[:, width : 3 * width] = (
        gkv.inside[...] + gkv_more.inside[...].astype(f32)
    ).astype(bf16)
    made[...] = dot_tn(normed.get()[...], grads[:, :lanes]).astype(bf16)
    if pair:
        rows_count, size, _ = narrow[1].inside.shape
        halves = (
            (narrow[0].inside.at[0], scalars[0][0]),
            (narrow[1].inside, 1 - scalars[0][0]),
        )
        for row in range(rows_count):
            for out, half in halves:
                start = pl.multiple_of((2 * row + half) * size, size)
                out[row] = made[pl.ds(start, size), :]
    else:
        narrow[0].inside[...] = made[...]
    own.get(), x.get(), gr.get(), sums.get()
    gain = gain.get()[...].reshape(1, D)
    gain_sum = jnp.zeros((1, D), f32)
    bias_sum = jnp.zeros((1, D), f32)
    for start in range(0, span, TILE):
        rows = slice(start, start + TILE)
        hat, scale = normalise(x.inside[rows, :].astype(f32))
        grad_normed = dot_nt(grads[rows, :], own.inside[...])
        gain_sum = gain_sum + jnp.sum(grad_normed * hat, axis=0, keepdims=True)
        bias_sum = bias_sum + jnp.sum(grad_normed, axis=0, keepdims=True)
        grad_in = gr.inside[rows, :].astype(f32) + norm_backward(hat, scale, grad_normed * gain)
        turned = grad_in.astype(bf16).T
        for at in range(start, start + TILE, piece):
            back.inside[at // piece] = turned[:, at - start : at - start + piece]
            back.send(at // piece)
    pieces = D // SLOT
    for at, row in enumerate(
        (gain_sum, bias_sum, sums.inside[0:1, :], sums.inside[1:2, :])
    ):
        for part in range(pieces):
            small[at * pieces + part : at * pieces + part + 1, :] = row[
                :, part * SLOT : (part + 1) * SLOT
            ]
    tail = small[...].astype(bf16)
    if pair:
        for row in range(rows_count):
            for out, _ in halves:
                out[row, :48, 3 * width :] = tail
        narrow[1].send()
        narrow[0].send()
    else:
        narrow[0].inside[:48, 3 * width :] = tail
        narrow[0].send()


def own_sum_kernel(parts, count, scalars, ins, outs, scratch):
    mine = outs[0].inside
    (small,) = scratch
    width = D // parts
    size = ins[0].inside.shape[1]
    half = size // 2
    out = ins[count].get()[0].astype(f32)
    for part in range(1, parts):
        out = out + ins[count].inside[part].astype(f32)
    mine[:half, 3 * width :] = out[:, :width].astype(bf16)
    mine[half:size, 3 * width :] = out[:, width:].astype(bf16)
    total = ins[0].get()[0].astype(f32)
    for one in ins[1:count]:
        total = total + one.get()[0].astype(f32)
    mine[:size, : 3 * width] = total[:, : 3 * width].astype(bf16)
    pieces = D // SLOT
    small[...] = jnp.zeros(small.shape, f32)
    for at in range(4):
        for part in range(pieces):
            row = at * pieces + part
            small[at : at + 1, part * SLOT : (part + 1) * SLOT] = total[
                row : row + 1, 3 * width :
            ]
    mine[size:, :] = small[...].astype(bf16)
    outs[0].send()


def output_kernel(scalars, ins, outs, scratch):
    got = ins[0].get()
    parts, _, piece = got.shape
    width = D // parts
    total = got[0, :D].astype(f32)
    for part in range(1, parts):
        total = total + got[part, :D].astype(f32)
    for at in range(parts):
        outs[0].inside[:, at * piece : (at + 1) * piece] = total[
            at * width : (at + 1) * width
        ].astype(bf16)
    outs[0].send()


def finish_kernel(scalars, ins, outs, scratch):
    grad_in, *vectors = outs
    (small,) = scratch
    size = ins[1].outside.shape[1] - 16
    ins[1].start(source=ins[1].outside.at[:, pl.ds(size, 16), :], target=small)
    back = ins[0].get()
    total = back[0].astype(f32)
    for at in range(1, back.shape[0]):
        total = total + back[at].astype(f32)
    grad_in.inside[...] = total.T.astype(bf16)
    grad_in.send()
    ins[1].get()
    sums = small[0].astype(f32)
    for at in range(1, small.shape[0]):
        sums = sums + small[at].astype(f32)
    for at, vector in enumerate(vectors):
        vector.inside[...] = sums[at]
        vector.send()


def spread_kernel(steps, scalars, ins, outs, scratch):
    (buffer,) = scratch
    row, seq = scalars
    size = buffer.shape[2]
    at = 0
    for step, (row_step, seq_step, count) in enumerate(steps):
        part = 0
        for one in ins[at : at + count]:
            got = one.get()
            for own in range(got.shape[0]):
                width = D // (got.shape[0] * count)
                columns = slice(part * width, (part + 1) * width)
                for grad in range(4):
                    buffer[grad, step, :, columns] = got[
                        own, :, grad * width : (grad + 1) * width
                    ].astype(f32)
                part += 1
        at += count
        start = pl.multiple_of((2 * (row[0] ^ row_step) + (seq[0] ^ seq_step)) * size, size)
        for grad in range(4):
            out = outs[grad]
            out.put(buffer.at[grad, step], out.outside.at[pl.ds(start, size), :])


def spread(row_here, here, steps, earlier=(), flops=0):
    count = sum(len(blocks) for _, _, blocks in steps)
    size = steps[0][2][0].shape[1]
    received = [block for _, _, blocks in steps for block in blocks]
    return staged_call(
        functools.partial(spread_kernel, [(a, b, len(c)) for a, b, c in steps]),
        [row_here, here],
        [*received, *earlier],
        (shape(D, D, kind=f32),) * 4,
        scratch=[pltpu.VMEM((4, len(steps), size, D), f32)],
        limit=SMALL_LIMIT,
        late=len(earlier),
        aliases=tuple((count + at, at) for at in range(len(earlier))),
        bare=range(4),
        flops=flops,
    )


def spread_ffn_kernel(scalars, ins, outs, scratch):
    (buffer,) = scratch
    size = buffer.shape[2]
    for half, one in enumerate(ins):
        got = one.get()
        for row in range(got.shape[0]):
            start = pl.multiple_of((2 * row + (scalars[0][0] ^ half)) * size, size)
            for grad, out in enumerate(outs):
                place = buffer.at[grad, half * got.shape[0] + row]
                place[...] = got[row, grad * size : (grad + 1) * size, :].astype(f32)
                out.put(place, out.outside.at[pl.ds(start, size), :])


def first_spread_kernel(steps, scalars, ins, outs, scratch):
    spread_ffn_kernel(scalars[1:], ins[:2], outs[:2], scratch[:1])
    spread_kernel(steps, scalars, ins[2:], outs[2:], scratch[1:])


def broadcast_exchange(value, axis):
    count = lax.axis_size(axis)
    return lax.all_to_all(
        jnp.broadcast_to(value[None], (count,) + value.shape), axis, 0, 0, tiled=False
    )


def swap(value):
    return lax.ppermute(value, "seq", [(0, 1), (1, 0)])


def trade(value, axis, step):
    return lax.ppermute(value, axis, [(a, a ^ step) for a in range(lax.axis_size(axis))])


def shape(*dims, kind=bf16):
    return jax.ShapeDtypeStruct(dims, kind)


def per_device(
    block_input,
    doc_ids,
    ln1_gain,
    ln1_bias,
    w_query,
    w_key,
    w_value,
    w_out,
    ln2_gain,
    ln2_bias,
    w_up,
    w_down,
    cotangent,
):
    span = block_input.shape[1]
    rows_count = lax.axis_size("row")
    seq_count = lax.axis_size("seq")
    parts = lax.axis_size("pat")
    row_index = lax.axis_index("row")
    seq_index = lax.axis_index("seq")
    pat_index = lax.axis_index("pat")
    pair = seq_count == 2
    heads = HEADS // parts
    width = D // parts
    quarter = span // parts
    size = D // (rows_count * seq_count) if pair else D
    here = seq_index.astype(jnp.int32)[None]
    row_here = row_index.astype(jnp.int32)[None]
    part_here = pat_index.astype(jnp.int32)[None]
    x = block_input[0]

    c_own = cotangent[0].T
    c_parts = [c_own] + [trade(c_own, "pat", s) for s in range(1, parts)]
    def window(scalars):
        return scalars[0][0] * width // 128 * 128

    far_shapes = (shape(span, 2 * width),) if pair else ()
    normed, q, kv, own, feats, *far = staged_call(
        functools.partial(project_kernel, parts, pair),
        [part_here, here],
        [x, doc_ids, ln1_gain, ln1_bias, w_query, w_key, w_value] + ([swap(x)] if pair else []),
        (
            shape(span, D),
            shape(span, width),
            shape(span, 2 * width),
            shape(D, D),
            shape(heads, doc_ids.shape[1], FEATS),
            *far_shapes,
        ),
        windows={4: window, 5: window, 6: window},
        flops=1 << 42,
    )

    kv_far = far[0] if pair else lax.all_gather(kv, "seq", axis=0, tiled=True)
    far_rows = kv_far.shape[0]

    mixed, mixed_t, lse = staged_call(
        functools.partial(attention_kernel, heads, span),
        [here],
        [q, kv, feats, kv_far],
        (shape(width, span), shape(width, span, kind=f32), shape(8, span, kind=f32)),
        scratch=[
            pltpu.VMEM((heads, span, width), bf16),
            pltpu.VMEM((span, width), bf16),
            pltpu.VMEM((width, span), bf16),
            pltpu.VMEM((far_rows, width), bf16),
            pltpu.VMEM((far_rows // span, width, span), bf16),
            pltpu.VMEM((heads * span // TILE + 8, TILE), f32),
            pltpu.VMEM((heads * span // TILE + 8, TILE), f32),
        ],
    )
    mixed, *c_parts = lax.optimization_barrier((mixed, *c_parts))
    mixed4 = lax.all_gather(mixed, "pat")

    wide_shapes = (shape(3, D, D),)
    if pair:
        wide_shapes = (shape(3, rows_count, size, D),) + (shape(rows_count, size, D),) * 3
    gm, sums, act, gh, branch, low, c, resids = staged_call(
        middle_kernel,
        [part_here],
        [mixed4, x, w_out, ln2_gain, ln2_bias, w_up, w_down, *c_parts],
        (shape(parts, width, span), shape(8, D, kind=f32)) + (shape(span, D),) * 6,
        scratch=[pltpu.VMEM((parts, width, span), bf16)],
        late=parts,
    )
    gm_parts = lax.all_to_all(gm, "pat", 0, 0, tiled=True)
    ffn, *wide = staged_call(
        functools.partial(weights_kernel, pair),
        [here],
        [act, c, low, gh, mixed4, branch, w_down, resids],
        (shape(parts, parts * width, quarter), *wide_shapes),
        scratch=[pltpu.VMEM((D, D), bf16)],
        flops=1 << 42,
    )

    if pair:
        keep, *sends = wide
        ordered = staged_call(
            add_kernel,
            [row_here],
            [keep, *[swap(send) for send in sends]],
            (shape(3, size, D),) * rows_count,
            limit=63 << 20,
        )
        wide_parts = [ordered[0]] + [trade(ordered[s], "row", s) for s in range(1, rows_count)]

    ffn, _ = lax.optimization_barrier((ffn, gm_parts))
    ffn_parts = lax.all_to_all(ffn, "pat", 0, 0, tiled=True)
    (out_t,) = staged_call(
        output_kernel,
        [],
        [ffn_parts],
        (shape(width, span),),
        limit=SMALL_LIMIT,
        flops=1 << 42,
    )
    gq, gkv, gkv_far = staged_call(
        functools.partial(attention_back_kernel, heads, span),
        [here],
        [gm_parts, q, mixed_t, lse, kv, feats, kv_far],
        (
            shape(span, width),
            shape(span, 2 * width, kind=f32),
            shape(far_rows, 2 * width),
        ),
        scratch=[
            pltpu.VMEM((heads, span, width), bf16),
            pltpu.VMEM((heads, span, width), bf16),
            pltpu.VMEM((8, span), f32),
            pltpu.VMEM((span, heads * span), bf16),
            pltpu.VMEM((span, heads * span), bf16),
            pltpu.VMEM((span, width), bf16),
            pltpu.VMEM((span, width), bf16),
            pltpu.VMEM((width, span), bf16),
            pltpu.VMEM((width, span), f32),
        ],
        flops=1 << 42,
    )

    if pair:
        gkv_more = swap(gkv_far)
        ffn_own, out_parts = staged_call(
            functools.partial(row_sum_kernel, parts),
            [],
            wide_parts,
            (shape(rows_count, 2 * size, D), shape(parts, size // 2, 2 * width)),
            scratch=[pltpu.VMEM((2 * size, D), bf16)],
            limit=SMALL_LIMIT,
            bare=(0,),
        )
        out_parts, _ = lax.optimization_barrier((out_parts, ffn_parts))
        out_parts = lax.all_to_all(out_parts, "pat", 0, 0, tiled=True)
    else:
        gkv_more = lax.psum_scatter(gkv_far, "seq", scatter_dimension=0, tiled=True)

    lanes = 3 * width + SLOT
    narrow_shapes = (shape(1, rows_count, size, lanes), shape(rows_count, size, lanes)) if pair else (shape(D, lanes),)
    back, *narrow = staged_call(
        functools.partial(last_kernel, parts, pair),
        [here],
        [gq, gkv, gkv_more, normed, own, x, ln1_gain, branch, sums],
        (shape(parts, parts * width, quarter), *narrow_shapes),
        scratch=[
            pltpu.VMEM((span, D), bf16),
            pltpu.VMEM((48, SLOT), f32),
            pltpu.VMEM((D, lanes), bf16),
        ],
    )

    if pair:
        keep, send = narrow
        send, *_ = lax.optimization_barrier((send, *wide_parts[1:]))
        keep, _ = lax.optimization_barrier((keep, ffn_own))
        ordered = staged_call(
            add_kernel, [row_here], [keep, swap(send)], (shape(1, size, lanes),) * rows_count,
            limit=65000 << 10,
        )
        received = [ordered[0]] + [trade(ordered[s], "row", s) for s in range(1, rows_count)]
        received[3], _ = lax.optimization_barrier((received[3], out_t))
        (mine,) = staged_call(
            functools.partial(own_sum_kernel, parts, rows_count),
            [],
            [*received, out_parts],
            (shape(size + 16, D),),
            scratch=[pltpu.VMEM((16, D), f32)],
            limit=SMALL_LIMIT,
        )
        gathered = lax.all_gather(mine, "pat")
        ffn_own, *_ = lax.optimization_barrier(
            (ffn_own, out_parts, *received[1:])
        )
        ffn_mine = lax.all_to_all(ffn_own, "row", 0, 0, tiled=True)
        gathered, ffn_mine, back = lax.optimization_barrier((gathered, ffn_mine, back))
        back_parts = lax.all_to_all(back, "pat", 0, 0, tiled=True)
        own = gathered[:, :size]
        near1, near2 = trade(own, "row", 1), trade(own, "row", 2)
        half1, half2 = near1[: parts // 2], near2[parts // 2 :]
        far = (trade(half1, "row", 2), trade(half2, "row", 1))
        sent1, _ = lax.optimization_barrier((near1, half1))
        sent2, _ = lax.optimization_barrier((near2, half2))
        steps = [(0, 0, 1), (1, 0, 1), (2, 0, 1), (0, 1, 1), (1, 1, 1), (2, 1, 1)]
        grad_down, grad_up, *grads = staged_call(
            functools.partial(first_spread_kernel, steps),
            [row_here, here],
            [
                ffn_mine,
                swap(ffn_mine),
                own,
                near1,
                near2,
                swap(own),
                swap(sent1),
                swap(sent2),
            ],
            (shape(D, D, kind=f32),) * 6,
            scratch=[
                pltpu.VMEM((2, 2 * rows_count, size, D), f32),
                pltpu.VMEM((4, len(steps), size, D), f32),
            ],
            limit=24 << 20,
            bare=range(6),
        )
        sent = lax.optimization_barrier((*far, grads[0]))[:2]
        grads = spread(
            row_here,
            here,
            [(3, 0, far), (3, 1, tuple(swap(value) for value in sent))],
            grads,
        )
    else:
        axes = ("row", "seq")
        back_parts = lax.all_to_all(back, "pat", 0, 0, tiled=True)
        wide_sum = lax.psum(wide[0], axes)
        grad_down, grad_up = wide_sum[0].astype(f32), wide_sum[1].astype(f32)
        grad_out = lax.psum(wide_sum[2], "pat").astype(f32)
        gathered = lax.all_gather(lax.psum(narrow[0], axes), "pat")
        small = gathered[:, :48, 3 * width :].reshape(parts, 4, D)
        small = jnp.pad(small, ((0, 0), (0, 12), (0, 0)))
        grads = [
            gathered[:, :, at * width : (at + 1) * width]
            .astype(f32)
            .transpose(1, 0, 2)
            .reshape(D, D)
            for at in range(3)
        ] + [grad_out]
    if pair:
        back_parts, _ = lax.optimization_barrier((back_parts, grads[0]))
    grad_in, *vectors = staged_call(
        finish_kernel,
        [],
        [back_parts, gathered if pair else small],
        (shape(quarter, D),) + (shape(D, kind=f32),) * 4,
        scratch=[pltpu.VMEM((parts, 16, D), bf16)],
        limit=SMALL_LIMIT,
        late=1,
    )
    return (
        out_t.T[None],
        grad_in[None],
        vectors[0],
        vectors[1],
        grads[0],
        grads[1],
        grads[2],
        grads[3],
        vectors[2],
        vectors[3],
        grad_up,
        grad_down,
    )


def solution(mesh):
    placed = (
        P("row", "seq", None),
        P("row", None),
        P(),
        P(),
        P(),
        P(),
        P(),
        P(),
        P(),
        P(),
        P(None, "pat"),
        P("pat", None),
        P("row", "seq", "pat"),
    )
    return jax.shard_map(
        per_device,
        mesh=mesh,
        in_specs=placed,
        out_specs=(
            P("row", "seq", "pat"),
            P("row", ("seq", "pat"), None),
            P(),
            P(),
            P(),
            P(),
            P(),
            P(),
            P(),
            P(),
            P(None, "pat"),
            P("pat", None),
        ),
        check_vma=False,
    )
```

```python
import functools

import jax
import jax.numpy as jnp
from jax import lax
from jax.experimental import pallas as pl
from jax.experimental.pallas import tpu as pltpu
from jax.sharding import PartitionSpec as P

D = 768
HEADS = 12
HDIM = 64

epsilon = 1e-05
masked_low = -1e30
segment_parts = (1, 2, 4, 8, 16)
dilations = (1, 2, 4, 6, 12)
DOCS = 3
FEATS = 128
TILE = 256
VMEM_LIMIT = 60 * 1024 * 1024
SMALL_LIMIT = 20 * 1024 * 1024
COPIES = 64
f32 = jnp.float32
bf16 = jnp.bfloat16


def dot(a, b):
    return lax.dot_general(a, b, (((1,), (0,)), ((), ())), preferred_element_type=f32)


def dot_nt(a, b):
    return lax.dot_general(a, b, (((1,), (1,)), ((), ())), preferred_element_type=f32)


def dot_tn(a, b):
    return lax.dot_general(a, b, (((0,), (0,)), ((), ())), preferred_element_type=f32)


class Staged:
    def __init__(self, outside, inside, sems, free):
        self.outside, self.inside, self.sems, self.free = outside, inside, sems, free
        self.pending = []

    def start(self, source=None, target=None):
        copy = pltpu.make_async_copy(
            self.outside if source is None else source,
            self.inside if target is None else target,
            self.sems.at[next(self.free)],
        )
        copy.start()
        self.pending.append(copy)

    def get(self):
        for copy in self.pending:
            copy.wait()
        self.pending = []
        return self.inside

    def put(self, source, target):
        copy = pltpu.make_async_copy(source, target, self.sems.at[next(self.free)])
        copy.start()
        self.pending.append(copy)

    def send(self, at=...):
        copy = pltpu.make_async_copy(
            self.inside.at[at], self.outside.at[at], self.sems.at[next(self.free)]
        )
        copy.start()
        self.pending.append(copy)


def staged_call(body, scalars, arrays, outs, scratch=(), windows=None, limit=VMEM_LIMIT, late=0, aliases=(), bare=(), flops=0):
    windows = windows or {}
    n_scalar, n_in, n_out = len(scalars), len(arrays), len(outs)

    def kernel(*refs):
        scalar_refs, refs = refs[:n_scalar], refs[n_scalar:]
        outside, refs = refs[: n_in + n_out], refs[n_in + n_out :]
        inside, refs = refs[: n_in + n_out], refs[n_in + n_out :]
        sems, rest = refs[0], refs[1:]
        free = iter(range(COPIES))
        every = [Staged(o, i, sems, free) for o, i in zip(outside, inside, strict=True)]
        ins, results = every[:n_in], every[n_in:]
        for at, one in enumerate(ins[: n_in - late]):
            if at in windows:
                start = windows[at](scalar_refs)
                size = one.inside.shape[-1]
                one.start(one.outside.at[:, pl.ds(pl.multiple_of(start, 128), size)])
            else:
                one.start()
        body(scalar_refs, ins, results, rest)
        for one in ins + results:
            one.get()

    def buffer(at, array):
        dims = array.shape
        if at >= n_in - late:
            return pltpu.VMEM((16, 128), array.dtype)
        if at in windows:
            dims = (*dims[:-1], 256)
        return pltpu.VMEM(dims, array.dtype)

    return pl.pallas_call(
        kernel,
        out_shape=tuple(outs),
        in_specs=[pl.BlockSpec(memory_space=pltpu.SMEM)] * n_scalar
        + [pl.BlockSpec(memory_space=pl.ANY)] * n_in,
        out_specs=(pl.BlockSpec(memory_space=pltpu.HBM),) * n_out,
        scratch_shapes=[buffer(at, a) for at, a in enumerate(arrays)]
        + [
            pltpu.VMEM((16, 128) if at in bare else o.shape, o.dtype)
            for at, o in enumerate(outs)
        ]
        + [pltpu.SemaphoreType.DMA((COPIES,))]
        + list(scratch),
        input_output_aliases={n_scalar + a: o for a, o in aliases},
        compiler_params=pltpu.CompilerParams(vmem_limit_bytes=limit),
        cost_estimate=pl.CostEstimate(flops=flops, bytes_accessed=0, transcendentals=0),
    )(*scalars, *arrays)


def normalise(values):
    center = values - jnp.mean(values, axis=-1, keepdims=True)
    scale = lax.rsqrt(jnp.mean(center * center, axis=-1, keepdims=True) + epsilon)
    return center * scale, scale


def norm_backward(hat, scale, grad):
    return scale * (
        grad
        - jnp.mean(grad, axis=-1, keepdims=True)
        - hat * jnp.mean(grad * hat, axis=-1, keepdims=True)
    )


def make_features(heads, part, docs, feats):
    _, length, _ = feats.inside.shape
    position = lax.broadcasted_iota(jnp.int32, (1, length), 1)
    feature = lax.broadcasted_iota(jnp.int32, (FEATS, length), 0)
    for h in range(heads):
        head = part * heads + h
        hit = None
        base = 0
        for size, dilation in zip(segment_parts, dilations, strict=True):
            seg_width = length * size // 16
            inside = lax.rem(
                lax.rem(position, seg_width) + dilation - lax.rem(head, dilation), dilation
            )
            key = base + lax.div(position, seg_width) * DOCS + docs
            key = jnp.where(inside == 0, key, -1)
            found = feature == key
            hit = found if hit is None else hit | found
            base += DOCS * (16 // size)
        feats.inside[h] = jnp.where(hit, 1.0, 0.0).T.astype(bf16)
        feats.send(h)


def project_kernel(parts, pair, scalars, ins, outs, scratch):
    x, docs, gain, bias, *weights = ins[:7]
    normed, q, kv, own, feats = outs[:5]
    width = D // parts
    where = scalars[0]
    own.inside[:, 3 * width :] = jnp.zeros((D, D - 3 * width), bf16)
    gain = gain.get()[...].reshape(1, D)
    bias = bias.get()[...].reshape(1, D)
    x.get()
    span = x.inside.shape[0]
    for start in range(0, span, TILE):
        rows = slice(start, start + TILE)
        hat, _ = normalise(x.inside[rows, :].astype(f32))
        normed.inside[rows, :] = (hat * gain + bias).astype(bf16)
    normed.send()
    for w in weights:
        w.get()
    for odd in range(2):

        @pl.when(where[0] % 2 == odd)
        def _():
            for at, w in enumerate(weights):
                own.inside[:, at * width : (at + 1) * width] = w.inside[
                    :, odd * 64 : odd * 64 + width
                ]

    own.send()
    for start in range(0, span, TILE):
        rows = slice(start, start + TILE)
        made = dot(normed.inside[rows, :], own.inside[:, : 3 * width]).astype(bf16)
        q.inside[rows, :] = (made[:, :width].astype(f32) * HDIM**-0.5).astype(bf16)
        kv.inside[rows, :] = made[:, width:]
    kv.send()
    q.send()
    if pair:
        x_far = ins[7].get()

        @pl.when(scalars[1][0] > 0)
        def _():
            for start in range(0, span, TILE):
                rows = slice(start, start + TILE)
                hat, _ = normalise(x_far[rows, :].astype(f32))
                low = (hat * gain + bias).astype(bf16)
                outs[5].inside[rows, :] = dot(low, own.inside[:, width : 3 * width]).astype(bf16)

        outs[5].send()
    make_features(feats.inside.shape[0], where[0], docs.get()[...], feats)


def head_mask(heads, width):
    lane = lax.broadcasted_iota(jnp.int32, (1, width), 1)
    return [((lane >= h * HDIM) & (lane < (h + 1) * HDIM)).astype(bf16) for h in range(heads)]


def attention_kernel(heads, span, scalars, ins, outs, scratch):
    where = scalars[0]
    q, kv, feats, kv_far = (one.get() for one in ins)
    mixed_low, mixed_t, lse = (one.inside for one in outs)
    q_head, k, v_t, kf, vf_t, tops, totals = scratch
    width = heads * HDIM
    masks = head_mask(heads, width)
    for h in range(heads):
        q_head[h] = q[...] * masks[h]
    k[...] = kv[:, :width]
    v_t[...] = kv[:, width:].T
    far = kv_far.shape[0] // span

    def turn(j, _):
        rows = pl.ds(pl.multiple_of(j * span, span), span)
        kf[rows, :] = kv_far[rows, :width]
        vf_t[j] = kv_far[rows, width:].T
        return 0

    mine = where[0]
    lax.fori_loop(0, jnp.minimum(mine, far), turn, 0)
    own_start = pl.multiple_of(mine * span, span)
    lse[...] = jnp.zeros(lse.shape, f32)
    pairs = [(start, h) for start in range(0, span, TILE) for h in range(heads)]

    def part(start, h, k_rows, f_rows, v_rows, causal):
        counts = dot_nt(f_rows, feats[h, pl.ds(own_start + start, TILE), :])
        if causal:
            at_k = lax.broadcasted_iota(jnp.int32, counts.shape, 0)
            at_q = lax.broadcasted_iota(jnp.int32, counts.shape, 1) + start
            counts = jnp.where(at_k <= at_q, counts, 0.0)
        scores = dot_nt(k_rows, q_head[h, start : start + TILE, :])
        scores = jnp.where(counts > 0, scores, masked_low)
        return counts, scores, v_rows

    for at, (start, h) in enumerate(pairs):
        size = start + TILE
        head_rows = slice(h * HDIM, (h + 1) * HDIM)
        counts, scores, v_rows = part(
            start,
            h,
            k[:size, :],
            feats[h, pl.ds(own_start, size), :],
            v_t[head_rows, :size],
            True,
        )
        top = jnp.max(scores, axis=0, keepdims=True)
        weights = counts * jnp.exp(scores - top)
        tops[at : at + 1, :] = top
        totals[at : at + 1, :] = jnp.sum(weights, axis=0, keepdims=True)
        mixed_t[head_rows, start : start + TILE] = dot(v_rows, weights.astype(bf16))

    def far_step(j, _):
        rows = pl.ds(pl.multiple_of(j * span, span), span)
        for at, (start, h) in enumerate(pairs):
            head_rows = slice(h * HDIM, (h + 1) * HDIM)
            counts, scores, v_rows = part(
                start, h, kf[rows, :], feats[h, rows, :], vf_t[j, head_rows, :], False
            )
            top = tops[at : at + 1, :]
            new_top = jnp.maximum(top, jnp.max(scores, axis=0, keepdims=True))
            weights = counts * jnp.exp(scores - new_top)
            factor = jnp.exp(top - new_top)
            tops[at : at + 1, :] = new_top
            totals[at : at + 1, :] = totals[at : at + 1, :] * factor + jnp.sum(
                weights, axis=0, keepdims=True
            )
            mixed_t[head_rows, start : start + TILE] = mixed_t[
                head_rows, start : start + TILE
            ] * factor + dot(v_rows, weights.astype(bf16))
        return 0

    lax.fori_loop(0, mine, far_step, 0)
    for at, (start, h) in enumerate(pairs):
        head_rows = slice(h * HDIM, (h + 1) * HDIM)
        total = totals[at : at + 1, :]
        done = mixed_t[head_rows, start : start + TILE] / total
        mixed_t[head_rows, start : start + TILE] = done
        mixed_low[head_rows, start : start + TILE] = done.astype(bf16)
        lse[h : h + 1, start : start + TILE] = tops[at : at + 1, :] + jnp.log(total)
    for one in outs:
        one.send()


def count_rows(f_rows, f_tile, low_from):
    counts = dot_nt(f_rows, f_tile)
    if low_from is not None:
        at_k = lax.broadcasted_iota(jnp.int32, counts.shape, 0)
        at_q = lax.broadcasted_iota(jnp.int32, counts.shape, 1) + low_from
        counts = jnp.where(at_k <= at_q, counts, 0.0)
    return counts


def attention_back_kernel(heads, span, scalars, ins, outs, scratch):
    where = scalars[0]
    parts, q, mixed_t, lse, kv, feats, kv_far = (one.get() for one in ins)
    grad_q, grad_kv, grad_far = (one.inside for one in outs)
    q_head, g_head, dots, probs, slopes, k, v, k_t, gq_t = scratch
    width = heads * HDIM
    masks = head_mask(heads, width)
    mine = where[0]
    far = kv_far.shape[0] // span
    total = parts[0].astype(f32)
    for part in range(1, parts.shape[0]):
        total = total + parts[part].astype(f32)
    low_t = total.astype(bf16)
    low = low_t.T
    for h in range(heads):
        q_head[h] = q[...] * masks[h]
        g_head[h] = low * masks[h]
    product = low_t.astype(f32) * mixed_t[...]
    for h in range(heads):
        dots[h : h + 1, :] = jnp.sum(product[h * HDIM : (h + 1) * HDIM], axis=0, keepdims=True)
    own_start = pl.multiple_of(mine * span, span)

    def block(h, start, size, rows, diagonal):
        tile = slice(start, start + TILE)
        columns = slice(h * span + start, h * span + start + TILE)
        f_rows = feats[h, pl.ds(own_start, size) if diagonal else rows, :]
        f_tile = feats[h, pl.ds(own_start + start, TILE), :]
        counts = count_rows(f_rows, f_tile, start if diagonal else None)
        scores = jnp.where(counts > 0, dot_nt(k[:size, :], q_head[h, tile, :]), masked_low)
        prob = counts * jnp.exp(scores - lse[h : h + 1, tile])
        grad_prob = dot_nt(v[:size, :], g_head[h, tile, :])
        slope = prob * (grad_prob - dots[h : h + 1, tile])
        probs[:size, columns] = prob.astype(bf16)
        slopes[:size, columns] = slope.astype(bf16)
        if size < span:
            probs[size:, columns] = jnp.zeros((span - size, TILE), bf16)
            slopes[size:, columns] = jnp.zeros((span - size, TILE), bf16)

    def finish():
        k_t[...] = k[...].T
        grad_v_rows = dot(probs[...], g_head[...].reshape(heads * span, width))
        grad_k_rows = dot(slopes[...], q_head[...].reshape(heads * span, width))
        terms = [
            dot(k_t[h * HDIM : (h + 1) * HDIM, :], slopes[:, h * span : (h + 1) * span])
            for h in range(heads)
        ]
        return grad_k_rows, grad_v_rows, terms

    k[...] = kv[:, :width]
    v[...] = kv[:, width:]
    for start in range(0, span, TILE):
        for h in range(heads):
            size = start + TILE
            block(h, start, size, None, True)
    grad_k_rows, grad_v_rows, terms = finish()
    grad_kv[:, :width] = grad_k_rows
    grad_kv[:, width:] = grad_v_rows
    outs[1].send()
    for h in range(heads):
        gq_t[h * HDIM : (h + 1) * HDIM, :] = terms[h]

    def far_block(j, _):
        rows = pl.ds(pl.multiple_of(j * span, span), span)
        k[...] = kv_far[rows, :width]
        v[...] = kv_far[rows, width:]
        for start in range(0, span, TILE):
            for h in range(heads):
                block(h, start, span, rows, False)
        grad_k_rows, grad_v_rows, terms = finish()
        grad_far[rows, :width] = grad_k_rows.astype(bf16)
        grad_far[rows, width:] = grad_v_rows.astype(bf16)
        for h in range(heads):
            gq_t[h * HDIM : (h + 1) * HDIM, :] += terms[h]
        return 0

    used = jnp.minimum(mine, far)
    lax.fori_loop(0, used, far_block, 0)

    def clear(j, _):
        grad_far[pl.ds(pl.multiple_of(j * span, span), span), :] = jnp.zeros((span, 2 * width), bf16)
        return 0

    lax.fori_loop(used, far, clear, 0)
    outs[2].send()
    grad_q[...] = (gq_t[...] * HDIM**-0.5).T.astype(bf16)
    outs[0].send()


def middle_kernel(scalars, ins, outs, scratch):
    mixed4, x, w_out, gain, bias, w_up, w_down, *c_parts = ins
    gm, sums, act, gh, branch, low, c, resids = outs
    (c4,) = scratch
    parts, width, span = mixed4.inside.shape
    for step, one in enumerate(c_parts):
        one.start(target=c4.at[scalars[0][0] ^ step])
    mixed_t = mixed4.get()[...].reshape(D, span)
    x.get(), w_out.get()
    gain = gain.get()[...].reshape(1, D)
    bias = bias.get()[...].reshape(1, D)
    gain_sum = jnp.zeros((1, D), f32)
    bias_sum = jnp.zeros((1, D), f32)
    for start in range(0, span, span):
        rows = slice(start, start + span)
        resid = x.inside[rows, :].astype(f32) + dot_tn(mixed_t[:, rows], w_out.inside[...])
        resids.inside[rows, :] = resid.astype(bf16)
        hat, scale = normalise(resid)
        normed = (hat * gain + bias).astype(bf16)
        low.inside[rows, :] = normed
        w_up.get()
        hidden = dot(normed, w_up.inside[...])
        bell = 0.5 + 0.5 * lax.erf(hidden * (0.5**0.5))
        act.inside[rows, :] = (hidden * bell).astype(bf16)
        slope = bell + hidden * jnp.exp(-0.5 * hidden * hidden) * 0.3989422804014327
        if start == 0:
            w_down.get()
            for one in c_parts:
                one.get()
            for part in range(parts):
                c.inside[:, part * width : (part + 1) * width] = c4[part].T
            c.send()
        c_rows = c.inside[rows, :]
        grad_hidden = (slope * dot_nt(c_rows, w_down.inside[...])).astype(bf16)
        gh.inside[rows, :] = grad_hidden
        grad_normed = dot_nt(grad_hidden, w_up.inside[...])
        gain_sum = gain_sum + jnp.sum(grad_normed * hat, axis=0, keepdims=True)
        bias_sum = bias_sum + jnp.sum(grad_normed, axis=0, keepdims=True)
        grad_resid = norm_backward(hat, scale, grad_normed * gain) + c_rows.astype(f32) * (
            1.0 / parts
        )
        grad_low = grad_resid.astype(bf16)
        branch.inside[rows, :] = grad_low
        for one in (act, low, gh, resids, branch):
            one.send(pl.ds(start, span))
        for part in range(parts):
            gm.inside[part, :, rows] = dot_nt(
                w_out.inside[part * width : (part + 1) * width, :], grad_low
            ).astype(bf16)
            gm.send(part)
    sums.inside[0:1, :] = gain_sum
    sums.inside[1:2, :] = bias_sum
    sums.send()


def weights_kernel(pair, scalars, ins, outs, scratch):
    act, c, low, gh, mixed4, branch, w_down, resids = ins
    ffn, *wide = outs
    (made,) = scratch
    parts, width, span = mixed4.inside.shape
    chunk = span // parts
    where = scalars[0]

    def out_product():
        mixed_t = mixed4.get()[...].reshape(D, span)
        return dot(mixed_t, branch.get()[...])

    products = (
        lambda: dot_tn(act.get()[...], c.get()[...]),
        lambda: dot_tn(low.get()[...], gh.get()[...]),
        out_product,
    )
    for at, product in enumerate(products):
        if not pair:
            wide[0].inside[at] = product().astype(bf16)
            continue
        made[...] = product().astype(bf16)
        rows_count = wide[0].inside.shape[1]
        size = D // (2 * rows_count)
        for row in range(rows_count):
            for out, half in ((wide[0].inside.at[at], where[0]), (wide[1 + at].inside, 1 - where[0])):
                start = pl.multiple_of((2 * row + half) * size, size)
                out[row] = made[pl.ds(start, size), :]
        wide[1 + at].send()
        wide[0].send(at)
    if not pair:
        wide[0].send()
    w_down.get(), resids.get()
    for start in range(0, span, TILE):
        rows = slice(start, start + TILE)
        out = dot(act.inside[rows, :], w_down.inside[...]) + resids.inside[rows, :].astype(f32) * (
            1.0 / parts
        )
        out_t = out.astype(bf16).T
        for part in range(parts):
            for at in range(start, start + TILE, chunk):
                ffn.inside[part, at // chunk * width : (at // chunk + 1) * width, :] = out_t[
                    part * width : (part + 1) * width, at - start : at - start + chunk
                ]
    ffn.send()


def add_kernel(scalars, ins, outs, scratch):
    keep, *more = ins
    keep.get()
    for group, one in enumerate(more):
        one.get()
        for at, out in enumerate(outs):
            block = scalars[0][0] ^ at
            out.inside[group] = (
                keep.inside[group, block].astype(f32) + one.inside[block].astype(f32)
            ).astype(bf16)
        for out in outs[1:] + outs[:1]:
            out.send(group)


def row_sum_kernel(parts, scalars, ins, outs, scratch):
    ffn_own, out_parts = outs
    (rows,) = scratch
    total = ins[0].get()[...].astype(f32)
    for one in ins[1:]:
        total = total + one.get()[...].astype(f32)
    total = total.astype(bf16)
    size = total.shape[1]
    half = size // 2
    width = D // parts
    for part in range(parts):
        columns = slice(part * width, (part + 1) * width)
        out_parts.inside[part, :, :width] = total[2, :half, columns]
        out_parts.inside[part, :, width:] = total[2, half:, columns]
    out_parts.send()
    rows[...] = total[:2].reshape(2 * size, D)
    for row in range(ffn_own.outside.shape[0]):
        ffn_own.put(rows, ffn_own.outside.at[row])


SLOT = 64


def last_kernel(parts, pair, scalars, ins, outs, scratch):
    gq, gkv, gkv_more, normed, own, x, gain, gr, sums = ins
    back, *narrow = outs
    grads, small, made = scratch
    width = D // parts
    span = x.inside.shape[0]
    piece = span // parts
    lanes = 3 * width + SLOT
    grads[:, 3 * width :] = jnp.zeros((span, D - 3 * width), bf16)
    grads[:, :width] = gq.get()[...]
    gkv.get(), gkv_more.get()
    grads[:, width : 3 * width] = (
        gkv.inside[...] + gkv_more.inside[...].astype(f32)
    ).astype(bf16)
    made[...] = dot_tn(normed.get()[...], grads[:, :lanes]).astype(bf16)
    if pair:
        rows_count, size, _ = narrow[1].inside.shape
        halves = (
            (narrow[0].inside.at[0], scalars[0][0]),
            (narrow[1].inside, 1 - scalars[0][0]),
        )
        for row in range(rows_count):
            for out, half in halves:
                start = pl.multiple_of((2 * row + half) * size, size)
                out[row] = made[pl.ds(start, size), :]
    else:
        narrow[0].inside[...] = made[...]
    own.get(), x.get(), gr.get(), sums.get()
    gain = gain.get()[...].reshape(1, D)
    gain_sum = jnp.zeros((1, D), f32)
    bias_sum = jnp.zeros((1, D), f32)
    for start in range(0, span, TILE):
        rows = slice(start, start + TILE)
        hat, scale = normalise(x.inside[rows, :].astype(f32))
        grad_normed = dot_nt(grads[rows, :], own.inside[...])
        gain_sum = gain_sum + jnp.sum(grad_normed * hat, axis=0, keepdims=True)
        bias_sum = bias_sum + jnp.sum(grad_normed, axis=0, keepdims=True)
        grad_in = gr.inside[rows, :].astype(f32) + norm_backward(hat, scale, grad_normed * gain)
        turned = grad_in.astype(bf16).T
        for at in range(start, start + TILE, piece):
            back.inside[at // piece] = turned[:, at - start : at - start + piece]
            back.send(at // piece)
    pieces = D // SLOT
    four = jnp.concatenate([gain_sum, bias_sum, sums.inside[0:2, :]], axis=0)
    for part in range(pieces):
        small[4 * part : 4 * part + 4, :] = four[:, part * SLOT : (part + 1) * SLOT]
    tail = small[...].astype(bf16)
    if pair:
        for row in range(rows_count):
            for out, _ in halves:
                out[row, :48, 3 * width :] = tail
        narrow[1].send()
        narrow[0].send()
    else:
        narrow[0].inside[:48, 3 * width :] = tail
        narrow[0].send()


def own_sum_kernel(parts, count, scalars, ins, outs, scratch):
    mine = outs[0].inside
    (small,) = scratch
    width = D // parts
    size = ins[0].inside.shape[1]
    half = size // 2
    out = ins[count].get()[0].astype(f32)
    for part in range(1, parts):
        out = out + ins[count].inside[part].astype(f32)
    mine[:half, 3 * width :] = out[:, :width].astype(bf16)
    mine[half:size, 3 * width :] = out[:, width:].astype(bf16)
    total = ins[0].get()[0].astype(f32)
    for one in ins[1:count]:
        total = total + one.get()[0].astype(f32)
    mine[:size, : 3 * width] = total[:, : 3 * width].astype(bf16)
    pieces = D // SLOT
    small[...] = jnp.zeros(small.shape, f32)
    for part in range(pieces):
        small[0:4, part * SLOT : (part + 1) * SLOT] = total[4 * part : 4 * part + 4, 3 * width :]
    mine[size:, :] = small[...].astype(bf16)
    outs[0].send()


def output_kernel(scalars, ins, outs, scratch):
    got = ins[0].get()
    parts, _, piece = got.shape
    width = D // parts
    total = got[0, :D].astype(f32)
    for part in range(1, parts):
        total = total + got[part, :D].astype(f32)
    for at in range(parts):
        outs[0].inside[:, at * piece : (at + 1) * piece] = total[
            at * width : (at + 1) * width
        ].astype(bf16)
    outs[0].send()


def finish_kernel(scalars, ins, outs, scratch):
    grad_in, *vectors = outs
    (small,) = scratch
    size = ins[1].outside.shape[1] - 16
    ins[1].start(source=ins[1].outside.at[:, pl.ds(size, 16), :], target=small)
    back = ins[0].get()
    total = back[0].astype(f32)
    for at in range(1, back.shape[0]):
        total = total + back[at].astype(f32)
    grad_in.inside[...] = total.T.astype(bf16)
    grad_in.send()
    ins[1].get()
    sums = small[0].astype(f32)
    for at in range(1, small.shape[0]):
        sums = sums + small[at].astype(f32)
    for at, vector in enumerate(vectors):
        vector.inside[...] = sums[at]
        vector.send()


def spread_kernel(steps, scalars, ins, outs, scratch):
    (buffer,) = scratch
    row, seq = scalars
    size = buffer.shape[2]
    at = 0
    for step, (row_step, seq_step, count) in enumerate(steps):
        part = 0
        for one in ins[at : at + count]:
            got = one.get()
            for own in range(got.shape[0]):
                width = D // (got.shape[0] * count)
                columns = slice(part * width, (part + 1) * width)
                for grad in range(4):
                    buffer[grad, step, :, columns] = got[
                        own, :, grad * width : (grad + 1) * width
                    ].astype(f32)
                part += 1
        at += count
        start = pl.multiple_of((2 * (row[0] ^ row_step) + (seq[0] ^ seq_step)) * size, size)
        for grad in range(4):
            out = outs[grad]
            out.put(buffer.at[grad, step], out.outside.at[pl.ds(start, size), :])


def spread(row_here, here, steps, earlier=(), flops=0):
    count = sum(len(blocks) for _, _, blocks in steps)
    size = steps[0][2][0].shape[1]
    received = [block for _, _, blocks in steps for block in blocks]
    return staged_call(
        functools.partial(spread_kernel, [(a, b, len(c)) for a, b, c in steps]),
        [row_here, here],
        [*received, *earlier],
        (shape(D, D, kind=f32),) * 4,
        scratch=[pltpu.VMEM((4, len(steps), size, D), f32)],
        limit=SMALL_LIMIT,
        late=len(earlier),
        aliases=tuple((count + at, at) for at in range(len(earlier))),
        bare=range(4),
        flops=flops,
    )


def spread_ffn_kernel(scalars, ins, outs, scratch):
    (buffer,) = scratch
    size = buffer.shape[2]
    for half, one in enumerate(ins):
        got = one.get()
        for row in range(got.shape[0]):
            start = pl.multiple_of((2 * row + (scalars[0][0] ^ half)) * size, size)
            for grad, out in enumerate(outs):
                place = buffer.at[grad, half * got.shape[0] + row]
                place[...] = got[row, grad * size : (grad + 1) * size, :].astype(f32)
                out.put(place, out.outside.at[pl.ds(start, size), :])


def first_spread_kernel(steps, scalars, ins, outs, scratch):
    spread_ffn_kernel(scalars[1:], ins[:2], outs[:2], scratch[:1])
    spread_kernel(steps, scalars, ins[2:], outs[2:], scratch[1:])


def broadcast_exchange(value, axis):
    count = lax.axis_size(axis)
    return lax.all_to_all(
        jnp.broadcast_to(value[None], (count,) + value.shape), axis, 0, 0, tiled=False
    )


def swap(value):
    return lax.ppermute(value, "seq", [(0, 1), (1, 0)])


def trade(value, axis, step):
    return lax.ppermute(value, axis, [(a, a ^ step) for a in range(lax.axis_size(axis))])


def shape(*dims, kind=bf16):
    return jax.ShapeDtypeStruct(dims, kind)


def per_device(
    block_input,
    doc_ids,
    ln1_gain,
    ln1_bias,
    w_query,
    w_key,
    w_value,
    w_out,
    ln2_gain,
    ln2_bias,
    w_up,
    w_down,
    cotangent,
):
    span = block_input.shape[1]
    rows_count = lax.axis_size("row")
    seq_count = lax.axis_size("seq")
    parts = lax.axis_size("pat")
    row_index = lax.axis_index("row")
    seq_index = lax.axis_index("seq")
    pat_index = lax.axis_index("pat")
    pair = seq_count == 2
    heads = HEADS // parts
    width = D // parts
    quarter = span // parts
    size = D // (rows_count * seq_count) if pair else D
    here = seq_index.astype(jnp.int32)[None]
    row_here = row_index.astype(jnp.int32)[None]
    part_here = pat_index.astype(jnp.int32)[None]
    x = block_input[0]

    c_own = cotangent[0].T
    c_parts = [c_own] + [trade(c_own, "pat", s) for s in range(1, parts)]
    def window(scalars):
        return scalars[0][0] * width // 128 * 128

    far_shapes = (shape(span, 2 * width),) if pair else ()
    normed, q, kv, own, feats, *far = staged_call(
        functools.partial(project_kernel, parts, pair),
        [part_here, here],
        [x, doc_ids, ln1_gain, ln1_bias, w_query, w_key, w_value] + ([swap(x)] if pair else []),
        (
            shape(span, D),
            shape(span, width),
            shape(span, 2 * width),
            shape(D, D),
            shape(heads, doc_ids.shape[1], FEATS),
            *far_shapes,
        ),
        windows={4: window, 5: window, 6: window},
        flops=1 << 42,
    )

    kv_far = far[0] if pair else lax.all_gather(kv, "seq", axis=0, tiled=True)
    far_rows = kv_far.shape[0]

    mixed, mixed_t, lse = staged_call(
        functools.partial(attention_kernel, heads, span),
        [here],
        [q, kv, feats, kv_far],
        (shape(width, span), shape(width, span, kind=f32), shape(8, span, kind=f32)),
        scratch=[
            pltpu.VMEM((heads, span, width), bf16),
            pltpu.VMEM((span, width), bf16),
            pltpu.VMEM((width, span), bf16),
            pltpu.VMEM((far_rows, width), bf16),
            pltpu.VMEM((far_rows // span, width, span), bf16),
            pltpu.VMEM((heads * span // TILE + 8, TILE), f32),
            pltpu.VMEM((heads * span // TILE + 8, TILE), f32),
        ],
    )
    mixed, *c_parts = lax.optimization_barrier((mixed, *c_parts))
    mixed4 = lax.all_gather(mixed, "pat")

    wide_shapes = (shape(3, D, D),)
    if pair:
        wide_shapes = (shape(3, rows_count, size, D),) + (shape(rows_count, size, D),) * 3
    gm, sums, act, gh, branch, low, c, resids = staged_call(
        middle_kernel,
        [part_here],
        [mixed4, x, w_out, ln2_gain, ln2_bias, w_up, w_down, *c_parts],
        (shape(parts, width, span), shape(8, D, kind=f32)) + (shape(span, D),) * 6,
        scratch=[pltpu.VMEM((parts, width, span), bf16)],
        late=parts,
    )
    gm_parts = lax.all_to_all(gm, "pat", 0, 0, tiled=True)
    ffn, *wide = staged_call(
        functools.partial(weights_kernel, pair),
        [here],
        [act, c, low, gh, mixed4, branch, w_down, resids],
        (shape(parts, parts * width, quarter), *wide_shapes),
        scratch=[pltpu.VMEM((D, D), bf16)],
        flops=1 << 42,
    )

    if pair:
        keep, *sends = wide
        ordered = staged_call(
            add_kernel,
            [row_here],
            [keep, *[swap(send) for send in sends]],
            (shape(3, size, D),) * rows_count,
            limit=63 << 20,
        )
        wide_parts = [ordered[0]] + [trade(ordered[s], "row", s) for s in range(1, rows_count)]

    ffn, _ = lax.optimization_barrier((ffn, gm_parts))
    ffn_parts = lax.all_to_all(ffn, "pat", 0, 0, tiled=True)
    (out_t,) = staged_call(
        output_kernel,
        [],
        [ffn_parts],
        (shape(width, span),),
        limit=SMALL_LIMIT,
        flops=1 << 42,
    )
    gq, gkv, gkv_far = staged_call(
        functools.partial(attention_back_kernel, heads, span),
        [here],
        [gm_parts, q, mixed_t, lse, kv, feats, kv_far],
        (
            shape(span, width),
            shape(span, 2 * width, kind=f32),
            shape(far_rows, 2 * width),
        ),
        scratch=[
            pltpu.VMEM((heads, span, width), bf16),
            pltpu.VMEM((heads, span, width), bf16),
            pltpu.VMEM((8, span), f32),
            pltpu.VMEM((span, heads * span), bf16),
            pltpu.VMEM((span, heads * span), bf16),
            pltpu.VMEM((span, width), bf16),
            pltpu.VMEM((span, width), bf16),
            pltpu.VMEM((width, span), bf16),
            pltpu.VMEM((width, span), f32),
        ],
        flops=1 << 42,
    )

    if pair:
        gkv_more = swap(gkv_far)
        ffn_own, out_parts = staged_call(
            functools.partial(row_sum_kernel, parts),
            [],
            wide_parts,
            (shape(rows_count, 2 * size, D), shape(parts, size // 2, 2 * width)),
            scratch=[pltpu.VMEM((2 * size, D), bf16)],
            limit=SMALL_LIMIT,
            bare=(0,),
        )
        out_parts, _ = lax.optimization_barrier((out_parts, ffn_parts))
        out_parts = lax.all_to_all(out_parts, "pat", 0, 0, tiled=True)
    else:
        gkv_more = lax.psum_scatter(gkv_far, "seq", scatter_dimension=0, tiled=True)

    lanes = 3 * width + SLOT
    narrow_shapes = (shape(1, rows_count, size, lanes), shape(rows_count, size, lanes)) if pair else (shape(D, lanes),)
    back, *narrow = staged_call(
        functools.partial(last_kernel, parts, pair),
        [here],
        [gq, gkv, gkv_more, normed, own, x, ln1_gain, branch, sums],
        (shape(parts, parts * width, quarter), *narrow_shapes),
        scratch=[
            pltpu.VMEM((span, D), bf16),
            pltpu.VMEM((48, SLOT), f32),
            pltpu.VMEM((D, lanes), bf16),
        ],
    )

    if pair:
        keep, send = narrow
        send, *_ = lax.optimization_barrier((send, *wide_parts[1:]))
        keep, _ = lax.optimization_barrier((keep, ffn_own))
        ordered = staged_call(
            add_kernel, [row_here], [keep, swap(send)], (shape(1, size, lanes),) * rows_count,
            limit=65000 << 10,
        )
        received = [ordered[0]] + [trade(ordered[s], "row", s) for s in range(1, rows_count)]
        received[3], _ = lax.optimization_barrier((received[3], out_t))
        (mine,) = staged_call(
            functools.partial(own_sum_kernel, parts, rows_count),
            [],
            [*received, out_parts],
            (shape(size + 16, D),),
            scratch=[pltpu.VMEM((16, D), f32)],
            limit=SMALL_LIMIT,
        )
        gathered = lax.all_gather(mine, "pat")
        ffn_own, *_ = lax.optimization_barrier(
            (ffn_own, out_parts, *received[1:])
        )
        ffn_mine = lax.all_to_all(ffn_own, "row", 0, 0, tiled=True)
        gathered, ffn_mine, back = lax.optimization_barrier((gathered, ffn_mine, back))
        back_parts = lax.all_to_all(back, "pat", 0, 0, tiled=True)
        own = gathered[:, :size]
        near1, near2 = trade(own, "row", 1), trade(own, "row", 2)
        half1, half2 = near1[: parts // 2], near2[parts // 2 :]
        far = (trade(half1, "row", 2), trade(half2, "row", 1))
        sent1, _ = lax.optimization_barrier((near1, half1))
        sent2, _ = lax.optimization_barrier((near2, half2))
        steps = [(0, 0, 1), (1, 0, 1), (2, 0, 1), (0, 1, 1), (1, 1, 1), (2, 1, 1)]
        grad_down, grad_up, *grads = staged_call(
            functools.partial(first_spread_kernel, steps),
            [row_here, here],
            [
                ffn_mine,
                swap(ffn_mine),
                own,
                near1,
                near2,
                swap(own),
                swap(sent1),
                swap(sent2),
            ],
            (shape(D, D, kind=f32),) * 6,
            scratch=[
                pltpu.VMEM((2, 2 * rows_count, size, D), f32),
                pltpu.VMEM((4, len(steps), size, D), f32),
            ],
            limit=24 << 20,
            bare=range(6),
        )
        sent = lax.optimization_barrier((*far, grads[0]))[:2]
        grads = spread(
            row_here,
            here,
            [(3, 0, far), (3, 1, tuple(swap(value) for value in sent))],
            grads,
        )
    else:
        axes = ("row", "seq")
        back_parts = lax.all_to_all(back, "pat", 0, 0, tiled=True)
        wide_sum = lax.psum(wide[0], axes)
        grad_down, grad_up = wide_sum[0].astype(f32), wide_sum[1].astype(f32)
        grad_out = lax.psum(wide_sum[2], "pat").astype(f32)
        gathered = lax.all_gather(lax.psum(narrow[0], axes), "pat")
        small = gathered[:, :48, 3 * width :].reshape(parts, D // SLOT, 4, SLOT)
        small = small.transpose(0, 2, 1, 3).reshape(parts, 4, D)
        small = jnp.pad(small, ((0, 0), (0, 12), (0, 0)))
        grads = [
            gathered[:, :, at * width : (at + 1) * width]
            .astype(f32)
            .transpose(1, 0, 2)
            .reshape(D, D)
            for at in range(3)
        ] + [grad_out]
    if pair:
        back_parts, _ = lax.optimization_barrier((back_parts, grads[0]))
    grad_in, *vectors = staged_call(
        finish_kernel,
        [],
        [back_parts, gathered if pair else small],
        (shape(quarter, D),) + (shape(D, kind=f32),) * 4,
        scratch=[pltpu.VMEM((parts, 16, D), bf16)],
        limit=SMALL_LIMIT,
        late=1,
    )
    return (
        out_t.T[None],
        grad_in[None],
        vectors[0],
        vectors[1],
        grads[0],
        grads[1],
        grads[2],
        grads[3],
        vectors[2],
        vectors[3],
        grad_up,
        grad_down,
    )


def solution(mesh):
    placed = (
        P("row", "seq", None),
        P("row", None),
        P(),
        P(),
        P(),
        P(),
        P(),
        P(),
        P(),
        P(),
        P(None, "pat"),
        P("pat", None),
        P("row", "seq", "pat"),
    )
    return jax.shard_map(
        per_device,
        mesh=mesh,
        in_specs=placed,
        out_specs=(
            P("row", "seq", "pat"),
            P("row", ("seq", "pat"), None),
            P(),
            P(),
            P(),
            P(),
            P(),
            P(),
            P(),
            P(),
            P(None, "pat"),
            P("pat", None),
        ),
        check_vma=False,
    )
```
